32 devices in a mesh: dp: 16 (over z, y, x), mp: 2 (over core).
Axes of the slice: x: 2, y: 2, z: 4, core: 2. Of those that a mesh axis runs over, the one named last changes fastest.
Arguments:
- tokens: bfloat16 [36864, 512], P(('dp', 'mp')), may hold values from -6 to 6
- query_key_value_matrix: bfloat16 [512, 3, 512], P(None, None, 'mp'), may hold values from -0.25 to 0.25
- query_value_bias: bfloat16 [2, 512], P(None, 'mp'), may hold values from -3 to 3
- head_logit_scale: bfloat16 [16], P('mp'), may hold values from 1.59375 to 2.6875
- bias_net_first_weight: float32 [2, 512], replicated, may hold values from -4 to 4
- bias_net_first_bias: float32 [512], replicated, may hold values from -3 to 3
- bias_net_second_weight: bfloat16 [512, 16], P(None, 'mp'), may hold values from -0.25 to 0.25
- relative_pair_index: int32 [576, 576], replicated, may hold values from 0 to 2208, as said below
- attention_out_weight: bfloat16 [512, 512], P('mp'), may hold values from -0.25 to 0.25
- attention_out_bias: float32 [512], replicated, may hold values from -0.6 to 0.6
- attention_norm_weight: float32 [512], replicated, may hold values from 0.5 to 1.5
- attention_norm_bias: float32 [512], replicated, may hold values from -1.2 to 1.2
- ffn_input_weight: bfloat16 [512, 2048], P(None, 'mp'), may hold values from -0.25 to 0.25
- hidden_ffn_bias: bfloat16 [2048], P('mp'), may hold values from -1.1953125 to 1.1953125
- ffn_output_weight: bfloat16 [2048, 512], P('mp'), may hold values from -0.125 to 0.125
- output_ffn_bias: float32 [512], replicated, may hold values from -1.2 to 1.2
- feedforward_norm_weight: float32 [512], replicated, may hold values from 0.5 to 1.5
- feedforward_norm_bias: float32 [512], replicated, may hold values from -1.2 to 1.2
- output_gradient: bfloat16 [36864, 512], P(('dp', 'mp')), may hold values from -6 to 6
Outputs:
- block_out: bfloat16 [36864, 512], P(('dp', 'mp'))
- tokens_grad: float32 [36864, 512], P(('dp', 'mp'))
- w_qkv_grad: float32 [512, 3, 512], P(None, None, 'mp')
- qv_bias_grad: float32 [2, 512], P(None, 'mp')
- logit_scale_grad: float32 [16], P('mp')
- cpb_w1_grad: float32 [2, 512], replicated
- cpb_b1_grad: float32 [512], replicated
- cpb_w2_grad: float32 [512, 16], P(None, 'mp')
- w_proj_grad: float32 [512, 512], P('mp')
- b_proj_grad: float32 [512], replicated
- ln1_gain_grad: float32 [512], replicated
- ln1_bias_grad: float32 [512], replicated
- w_fc1_grad: float32 [512, 2048], P(None, 'mp')
- b_fc1_grad: float32 [2048], P('mp')
- w_fc2_grad: float32 [2048, 512], P('mp')
- b_fc2_grad: float32 [512], replicated
- ln2_gain_grad: float32 [512], replicated
- ln2_bias_grad: float32 [512], replicated
The draws below stay inside these ranges and needn't reach their ends.
Inputs may be any that keep to these rules, and one draw needn't show every extreme that they name: relative_pair_index[i, j] = (r_i - r_j + 23) * 47 + (c_i - c_j + 23), where (r_i, c_i) is the cell of a 24 x 24 window whose token is stored at place i of every image; places and cells correspond one to one.
All inputs are finite; a program needn't handle non-finite values.
Results may differ from the reference program's by a relative error of at most 0.015.
The reference program's roundings to bfloat16 on the way count: a program that leaves them out, or rounds other values in their place, can miss the bound.
Values may be sent and summed in bfloat16 or wider, within the bound.
No kernel may reach another device: no remote copies, remote signals or barrier semaphores. Data moves between devices by JAX's collectives and lax.ppermute only.
A program may use at most 320 MiB of HBM per device.

```python
import jax
import jax.numpy as jnp
from jax import lax

D = 512
HEAD_COUNT = 16
HEAD = 32
FF = 2048
BIAS_NET_UNITS = 512
SIDE = 24
IMAGES = 64
WIN = 576
TOKENS = 36864


def draw_relative_pair_index(key, part):
    key = jax.random.fold_in(key, 11)
    placed = jax.random.permutation(key, WIN)
    row_cell = placed // SIDE
    col_cell = placed % SIDE
    table_side = 2 * SIDE - 1
    return ((row_cell[:, None] - row_cell[None, :] + SIDE - 1) * table_side + col_cell[:, None] - col_cell[None, :] + SIDE - 1).astype(jnp.int32)


def block_levels(key, dims, cuts, least, largest):
    level, own = 1.0, jax.random.fold_in(key, 6)
    for dim, parts in cuts:
        steps = jnp.exp(jax.random.uniform(jax.random.fold_in(own, dim), (parts,), jnp.float32, least / len(cuts), largest / len(cuts)))
        level = level * jnp.repeat(steps, dims[dim] // parts).reshape([-1 if axis == dim else 1 for axis in range(len(dims))])
    return level


def centred(key, extent, deviation, reach, shards=(), held_as=jnp.bfloat16):
    entries = jax.random.normal(key, extent, jnp.float32) * deviation
    if len(shards) > 0:
        entries = block_levels(key, extent, shards, -0.22, 0.18) * entries
    return jnp.clip(entries, min=-reach, max=reach).astype(held_as)


def setup_inputs(seed: int = 0) -> dict:
    seeds = jax.random.split(jax.random.key(seed), 20)
    return {
        "tokens": centred(seeds[0], (TOKENS, D), 1.0, 6.0, ((0, 32),)),
        "query_key_value_matrix": centred(seeds[1], (D, 3, D), D ** -0.5, 0.25, ((2, 2),)),
        "query_value_bias": centred(seeds[2], (2, D), 0.5, 3.0, ((1, 2),)),
        "head_logit_scale": jnp.clip(1.59375 + 1.09375 * jax.random.uniform(seeds[3], (HEAD_COUNT,), jnp.float32) ** block_levels(seeds[3], (HEAD_COUNT,), ((0, 2),), -0.2, 0.2), 1.59375, 2.6875).astype(jnp.bfloat16),
        "bias_net_first_weight": centred(seeds[4], (2, BIAS_NET_UNITS), 2 ** -0.5, 4.0, (), jnp.float32),
        "bias_net_first_bias": centred(seeds[5], (BIAS_NET_UNITS,), 0.5, 3.0, (), jnp.float32),
        "bias_net_second_weight": centred(seeds[6], (BIAS_NET_UNITS, HEAD_COUNT), BIAS_NET_UNITS ** -0.5, 0.25, ((1, 2),)),
        "relative_pair_index": draw_relative_pair_index(jax.random.fold_in(seeds[19], 71), 0),
        "attention_out_weight": centred(seeds[8], (D, D), D ** -0.5, 0.25, ((0, 2),)),
        "attention_out_bias": centred(seeds[9], (D,), 0.1, 0.6, (), jnp.float32),
        "attention_norm_weight": jnp.clip(1.0 + 0.1 * jax.random.normal(seeds[10], (D,), jnp.float32), 0.5, 1.5),
        "attention_norm_bias": centred(seeds[11], (D,), 0.2, 1.2, (), jnp.float32),
        "ffn_input_weight": centred(seeds[12], (D, FF), D ** -0.5, 0.25, ((1, 2),)),
        "hidden_ffn_bias": centred(seeds[13], (FF,), 0.2, 1.1953125, ((0, 2),)),
        "ffn_output_weight": centred(seeds[14], (FF, D), FF ** -0.5, 0.125, ((0, 2),)),
        "output_ffn_bias": centred(seeds[15], (D,), 0.2, 1.2, (), jnp.float32),
        "feedforward_norm_weight": jnp.clip(1.0 + 0.1 * jax.random.normal(seeds[16], (D,), jnp.float32), 0.5, 1.5),
        "feedforward_norm_bias": centred(seeds[17], (D,), 0.2, 1.2, (), jnp.float32),
        "output_gradient": centred(seeds[18], (TOKENS, D), 1.0, 6.0, ((0, 32),)),
    }


@jax.custom_vjp
def low(v):
    return lax.optimization_barrier(v.astype(jnp.bfloat16)).astype(jnp.float32)

@jax.custom_vjp
def low_back(v):
    return v

def low_keep(v):
    return (low(v), None)

def low_pass(kept, grad):
    return (grad,)

def back_keep(v):
    return (v, None)

def back_low(kept, grad):
    return (low(grad),)
low.defvjp(low_keep, low_pass)
low_back.defvjp(back_keep, back_low)

def matrix_product(left, right):
    return jnp.dot(left, right, precision=lax.Precision.HIGHEST, preferred_element_type=jnp.float32)

def exact_error_gelu(values):
    return jax.nn.gelu(values, approximate=False)

def layer_norm(values, gain, shift):
    center = values - lax.optimization_barrier(jnp.mean(values, axis=-1, keepdims=True))
    spread = lax.optimization_barrier(jnp.mean(center * center, axis=-1, keepdims=True))
    return center * lax.rsqrt(spread + 1e-05) * gain + shift

def unit_rows(values):
    return values * lax.rsqrt(lax.optimization_barrier(jnp.sum(values * values, axis=-1, keepdims=True)) + 1.0)

def coord_table(side):
    offsets = jnp.arange(1 - side, side).astype(jnp.float32) * (8.0 / 15.0)
    logged = jnp.sign(offsets) * jnp.log2(jnp.abs(offsets) + 1.0) / 3.0
    return jnp.stack([jnp.repeat(logged, 2 * side - 1), jnp.tile(logged, 2 * side - 1)], axis=1)

def reference(tokens, query_key_value_matrix, query_value_bias, head_logit_scale, bias_net_first_weight, bias_net_first_bias, bias_net_second_weight, relative_pair_index, attention_out_weight, attention_out_bias, attention_norm_weight, attention_norm_bias, ffn_input_weight, hidden_ffn_bias, ffn_output_weight, output_ffn_bias, feedforward_norm_weight, feedforward_norm_bias, output_gradient):
    parameter_tree = tuple((make_array.astype(jnp.float32) for make_array in (query_key_value_matrix, query_value_bias, head_logit_scale, bias_net_first_weight, bias_net_first_bias, bias_net_second_weight, attention_out_weight, attention_out_bias, attention_norm_weight, attention_norm_bias, ffn_input_weight, hidden_ffn_bias, ffn_output_weight, output_ffn_bias, feedforward_norm_weight, feedforward_norm_bias)))
    coordinate_grid = coord_table(SIDE)

    def block_forward(weight_list, rows):
        query_key_value_weight, query_value_offset, logarithm_scale, bias_net_first_matrix, bias_net_hidden_bias, bias_net_second_matrix, output_projection_weight, output_projection_bias, attention_norm_gain, attention_norm_offset, upper_ffn_weight, upper_ffn_bias, lower_ffn_weight, lower_ffn_bias, feedforward_norm_gain, feedforward_norm_offset = weight_list
        bias_net_hidden_state = exact_error_gelu(matrix_product(coordinate_grid, bias_net_first_matrix) + bias_net_hidden_bias)
        head_bias_table = 16.0 * jax.nn.sigmoid(matrix_product(bias_net_hidden_state, bias_net_second_matrix))
        bias_heads = jnp.transpose(head_bias_table[relative_pair_index], (2, 0, 1))
        count_rows = rows.shape[0]
        qkv = low_back(matrix_product(rows, query_key_value_weight.reshape(D, 3 * D))).reshape(count_rows, 3, D)
        qkv = qkv + jnp.stack([query_value_offset[0], jnp.zeros_like(query_value_offset[0]), query_value_offset[1]])
        scale = jnp.exp(logarithm_scale)

        def attend(image_qkv):
            shaped = image_qkv.reshape(WIN, 3, HEAD_COUNT, HEAD)
            query = low(unit_rows(shaped[:, 0]))
            keys = low(unit_rows(shaped[:, 1]))
            values = low(shaped[:, 2])
            cosine = low_back(jnp.einsum('ihd,jhd->hij', query, keys, precision=lax.Precision.HIGHEST))
            attn_probs = jax.nn.softmax(cosine * scale[:, None, None] + bias_heads, axis=-1)
            mixed = jnp.einsum('hij,jhd->ihd', low(attn_probs), values, precision=lax.Precision.HIGHEST)
            return mixed.reshape(WIN, D)
        context = lax.map(jax.checkpoint(attend), qkv.reshape(count_rows // WIN, WIN, 3, D)).reshape(count_rows, D)
        context = low(low_back(context))
        attn = low_back(matrix_product(context, output_projection_weight)) + output_projection_bias
        middle = rows + layer_norm(attn, attention_norm_gain, attention_norm_offset)
        pre_act = low_back(matrix_product(low(middle), upper_ffn_weight)) + upper_ffn_bias
        mlp = low_back(matrix_product(low(exact_error_gelu(pre_act)), lower_ffn_weight)) + lower_ffn_bias
        return middle + layer_norm(mlp, feedforward_norm_gain, feedforward_norm_offset)
    per_group = max((count for count in range(1, 8) if IMAGES % count == 0))
    groups = IMAGES // per_group
    rows_all = tokens.astype(jnp.float32).reshape(groups, per_group * WIN, D)
    cotangents = output_gradient.astype(jnp.float32).reshape(groups, per_group * WIN, D)

    def add_pair(left, right):
        return left + right

    def one_group(totals, inputs):
        rows, cotangent = inputs
        result, pullback = jax.vjp(block_forward, parameter_tree, rows)
        param_grads, row_grads = pullback(cotangent)
        return (jax.tree.map(add_pair, totals, param_grads), (result, row_grads))
    totals, (results, row_grads) = lax.scan(one_group, jax.tree.map(jnp.zeros_like, parameter_tree), (rows_all, cotangents))
    return (results.reshape(TOKENS, D).astype(jnp.bfloat16), row_grads.reshape(TOKENS, D), totals[0], totals[1], totals[2], totals[3], totals[4], totals[5], totals[6], totals[7], totals[8], totals[9], totals[10], totals[11], totals[12], totals[13], totals[14], totals[15])
```

```python
import functools

import jax
import jax.numpy as jnp
import numpy as np
from jax import lax
from jax.experimental import pallas as pl
from jax.experimental.pallas import tpu as pltpu
from jax.sharding import PartitionSpec as P

SIDE = 24
WIN = SIDE * SIDE
TABLE_SIDE = 2 * SIDE - 1
PITCH = 2 * SIDE
WIDE = SIDE * PITCH
HEAD = 32
LANES = 128
PER_GROUP = LANES // HEAD
TILE = 256
SMALL_ROWS = 96
LOG2E = 1.4426950408889634
VMEM_BYTES = 58 * 1024 * 1024
BF = jnp.bfloat16
F32 = jnp.float32


def mm(left, right):
    return lax.dot_general(left, right, (((1,), (0,)), ((), ())), preferred_element_type=F32)


def mm_nt(left, right):
    return lax.dot_general(left, right, (((1,), (1,)), ((), ())), preferred_element_type=F32)


def mm_tn(left, right):
    return lax.dot_general(left, right, (((0,), (0,)), ((), ())), preferred_element_type=F32)


def split(values):
    high = values.astype(BF)
    return high, (values - high.astype(F32)).astype(BF)


def iota(shape, axis):
    return lax.broadcasted_iota(jnp.int32, shape, axis)


def cat(parts, axis=1):
    return jnp.concatenate(parts, axis=axis)


def flag(condition):
    return jnp.where(condition, 1.0, 0.0).astype(BF)


def column_sums(values):
    return jnp.sum(values, axis=0, keepdims=True)


def gelu_with_slope(values):
    cdf = 0.5 + 0.5 * lax.erf(values * 0.7071067811865476)
    bell = jnp.exp2(values * values * (-0.5 * LOG2E)) * 0.3989422804014327
    return values * cdf, cdf + values * bell


def cell_of_places(index_line, axis):
    row_part = (index_line * 22311) >> 20
    col_part = index_line - row_part * TABLE_SIDE
    if axis == 1:
        rows = jnp.max(row_part, axis=1, keepdims=True) - row_part
        cols = jnp.max(col_part, axis=1, keepdims=True) - col_part
    else:
        rows = row_part - jnp.min(row_part, axis=0, keepdims=True)
        cols = col_part - jnp.min(col_part, axis=0, keepdims=True)
    return rows * SIDE + cols


def head_sum_matrix(turn=0):
    row = iota((2 * LANES, LANES), 0)
    col = iota((2 * LANES, LANES), 1)
    return flag((((row >> 5) + turn) & 3) == (col >> 5))


def head_sums(values, matrix):
    return mm(cat(split(values)), matrix)


def whole(shape):
    return pl.BlockSpec(shape, lambda *_: (0,) * len(shape))


def params(**more):
    return pltpu.CompilerParams(vmem_limit_bytes=VMEM_BYTES, **more)


def cost(flops, moved):
    return pl.CostEstimate(flops=flops, bytes_accessed=moved, transcendentals=0)


def coord_rows():
    def u(offset):
        c = np.float32(offset) * np.float32(8.0 / 15.0)
        return np.sign(c) * np.log2(np.abs(c) + np.float32(1.0)) / np.float32(3.0)

    lane = np.arange(WIDE)
    out = []
    for parity in range(2):
        e = 2 * (lane // PITCH) + parity
        k = lane % PITCH
        out.append(np.stack([u(SIDE - 1 - e), u(SIDE - 1 - k)] + [np.ones(WIDE)] + [np.zeros(WIDE)] * 5))
    return np.stack(out).astype(np.float32)


def table_pre(coord_ref, cols_ref, parity):
    pre = cols_ref[:, 0:1] * coord_ref[parity, 0:1, :] + cols_ref[:, 1:2] * coord_ref[parity, 1:2, :]
    return pre + cols_ref[:, 2:3]


def table_of(hidden, w2s):
    parts = split(hidden)
    z = cat([mm(w2, parts[0]) + mm(w2, parts[1]) for w2 in w2s], 0)
    return 16.0 / (1.0 + jnp.exp(-z))


def stat_lane(kind, group, head):
    return kind * 16 + group * PER_GROUP + head


def forward_kernel(
    images, halves, row_ref, col_ref, x_ref, w_a_ref, w_b_ref, p_a_ref, p_b_ref, coord_ref, cols_ref, w2_a_ref, w2_b_ref,
    e_ref, ctx_ref, rest_ref, ql_ref, kl_ref, vl_ref, stat_ref, gather_ref, scatter_ref,
    cell_ref, table_ref, pos_ref,
):
    g = pl.program_id(0)

    @pl.when(g == 0)
    def prepare():
        gather = flag(iota((WIN, WIN), 0) == cell_of_places(row_ref[0:1, :], 1))
        gather_ref[...] = gather
        scatter_ref[...] = flag(iota((WIN, WIN), 1) == cell_of_places(col_ref[:, 0:1], 0))
        stat_ref[...] = jnp.zeros_like(stat_ref)
        for m in range(images):
            rows = slice(m * WIN, (m + 1) * WIN)
            cell_ref[rows, :] = mm(gather, x_ref[rows, :]).astype(BF)
        for parity in range(2):
            hidden, _ = gelu_with_slope(table_pre(coord_ref, cols_ref, parity))
            table_ref[parity] = table_of(hidden, (w2_a_ref[...], w2_b_ref[...])) * LOG2E

    first = g < halves
    w = cat([jnp.where(first, w_a_ref[i], w_b_ref[i]) for i in range(3)])
    p = jnp.where(first, p_a_ref[...], p_b_ref[...])
    lower = iota((1, WIDE), 1) % PITCH < SIDE
    lane = iota((1, LANES), 1)
    group_lane = lane >> 5
    ones = jnp.ones((WIN, LANES), BF)
    row = iota((2 * LANES, LANES), 0) & (LANES - 1)
    col = iota((2 * LANES, LANES), 1)
    same = flag((row >> 5) == (col >> 5))
    sums = [cat([same, flag(stat_lane(i, g, row >> 5) == col)]) for i in range(2)]
    pick = flag(((row & (HEAD - 1)) == 0) & (stat_lane(2, g, row >> 5) == col))
    stat_here = [(lane >> 2) == i * 4 + g for i in range(2)]
    operands = []
    for m in range(images):
        rows = slice(m * WIN, (m + 1) * WIN)
        qkv = mm(cell_ref[rows, :], w)
        q = qkv[:, :LANES] + p[0:1, :]
        k = qkv[:, LANES : 2 * LANES]
        vl = (qkv[:, 2 * LANES :] + p[1:2, :]).astype(BF)
        rq = lax.rsqrt(head_sums(q * q, sums[0]) + 1.0)
        rk = lax.rsqrt(head_sums(k * k, sums[1]) + 1.0)
        ql = (q * rq[:, :LANES]).astype(BF)
        kl = (k * rk[:, :LANES]).astype(BF)
        stat = jnp.where(stat_here[0], rq[:, LANES:], stat_ref[rows, :])
        stat_ref[rows, :] = jnp.where(stat_here[1], rk[:, LANES:], stat)
        ql_ref[rows, :] = ql
        kl_ref[rows, :] = kl
        vl_ref[rows, :] = vl
        scaled = split(ql.astype(F32) * (p[2:3, :] * LOG2E))
        operands.append((cat(scaled), cat([kl, kl]), cat([vl, ones])))

    mixes = [jnp.zeros((WIN, LANES), F32)] * images
    inverses = [jnp.zeros((WIN, LANES), F32)] * images
    for own in range(PER_GROUP):
        head = pl.ds(g * PER_GROUP + own, 1)
        even = pltpu.roll(
            jnp.broadcast_to(table_ref[0, head, :], (SIDE, WIDE)), WIDE - SIDE + 1, 1, stride=1, stride_axis=0
        )
        odd = pltpu.roll(jnp.broadcast_to(table_ref[1, head, :], (SIDE, WIDE)), 1, 1, stride=1, stride_axis=0)
        bands = jnp.where(lower, even, odd)
        slot = own % 2
        for r in range(SIDE):
            offset = (SIDE - 1 - r) * SIDE
            pos_ref[slot, pl.ds(r * SIDE, SIDE), :] = pltpu.roll(bands, (WIDE - offset) % WIDE, 1)[:, :WIN]
        here = group_lane == own
        mask = flag(here)
        mask = cat([mask, mask])
        for m in range(images):
            left, right, values = operands[m]
            weights = jnp.exp2(mm_nt(left * mask, right) + pos_ref[slot]).astype(BF)
            e_ref[own, m] = weights
            mixed = mm(weights, values)
            inverse = 1.0 / mixed[:, LANES:]
            mixes[m] = jnp.where(here, mixed[:, :LANES] * inverse, mixes[m])
            inverses[m] = jnp.where(here, inverse, inverses[m])
    for m in range(images):
        rows = slice(m * WIN, (m + 1) * WIN)
        high, low = split(mixes[m])
        ctx_ref[rows, :] = high
        rest_ref[rows, :] = low
        stat_ref[rows, :] += head_sums(inverses[m], pick)


def attention_forward(index, x, ws, ps, coords, columns, w2s):
    count, depth = x.shape
    images = count // WIN
    halves = ws[0].shape[2] // LANES
    groups = 2 * halves
    heads = groups * PER_GROUP
    wide = groups * LANES
    block = pl.BlockSpec((count, LANES), lambda g: (0, g))
    low = jax.ShapeDtypeStruct((count, wide), BF)
    place = jax.ShapeDtypeStruct((WIN, WIN), BF)
    own = lambda g: jnp.minimum(g, halves - 1)
    other = lambda g: jnp.maximum(g - halves, 0)
    w_block = (3, depth, LANES)
    p_block = (ps[0].shape[0], LANES)
    return pl.pallas_call(
        functools.partial(forward_kernel, images, halves),
        grid=(groups,),
        in_specs=[
            pl.BlockSpec((8, WIN), lambda g: (0, 0)), pl.BlockSpec((WIN, LANES), lambda g: (0, 0)), whole(x.shape),
            pl.BlockSpec(w_block, lambda g: (0, 0, own(g))), pl.BlockSpec(w_block, lambda g: (0, 0, other(g))),
            pl.BlockSpec(p_block, lambda g: (0, own(g))), pl.BlockSpec(p_block, lambda g: (0, other(g))),
            whole(coords.shape), whole(columns.shape), whole(w2s[0].shape), whole(w2s[1].shape),
        ],
        out_specs=[pl.BlockSpec((PER_GROUP, images, WIN, WIN), lambda g: (g, 0, 0, 0))]
        + [block] * 5 + [whole((count, LANES))] + [whole((WIN, WIN))] * 2,
        out_shape=[jax.ShapeDtypeStruct((heads, images, WIN, WIN), BF)] + [low] * 5
        + [jax.ShapeDtypeStruct((count, LANES), F32), place, place],
        scratch_shapes=[
            pltpu.VMEM((count, depth), BF),
            pltpu.VMEM((2, heads, WIDE), F32),
            pltpu.VMEM((2, WIN, WIN), F32),
        ],
        compiler_params=params(dimension_semantics=("arbitrary",)),
        cost_estimate=cost(8_000_000_000, 40_000_000),
        name="attention_forward",
    )(index, index, x, *ws, *ps, coords, columns, *w2s)


def norm_stats(values):
    center = values - jnp.mean(values, axis=1, keepdims=True)
    inverse = lax.rsqrt(jnp.mean(center * center, axis=1, keepdims=True) + 1e-05)
    return center * inverse, inverse


def norm_back(grad, unit, inverse, gain):
    scaled = grad * gain
    mean = jnp.mean(scaled, axis=1, keepdims=True)
    along = jnp.mean(scaled * unit, axis=1, keepdims=True)
    return inverse * (scaled - mean - unit * along)


def feed_kernel(
    images, scatter_ref, x_ref, mix_ref, wo_a_ref, wo_b_ref, p_a_ref, p_b_ref,
    bo_ref, g1_ref, s1_ref, b2_ref, g2_ref, s2_ref, w1_a_hbm, w1_b_hbm, w2_a_hbm, w2_b_hbm, og_hbm,
    out_hbm, dmid_hbm, da_hbm, own_hbm, other_hbm, small_ref, gb1_ref,
    w1_ref, w2_ref, og_ref, out_ref, da_ref, pack_ref, mid_ref,
    ctx_ref, low_ref, pre_ref, hid_ref, slope_ref, acc_ref, unit_ref, in_sem, out_sem,
):
    half = w1_ref.shape[2]
    depth = x_ref.shape[1]
    narrow = wo_a_ref.shape[0]
    tiles = 2 * half // TILE
    ps = (p_a_ref, p_b_ref)
    packed = (own_hbm, other_hbm)
    loads = [
        pltpu.make_async_copy(source, target, in_sem.at[i])
        for i, (source, target) in enumerate(
            (
                (w1_a_hbm, w1_ref.at[0]), (w1_b_hbm, w1_ref.at[1]), (w2_a_hbm, w2_ref.at[0]),
                (w2_b_hbm, w2_ref.at[1]), (og_hbm, og_ref),
            )
        )
    ]
    for load in loads:
        load.start()
    stores = []

    def store(source, target):
        copy = pltpu.make_async_copy(source, target, out_sem.at[len(stores)])
        copy.start()
        stores.append(copy)

    def place_of(tile):
        at = tile * TILE
        return at // half, slice(at % half, at % half + TILE)

    inverse_ones = []
    for m in range(images):
        rows = slice(m * WIN, (m + 1) * WIN)
        ctx = mm(scatter_ref[...], mix_ref[rows, :]).astype(BF)
        ctx_ref[rows, :] = ctx
        attn = mm(ctx[:, :narrow], wo_a_ref[...]) + mm(ctx[:, narrow:], wo_b_ref[...]) + bo_ref[...]
        unit_one, inverse = norm_stats(attn)
        inverse_ones.append(inverse)
        unit_ref[rows, :] = unit_one
        middle = x_ref[rows, :].astype(F32) + unit_one * g1_ref[...] + s1_ref[...]
        mid_ref[rows, :] = middle
        low_ref[rows, :] = middle.astype(BF)

    def up(tile):
        which, cols = place_of(tile)
        if cols.start == 0:
            loads[which].wait()
        row = 3 + cols.start // TILE
        pre_ref[tile % 2] = mm(low_ref[...], w1_ref[which, :, cols]) + ps[which][row : row + 1, :]

    def down(tile):
        which, cols = place_of(tile)
        if cols.start == 0:
            loads[2 + which].wait()
        term = mm(hid_ref[which, :, cols], w2_ref[which, cols, :])
        if tile == 0:
            acc_ref[...] = term
        else:
            acc_ref[...] += term

    up(0)
    for tile in range(tiles):
        if tile + 1 < tiles:
            up(tile + 1)
        which, cols = place_of(tile)
        hidden, slope = gelu_with_slope(pre_ref[tile % 2])
        hid_ref[which, :, cols] = hidden.astype(BF)
        slope_ref[which, :, cols] = slope
        if tile > 0:
            down(tile - 1)
    down(tiles - 1)

    loads[4].wait()
    sums = [jnp.zeros((1, depth), F32)] * 3
    for m in range(images):
        rows = slice(m * WIN, (m + 1) * WIN)
        unit_two, inverse_two = norm_stats(acc_ref[rows, :] + b2_ref[...])
        out_ref[rows, :] = (mid_ref[rows, :] + (unit_two * g2_ref[...] + s2_ref[...])).astype(BF)
        grad = og_ref[rows, :].astype(F32)
        d_mlp = norm_back(grad, unit_two, inverse_two, g2_ref[...])
        terms = (column_sums(d_mlp), column_sums(grad * unit_two), column_sums(grad))
        sums = [a + b for a, b in zip(sums, terms)]
        da_ref[rows, :] = d_mlp.astype(BF)
        acc_ref[rows, :] = grad
    store(out_ref, out_hbm)
    for i in range(3):
        small_ref[3 + i : 4 + i, :] = sums[i]

    for tile in range(tiles):
        which, cols = place_of(tile)
        d_pre = mm_nt(da_ref[...], w2_ref[which, cols, :]) * slope_ref[which, :, cols]
        gb1_ref[which : which + 1, cols] = column_sums(d_pre)
        d_pre_low = d_pre.astype(BF)
        at = cols.start
        pack_ref[which, half + at : half + at + TILE, :] = mm_tn(hid_ref[which, :, cols], da_ref[...]).astype(BF)
        rows = slice(at // depth * depth, (at // depth + 1) * depth)
        pack_ref[which, rows, at % depth : at % depth + TILE] = mm_tn(low_ref[...], d_pre_low).astype(BF)
        acc_ref[...] += mm_nt(d_pre_low, w1_ref[which, :, cols])
        if at + TILE == half:
            span = pl.ds(0, 2 * half)
            store(pack_ref.at[which, span], packed[which].at[span])
    store(acc_ref, dmid_hbm)

    sums = [jnp.zeros((1, depth), F32)] * 3
    for m in range(images):
        rows = slice(m * WIN, (m + 1) * WIN)
        d_middle = acc_ref[rows, :]
        unit_one = unit_ref[rows, :]
        d_attn = norm_back(d_middle, unit_one, inverse_ones[m], g1_ref[...])
        terms = (column_sums(d_attn), column_sums(d_middle * unit_one), column_sums(d_middle))
        sums = [a + b for a, b in zip(sums, terms)]
        da_ref[rows, :] = d_attn.astype(BF)
    store(da_ref, da_hbm)
    for i in range(3):
        small_ref[i : i + 1, :] = sums[i]
    span = pl.ds(2 * half, narrow)
    for which in range(2):
        pack_ref[which, 2 * half : 2 * half + narrow, :] = mm_tn(
            ctx_ref[:, which * narrow : (which + 1) * narrow], da_ref[...]
        ).astype(BF)
        store(pack_ref.at[which, span], packed[which].at[span])
    for copy in stores:
        copy.wait()


def feed_forward(scatter, x, ctx, wos, w1s, w2s, ps, vectors, cotangent):
    count, depth = x.shape
    images = count // WIN
    narrow = wos[0].shape[0]
    half = w1s[0].shape[1]
    packed = 2 * half + narrow
    far = pl.BlockSpec(memory_space=pl.ANY)
    near = pl.BlockSpec(memory_space=pltpu.VMEM)
    low = pltpu.VMEM((count, depth), BF)
    full = pltpu.VMEM((count, depth), F32)
    return pl.pallas_call(
        functools.partial(feed_kernel, images),
        in_specs=[near] * 13 + [far] * 5,
        out_specs=[far] * 5 + [near] * 2,
        out_shape=[
            jax.ShapeDtypeStruct((count, depth), BF),
            jax.ShapeDtypeStruct((count, depth), F32),
            jax.ShapeDtypeStruct((count, depth), BF),
            jax.ShapeDtypeStruct((packed, depth), BF),
            jax.ShapeDtypeStruct((packed, depth), BF),
            jax.ShapeDtypeStruct((8, depth), F32),
            jax.ShapeDtypeStruct((2, half), F32),
        ],
        scratch_shapes=[
            pltpu.VMEM((2, depth, half), BF),
            pltpu.VMEM((2, half, depth), BF),
            low, low, low,
            pltpu.VMEM((2, packed, depth), BF),
            full,
            pltpu.VMEM((count, 2 * narrow), BF),
            low,
            pltpu.VMEM((2, count, TILE), F32),
            pltpu.VMEM((2, count, half), BF),
            pltpu.VMEM((2, count, half), F32),
            full, full,
            pltpu.SemaphoreType.DMA((5,)),
            pltpu.SemaphoreType.DMA((7,)),
        ],
        compiler_params=params(),
        cost_estimate=cost(2 * count * depth * (2 * depth + 12 * half), 30_000_000),
        name="feed_forward",
    )(scatter, x, ctx, *wos, *ps, *vectors, *w1s, *w2s, cotangent)


def context_grad_kernel(images, gather_ref, da_ref, wo_a_ref, wo_b_ref, out_ref):
    for m in range(images):
        rows = slice(m * WIN, (m + 1) * WIN)
        grad = cat([mm_nt(da_ref[rows, :], wo_a_ref[...]), mm_nt(da_ref[rows, :], wo_b_ref[...])]).astype(BF)
        out_ref[rows, :] = mm(gather_ref[...], grad).astype(BF)


def context_grad(gather, d_attn, wos):
    return pl.pallas_call(
        functools.partial(context_grad_kernel, d_attn.shape[0] // WIN),
        out_shape=jax.ShapeDtypeStruct((d_attn.shape[0], 2 * wos[0].shape[0]), BF),
        compiler_params=params(),
        cost_estimate=cost(2_000_000_000, 5_000_000),
        name="context_grad",
    )(gather, d_attn, *wos)


def backward_kernel(
    images, first, into, scatter_ref, x_ref, p_ref, dctx_ref, e_ref, ctx_ref, rest_ref, ql_ref, kl_ref, vl_ref, stat_ref,
    *refs,
):
    gw_ref, dqkv_ref, dm_ref, small_ref = refs[into : into + 4]
    dh_ref, dd_ref, vv_ref, qt_ref, dt_ref, r_ref, sum_ref, duq_ref, dkt_ref, dvt_ref = refs[into + 4 :]
    step = pl.program_id(0)
    own = step & (PER_GROUP - 1)
    group = first + (step >> 2)

    @pl.when(own == 0)
    def prepare():
        turned = head_sum_matrix(1)
        unit = flag(iota((LANES, LANES), 0) == iota((LANES, LANES), 1))
        shape = (2 * LANES, 3 * LANES)
        col = iota(shape, 1)
        spread = flag((iota(shape, 0) & (LANES - 1)) == stat_lane(col >> 7, group, (col & (LANES - 1)) >> 5))
        for m in range(images):
            rows = slice(m * WIN, (m + 1) * WIN)
            stats = head_sums(stat_ref[rows, :], spread)
            r_ref[rows, :] = stats[:, : 2 * LANES]
            grad = dctx_ref[rows, :].astype(F32) * (stats[:, 2 * LANES :] * p_ref[2:3, :])
            high, low = split(grad)
            dh_ref[m] = cat([high, low])
            mix = ctx_ref[rows, :].astype(F32) + rest_ref[rows, :].astype(F32)
            dd_ref[m] = cat(split(-head_sums(grad * mix, turned)))
            vl = vl_ref[rows, :]
            vv_ref[m] = cat([vl, vl])
            qt_ref[m] = mm_nt(unit, ql_ref[rows, :]).astype(BF).reshape(PER_GROUP, HEAD, WIN)
            high_t = mm_nt(unit, high).astype(BF).reshape(PER_GROUP, HEAD, WIN)
            low_t = mm_nt(unit, low).astype(BF).reshape(PER_GROUP, HEAD, WIN)
            dt_ref[m] = cat([high_t, low_t], 1)
            dkt_ref[m, :, WIN:] = jnp.zeros((LANES, dkt_ref.shape[2] - WIN), F32)
            dvt_ref[m, :, WIN:] = jnp.zeros((LANES, dkt_ref.shape[2] - WIN), F32)

    lane = iota((1, 2 * LANES), 1) & (LANES - 1)
    mask = (lane >> 5) == own
    mask_low = flag(mask)
    spot_low = flag(lane == ((own + 1) & 3) * HEAD)
    head_rows = pl.ds(pl.multiple_of(own * HEAD, HEAD), HEAD)
    for m in range(images):
        rows = slice(m * WIN, (m + 1) * WIN)
        left = dh_ref[m] * mask_low + dd_ref[m] * spot_low
        right = vv_ref[m] * (1 - spot_low) + spot_low
        weights = e_ref[0, m]
        d_cos = weights.astype(F32) * mm_nt(left, right)
        if m == 0:
            sum_ref[...] = d_cos
        else:
            sum_ref[...] += d_cos
        d_low = d_cos.astype(BF)
        duq_ref[rows, :] = jnp.where(mask[:, :LANES], mm(d_low, kl_ref[rows, :]), duq_ref[rows, :])
        dkt_ref[m, head_rows, :WIN] = mm(qt_ref[m, own], d_low)
        both = mm(dt_ref[m, own], weights)
        dvt_ref[m, head_rows, :WIN] = both[:HEAD] + both[HEAD:]
    rest = jnp.zeros((SIDE, WIDE - WIN), F32)
    total = None
    for r in range(SIDE):
        offset = (SIDE - 1 - r) * SIDE
        band = cat([sum_ref[pl.ds(r * SIDE, SIDE), :], rest])
        band = pltpu.roll(band, offset, 1) if offset else band
        total = band if total is None else total + band
    dm_ref[0] = total

    @pl.when(own == PER_GROUP - 1)
    def finish():
        summing = head_sum_matrix()
        sums = [jnp.zeros((1, LANES), F32)] * 3
        for m in range(images):
            rows = slice(m * WIN, (m + 1) * WIN)
            uq = ql_ref[rows, :].astype(F32)
            duq = duq_ref[rows, :]
            along_q = head_sums(uq * duq, summing)
            dq = r_ref[rows, :LANES] * (duq - uq * along_q)
            uk = kl_ref[rows, :].astype(F32)
            duk = jnp.transpose(dkt_ref[m])[:WIN]
            dk = r_ref[rows, LANES:] * (duk - uk * head_sums(uk * duk, summing))
            dv = jnp.transpose(dvt_ref[m])[:WIN] / p_ref[2:3, :]
            sums = [a + column_sums(t) for a, t in zip(sums, (dq, dv, along_q))]
            grads = cat([dq.astype(BF), dk.astype(BF), dv.astype(BF)])
            dqkv_ref[rows, :] = mm(scatter_ref[...], grads).astype(BF)
        for i in range(3):
            small_ref[0, i : i + 1, :] = sums[i]
        gw = mm_tn(x_ref[...], dqkv_ref[...]).astype(BF)
        for i in range(3):
            gw_ref[0, i] = gw[:, i * LANES : (i + 1) * LANES]


def attention_backward(first, span, halves, scatter, x, p, dctx, saved, earlier=None):
    count, depth = x.shape
    images = count // WIN
    padded = -(-WIN // LANES) * LANES
    block = pl.BlockSpec((count, LANES), lambda h: (0, first + (h >> 2)))
    inner = first % halves
    into = 0 if earlier is None else 1
    arguments = [scatter, x, p, dctx, *saved] + [earlier] * into
    return pl.pallas_call(
        functools.partial(backward_kernel, images, first, into),
        grid=(span * PER_GROUP,),
        in_specs=[
            whole(scatter.shape), whole(x.shape), pl.BlockSpec((p.shape[0], LANES), lambda h: (0, inner + (h >> 2))),
            block, pl.BlockSpec((1, images, WIN, WIN), lambda h: (first * PER_GROUP + h, 0, 0, 0)),
        ] + [block] * 5 + [whole((count, LANES))] + [pl.BlockSpec(memory_space=pl.ANY)] * into,
        out_specs=[
            pl.BlockSpec((1, 3, depth, LANES), lambda h: (inner + (h >> 2), 0, 0, 0)),
            pl.BlockSpec((count, 3 * LANES), lambda h: (0, h >> 2)),
            pl.BlockSpec((1, SIDE, WIDE), lambda h: (h, 0, 0)),
            pl.BlockSpec((1, 8, LANES), lambda h: (h >> 2, 0, 0)),
        ],
        out_shape=[
            jax.ShapeDtypeStruct((halves, 3, depth, LANES), BF),
            jax.ShapeDtypeStruct((count, span * 3 * LANES), BF),
            jax.ShapeDtypeStruct((span * PER_GROUP, SIDE, WIDE), F32),
            jax.ShapeDtypeStruct((span, 8, LANES), F32),
        ],
        scratch_shapes=[
            pltpu.VMEM((images, WIN, 2 * LANES), BF),
            pltpu.VMEM((images, WIN, 2 * LANES), BF),
            pltpu.VMEM((images, WIN, 2 * LANES), BF),
            pltpu.VMEM((images, PER_GROUP, HEAD, WIN), BF),
            pltpu.VMEM((images, PER_GROUP, 2 * HEAD, WIN), BF),
            pltpu.VMEM((count, 2 * LANES), F32),
            pltpu.VMEM((WIN, WIN), F32),
            pltpu.VMEM((count, LANES), F32),
            pltpu.VMEM((images, LANES, padded), F32),
            pltpu.VMEM((images, LANES, padded), F32),
        ],
        input_output_aliases={len(arguments) - 1: 0} if into else {},
        compiler_params=params(dimension_semantics=("arbitrary",)),
        cost_estimate=cost(8_000_000_000 * span, 20_000_000 * span),
        name=f"attention_backward_{first}",
    )(*arguments)


def input_grad_kernel(widths, dmid_ref, *refs):
    grads, (w_a_ref, w_b_ref, out_ref) = refs[:-3], refs[-3:]
    pieces = [ref[:, i * LANES : (i + 1) * LANES] for ref, span in zip(grads, widths) for i in range(3 * span)]
    half = len(pieces) // 2
    total = dmid_ref[...]
    for which, w_ref in enumerate((w_a_ref, w_b_ref)):
        mine = pieces[which * half : (which + 1) * half]
        for i in range(3):
            total = total + mm_nt(cat(mine[i::3]), w_ref[i])
    out_ref[...] = total


def input_grad(d_middle, grads, ws):
    count, depth = d_middle.shape
    tall = count // 4
    widths = [g.shape[1] // (3 * LANES) for g in grads]
    rows = lambda width: pl.BlockSpec((tall, width), lambda i: (i, 0))
    return pl.pallas_call(
        functools.partial(input_grad_kernel, widths),
        grid=(4,),
        in_specs=[rows(depth)] + [rows(g.shape[1]) for g in grads] + [whole(w.shape) for w in ws],
        out_specs=rows(depth),
        out_shape=jax.ShapeDtypeStruct(d_middle.shape, F32),
        compiler_params=params(dimension_semantics=("arbitrary",)),
        cost_estimate=cost(2_000_000_000, 12_000_000),
        name="input_grad",
    )(d_middle, *grads, *ws)


def table_back_kernel(spans, coord_ref, cols_ref, w2_a_ref, w2_b_ref, scale_ref, vec_ref, gb1_ref, *refs):
    calls = len(spans)
    dms, smalls, (own_ref, other_ref) = refs[:calls], refs[calls : 2 * calls], refs[2 * calls :]
    lower = iota((1, WIDE), 1) % PITCH < SIDE
    even, odd = [], []
    for ref in dms:
        e = jnp.zeros((ref.shape[0], WIDE), F32)
        o = jnp.zeros((ref.shape[0], WIDE), F32)
        for c in range(SIDE):
            slab = ref[:, c, :]
            e = e + pltpu.roll(jnp.where(lower, slab, 0.0), (SIDE - 1 - c) % WIDE, 1)
            o = o + pltpu.roll(jnp.where(lower, 0.0, slab), (-1 - c) % WIDE, 1)
        even.append(e)
        odd.append(o)
    w2s = (w2_a_ref[...], w2_b_ref[...])
    dw2 = None
    dcols = None
    for parity, grads in enumerate((even, odd)):
        hidden, slope = gelu_with_slope(table_pre(coord_ref, cols_ref, parity))
        table = table_of(hidden, w2s)
        dz = cat(grads, 0) * scale_ref[...] * table * (1.0 - table * 0.0625)
        hidden_high, hidden_low = split(hidden)
        dz_high, dz_low = split(dz)
        term = mm_nt(dz_high, hidden_high) + mm_nt(dz_high, hidden_low) + mm_nt(dz_low, hidden_high)
        dw2 = term if dw2 is None else dw2 + term
        w2 = cat(w2s, 0)
        high, low = split((mm_tn(w2, dz_high) + mm_tn(w2, dz_low)) * slope)
        c_high, c_low = split(coord_ref[parity])
        term = mm_nt(c_high, high) + mm_nt(c_high, low) + mm_nt(c_low, high)
        dcols = term if dcols is None else dcols + term
    heads = w2s[0].shape[0]
    groups = [(ref, g) for ref, span in zip(smalls, spans) for g in range(span)]
    for which, out in enumerate((own_ref, other_ref)):
        lines = [(vec_ref, i) for i in range(6)] + [(dcols, i) for i in range(3)] + [(gb1_ref, which)]
        row = 0
        for source, i in lines + [(dw2, which * heads + h) for h in range(heads)]:
            for at in range(0, source.shape[1], LANES):
                out[row : row + 1, :] = source[i : i + 1, at : at + LANES]
                row += 1
        for ref, g in groups[which * len(groups) // 2 : (which + 1) * len(groups) // 2]:
            for i in range(3):
                out[row : row + 1, :] = ref[g, i : i + 1, :]
                row += 1
        out[row:, :] = jnp.zeros((SMALL_ROWS - row, LANES), F32)


def table_back(coords, columns, w2s, inv_scale, vectors, gb1, dms, smalls):
    small = jax.ShapeDtypeStruct((SMALL_ROWS, LANES), F32)
    return pl.pallas_call(
        functools.partial(table_back_kernel, [s.shape[0] for s in smalls]),
        out_shape=(small, small),
        compiler_params=params(),
        cost_estimate=cost(1_000_000_000, 10_000_000),
        name="table_back",
    )(coords, columns, *w2s, inv_scale, vectors, gb1, *dms, *smalls)


def swap(array):
    return lax.ppermute(array, "mp", [(0, 1), (1, 0)])


def tie(*trees):
    leaves, kind = jax.tree.flatten(trees)
    return jax.tree.unflatten(kind, lax.optimization_barrier(leaves))


def send(array, plan, phase, step):
    pairs = []
    for mp, strides in enumerate(plan):
        stride = strides[phase]
        for dp in range(16):
            digit = dp // stride % 4
            pairs.append((2 * dp + mp, 2 * (dp + ((digit + step) % 4 - digit) * stride) + mp))
    return lax.ppermute(array, ("dp", "mp"), pairs)


def rotate_kernel(parts, _, *refs):
    for t in range(4):
        total = refs[t * parts][...].astype(F32)
        for i in range(1, parts):
            total = total + refs[t * parts + i][...].astype(F32)
        refs[4 * parts + t][...] = total.astype(BF)


def rotate_sum(arrays, digit):
    rows, lanes = arrays[0].shape
    rows //= 4
    cuts = 2 if rows % 32 == 0 and rows > 256 else 1
    tall = rows // cuts

    def spec(t):
        return pl.BlockSpec((tall, lanes), lambda i, d: (((d[0] + t) & 3) * cuts + i, 0))

    return pl.pallas_call(
        functools.partial(rotate_kernel, len(arrays)),
        grid_spec=pltpu.PrefetchScalarGridSpec(
            num_scalar_prefetch=1,
            grid=(cuts,),
            in_specs=[spec(t) for t in range(4) for _ in arrays],
            out_specs=[pl.BlockSpec((tall, lanes), lambda i, d: (i, 0))] * 4,
        ),
        out_shape=[jax.ShapeDtypeStruct((rows, lanes), BF)] * 4,
        compiler_params=params(dimension_semantics=("arbitrary",)),
        cost_estimate=cost(1_000_000, 6 * rows * lanes * len(arrays)),
        name="rotate_sum",
    )(digit, *(arrays * 4))


def add_all(blocks):
    total = blocks[0].astype(F32)
    for block in blocks[1:]:
        total = total + block.astype(F32)
    return total


def settle(digit_ref, refs, held_ref):
    outer, inner = digit_ref[0], digit_ref[1]
    piece = held_ref.shape[0] // 16
    for s, ref in enumerate(refs):
        for t in range(4):
            at = ((outer - s) & 3) * 4 + ((inner - t) & 3)
            held_ref[pl.ds(pl.multiple_of(at * piece, 16), piece), :] = ref[t * piece : (t + 1) * piece, :]


def lay_feed_kernel(digit_ref, a, b, c, d, up_ref, down_ref, proj_ref, held_ref):
    settle(digit_ref, (a, b, c, d), held_ref)
    depth, half = up_ref.shape
    for piece in range(half // depth):
        span = slice(piece * depth, (piece + 1) * depth)
        up_ref[:, span] = held_ref[span, :].astype(F32)
    down_ref[...] = held_ref[half : 2 * half, :].astype(F32)
    proj_ref[...] = held_ref[2 * half :, :].astype(F32)


SMEM = pl.BlockSpec(memory_space=pltpu.SMEM)
VMEM = pl.BlockSpec(memory_space=pltpu.VMEM)


def lay_feed(digits, blocks, depth, half, narrow):
    return pl.pallas_call(
        lay_feed_kernel,
        in_specs=[SMEM] + [VMEM] * 4,
        out_specs=[VMEM] * 3,
        out_shape=[
            jax.ShapeDtypeStruct((depth, half), F32),
            jax.ShapeDtypeStruct((half, depth), F32),
            jax.ShapeDtypeStruct((narrow, depth), F32),
        ],
        scratch_shapes=[pltpu.VMEM((2 * half + narrow, depth), BF)],
        compiler_params=params(),
        cost_estimate=cost(1_000_000, 8_000_000),
        name="lay_feed",
    )(digits, *blocks)


def lay_rest_kernel(
    halves, digit_ref, a, b, c, d,
    gw_ref, shift_ref, scale_ref, w1_ref, b1_ref, w2_ref, gb1_ref, bp_ref, g1_ref, h1_ref, bd_ref, g2_ref, h2_ref, held_ref,
):
    depth = gw_ref.shape[1]
    quarter = held_ref.shape[0] // 4
    small = None
    for s, ref in enumerate((a, b, c, d)):
        at = ((digit_ref[0] - s) & 3) * quarter
        held_ref[pl.ds(pl.multiple_of(at, 16), quarter), :] = ref[:quarter, :]
        term = ref[quarter:, :].astype(F32)
        small = term if small is None else small + term
    for g in range(halves):
        for i in range(3):
            at = (g * 3 + i) * depth
            gw_ref[i, :, g * LANES : (g + 1) * LANES] = held_ref[at : at + depth, :].astype(F32)
    row = 0

    def line(length):
        nonlocal row
        count = length // LANES
        out = cat([small[row + i : row + i + 1, :] for i in range(count)])
        row += count
        return out

    for ref in (bp_ref, g1_ref, h1_ref, bd_ref, g2_ref, h2_ref):
        ref[...] = line(ref.shape[1])
    w1_ref[...] = cat([line(w1_ref.shape[1]) for _ in range(2)], 0)
    b1_ref[...] = line(b1_ref.shape[1])
    gb1_ref[...] = line(gb1_ref.shape[1])
    heads, units = w2_ref.shape
    w2_ref[...] = cat([line(units) for _ in range(heads)], 0)
    groups = [[line(LANES) for _ in range(3)] for _ in range(halves)]
    for i in range(2):
        shift_ref[i : i + 1, :] = cat([group[i] for group in groups])
    scale = cat([group[2] for group in groups])
    pick = iota((1, scale.shape[1]), 1)
    scale_ref[...] = cat(
        [jnp.sum(jnp.where(pick == h * HEAD, scale, 0.0), axis=1, keepdims=True) for h in range(heads)]
    )


def lay_rest(digits, blocks, depth, halves, half, units):
    width = halves * LANES
    heads = halves * PER_GROUP
    shapes = [(3, depth, width), (2, width), (1, heads), (2, units), (1, units), (heads, units), (1, half)]
    shapes += [(1, depth)] * 6
    return pl.pallas_call(
        functools.partial(lay_rest_kernel, halves),
        in_specs=[SMEM] + [VMEM] * 4,
        out_specs=[VMEM] * len(shapes),
        out_shape=[jax.ShapeDtypeStruct(s, F32) for s in shapes],
        scratch_shapes=[pltpu.VMEM((halves * 3 * depth, LANES), BF)],
        compiler_params=params(),
        cost_estimate=cost(1_000_000, 8_000_000),
        name="lay_rest",
    )(digits, *blocks)


def on_device(
    size, tokens, query_key_value_matrix, query_value_bias, head_logit_scale, bias_net_first_weight,
    bias_net_first_bias, bias_net_second_weight, relative_pair_index, attention_out_weight, attention_out_bias,
    attention_norm_weight, attention_norm_bias, ffn_input_weight, hidden_ffn_bias, ffn_output_weight,
    output_ffn_bias, feedforward_norm_weight, feedforward_norm_bias, output_gradient,
):
    depth = tokens.shape[1]
    width = query_key_value_matrix.shape[2]
    halves = width // LANES
    half = ffn_input_weight.shape[1]
    units = bias_net_first_bias.shape[0]

    def pair(array):
        return array, swap(array)

    ws = pair(jnp.transpose(query_key_value_matrix, (1, 0, 2)))
    ps = pair(
        jnp.concatenate(
            [
                query_value_bias.astype(F32),
                jnp.repeat(jnp.exp(head_logit_scale.astype(F32)), HEAD)[None],
                hidden_ffn_bias.astype(F32).reshape(-1, TILE),
                jnp.zeros((5 - half // TILE, width), F32),
            ]
        )
    )
    net_seconds = pair(bias_net_second_weight.T)
    wos = pair(attention_out_weight)
    w1s = pair(ffn_input_weight)
    w2s = pair(ffn_output_weight)

    coords = jnp.asarray(coord_rows())
    columns = jnp.concatenate([bias_net_first_weight, bias_net_first_bias[None]]).T
    *saved, gather, scatter = attention_forward(relative_pair_index, tokens, ws, ps, coords, columns, net_seconds)
    vectors = [
        v.reshape(1, depth)
        for v in (
            attention_out_bias, attention_norm_weight, attention_norm_bias,
            output_ffn_bias, feedforward_norm_weight, feedforward_norm_bias,
        )
    ]
    block_out, d_middle, d_attn, own, other, vector_grads, gb1 = feed_forward(
        scatter, tokens, saved[1], wos, w1s, w2s, ps, vectors, output_gradient
    )
    inv_scale = 1.0 / jnp.concatenate([p[2, ::HEAD] for p in ps])[:, None]

    def backward(first, span, dctx, earlier=None):
        return attention_backward(first, span, halves, scatter, tokens, ps[first // halves], dctx, saved, earlier)

    def tail_small(results):
        return table_back(
            coords, columns, net_seconds, inv_scale, vector_grads, gb1,
            [r[2] for r in results], [r[3] for r in results],
        )

    def lines(array):
        return array.reshape(-1, LANES)

    dctx = context_grad(gather, d_attn, wos)
    if size == 16:
        dp, mp = lax.axis_index("dp"), lax.axis_index("mp")
        plan = ((1, 4), (4, 1))
        near, far = dp & 3, dp >> 2
        outer = jnp.where(mp == 0, near, far)
        inner = jnp.where(mp == 0, far, near)
        digits = jnp.stack([outer, inner])
        outer, inner = digits[:1], digits[1:]

        def spread(blocks, phase):
            return [send(b, plan, phase, t + 1) for t, b in enumerate(blocks)]

        got, dctx = tie(swap(other), dctx)
        blocks = rotate_sum([own, got], outer)
        blocks, dctx = tie(blocks, dctx)
        got = spread(blocks[1:], 0)
        theirs = backward(halves, halves, dctx)
        got, theirs, dctx = tie(got, theirs, dctx)
        blocks = rotate_sum([blocks[0]] + got, inner)
        blocks, dctx = tie(blocks, dctx)
        got = spread(blocks[1:], 1)
        mine = [backward(0, 1, dctx)]
        got, mine, dctx = tie(got, mine, dctx)
        low = add_all([blocks[0]] + got).astype(BF)
        low, dctx = tie(low, dctx)
        got = spread([low] * 3, 1)
        rest_got = swap(lines(theirs[0]))
        mine += [backward(1, 1, dctx, mine[0][0])]
        got, rest_got, mine = tie(got, rest_got, mine)
        rest = rotate_sum([lines(mine[-1][0]), rest_got], outer)
        low = jnp.concatenate([low] + got)
        rest, low = tie(rest, low)
        rest_got = spread(rest[1:], 0)
        gathered = spread([low] * 3, 0)
        results = mine + [theirs]
        small_own, small_other = tail_small(results)
        small = small_own + swap(small_other)
        rest_got, small = tie(rest_got, small)
        message = jnp.concatenate([add_all([rest[0]] + rest_got), small]).astype(BF)
        rest_got = spread([message] * 3, 1)
        tokens_grad = input_grad(d_middle, [r[1] for r in results], ws)
        gathered, rest_got, tokens_grad = tie(gathered, rest_got, tokens_grad)
        message = add_all([message] + rest_got).astype(BF)
        rest_got = spread([message] * 3, 0)
        feed = lay_feed(digits, [low] + gathered, depth, half, width)
        rest_got, feed = tie(rest_got, feed)
        final = lay_rest(digits, [message] + rest_got, depth, halves, half, units)
    else:
        results = [backward(0, halves, dctx), backward(halves, halves, dctx)]
        small_own, small_other = tail_small(results)
        tokens_grad = input_grad(d_middle, [r[1] for r in results], ws)
        digits = jnp.zeros((2,), jnp.int32)

        def total(array):
            return lax.psum(array, "dp").astype(BF)

        def quarters(array):
            rows = array.shape[0] // 4
            return [array[(-s % 4) * rows : (-s % 4 + 1) * rows] for s in range(4)]

        def pieces(array):
            return [jnp.concatenate(quarters(block)) for block in quarters(array)]

        feed = lay_feed(digits, pieces(total(own.astype(F32) + swap(other).astype(F32))), depth, half, width)
        rest = total(lines(results[0][0]).astype(F32) + swap(lines(results[1][0])).astype(F32))
        small = total(small_own + swap(small_other))
        none = jnp.zeros_like(small)
        blocks = [jnp.concatenate([block, none if s else small]) for s, block in enumerate(quarters(rest))]
        final = lay_rest(digits, blocks, depth, halves, half, units)

    grad_up, grad_down, grad_proj = feed
    grad_qkv, grad_shift, grad_scale, grad_w1, grad_b1, grad_w2, grad_hidden, *vec = final
    vec = [v.reshape(-1) for v in vec]
    return (
        block_out, tokens_grad, jnp.transpose(grad_qkv, (1, 0, 2)), grad_shift, grad_scale.reshape(-1),
        grad_w1, grad_b1.reshape(-1), grad_w2.T, grad_proj, vec[0], vec[1], vec[2],
        grad_up, grad_hidden.reshape(-1), grad_down, vec[3], vec[4], vec[5],
    )


def solution(mesh):
    in_specs = (
        P(("dp", "mp"), None), P(None, None, "mp"), P(None, "mp"), P("mp"), P(), P(), P(None, "mp"), P(),
        P("mp", None), P(), P(), P(), P(None, "mp"), P("mp"), P("mp", None), P(), P(), P(), P(("dp", "mp"), None),
    )
    out_specs = (
        P(("dp", "mp"), None), P(("dp", "mp"), None), P(None, None, "mp"), P(None, "mp"), P("mp"), P(), P(),
        P(None, "mp"), P("mp", None), P(), P(), P(), P(None, "mp"), P("mp"), P("mp", None), P(), P(), P(),
    )
    return jax.shard_map(
        functools.partial(on_device, mesh.shape["dp"]),
        mesh=mesh, in_specs=in_specs, out_specs=out_specs, check_vma=False,
    )
```

```python
import functools

import jax
import jax.numpy as jnp
import numpy as np
from jax import lax
from jax.experimental import pallas as pl
from jax.experimental.pallas import tpu as pltpu
from jax.sharding import PartitionSpec as P

SIDE = 24
WIN = SIDE * SIDE
TABLE_SIDE = 2 * SIDE - 1
PITCH = 2 * SIDE
WIDE = SIDE * PITCH
HEAD = 32
LANES = 128
PER_GROUP = LANES // HEAD
TILE = 256
SMALL_ROWS = 96
LOG2E = 1.4426950408889634
VMEM_BYTES = 58 * 1024 * 1024
BF = jnp.bfloat16
F32 = jnp.float32


def mm(left, right):
    return lax.dot_general(left, right, (((1,), (0,)), ((), ())), preferred_element_type=F32)


def mm_nt(left, right):
    return lax.dot_general(left, right, (((1,), (1,)), ((), ())), preferred_element_type=F32)


def mm_tn(left, right):
    return lax.dot_general(left, right, (((0,), (0,)), ((), ())), preferred_element_type=F32)


def split(values):
    high = values.astype(BF)
    return high, (values - high.astype(F32)).astype(BF)


def iota(shape, axis):
    return lax.broadcasted_iota(jnp.int32, shape, axis)


def cat(parts, axis=1):
    return jnp.concatenate(parts, axis=axis)


def flag(condition):
    return jnp.where(condition, 1.0, 0.0).astype(BF)


def column_sums(values):
    return jnp.sum(values, axis=0, keepdims=True)


def gelu_with_slope(values):
    cdf = 0.5 + 0.5 * lax.erf(values * 0.7071067811865476)
    bell = jnp.exp2(values * values * (-0.5 * LOG2E)) * 0.3989422804014327
    return values * cdf, cdf + values * bell


def cell_of_places(index_line, axis):
    row_part = (index_line * 22311) >> 20
    col_part = index_line - row_part * TABLE_SIDE
    if axis == 1:
        rows = jnp.max(row_part, axis=1, keepdims=True) - row_part
        cols = jnp.max(col_part, axis=1, keepdims=True) - col_part
    else:
        rows = row_part - jnp.min(row_part, axis=0, keepdims=True)
        cols = col_part - jnp.min(col_part, axis=0, keepdims=True)
    return rows * SIDE + cols


def head_sum_matrix():
    row = iota((2 * LANES, LANES), 0)
    col = iota((2 * LANES, LANES), 1)
    return flag(((row >> 5) & 3) == (col >> 5))


def head_sums(values, matrix):
    return mm(cat(split(values)), matrix)


def whole(shape):
    return pl.BlockSpec(shape, lambda *_: (0,) * len(shape))


def params(**more):
    return pltpu.CompilerParams(vmem_limit_bytes=VMEM_BYTES, **more)


def cost(flops, moved):
    return pl.CostEstimate(flops=flops, bytes_accessed=moved, transcendentals=0)


def coord_rows():
    def u(offset):
        c = np.float32(offset) * np.float32(8.0 / 15.0)
        return np.sign(c) * np.log2(np.abs(c) + np.float32(1.0)) / np.float32(3.0)

    lane = np.arange(WIDE)
    out = []
    for parity in range(2):
        e = 2 * (lane // PITCH) + parity
        k = lane % PITCH
        out.append(np.stack([u(SIDE - 1 - e), u(SIDE - 1 - k)] + [np.ones(WIDE)] + [np.zeros(WIDE)] * 5))
    return np.stack(out).astype(np.float32)


def table_pre(coord_ref, cols_ref, parity):
    pre = cols_ref[:, 0:1] * coord_ref[parity, 0:1, :] + cols_ref[:, 1:2] * coord_ref[parity, 1:2, :]
    return pre + cols_ref[:, 2:3]


def table_of(hidden, w2s):
    parts = split(hidden)
    z = cat([mm(w2, parts[0]) + mm(w2, parts[1]) for w2 in w2s], 0)
    return 16.0 / (1.0 + jnp.exp(-z))


def stat_lane(kind, group, head):
    return kind * 16 + group * PER_GROUP + head


def head_masks():
    lane = iota((1, LANES), 1) >> 5
    return [flag(lane == h) for h in range(PER_GROUP)]


def forward_kernel(
    images, halves, row_ref, col_ref, x_ref, w_a_ref, w_b_ref, p_a_ref, p_b_ref, coord_ref, cols_ref, w2_a_ref, w2_b_ref,
    e_hbm, ctx_ref, rest_ref, ql_ref, kl_ref, vl_ref, stat_ref, cell_ref, gather_ref, scatter_ref,
    e_ref, table_ref, pos_ref, logit_ref, mix_ref, sem,
):
    gather = flag(iota((WIN, WIN), 0) == cell_of_places(row_ref[0:1, :], 1))
    gather_ref[...] = gather
    scatter_ref[...] = flag(iota((WIN, WIN), 1) == cell_of_places(col_ref[:, 0:1], 0))
    stat_ref[...] = jnp.zeros_like(stat_ref)
    for m in range(images):
        rows = slice(m * WIN, (m + 1) * WIN)
        cell_ref[rows, :] = mm(gather, x_ref[rows, :]).astype(BF)
    for parity in range(2):
        hidden, _ = gelu_with_slope(table_pre(coord_ref, cols_ref, parity))
        table_ref[parity] = table_of(hidden, (w2_a_ref[...], w2_b_ref[...])) * LOG2E

    masks = head_masks()
    lane = iota((1, LANES), 1)
    row = iota((2 * LANES, LANES), 0) & (LANES - 1)
    col = iota((2 * LANES, LANES), 1)
    same = flag((row >> 5) == (col >> 5))
    lower = iota((1, WIDE), 1) % PITCH < SIDE
    left_half = iota((1, WIDE), 1) < WIN
    ones = jnp.ones((WIN, LANES), BF)

    def prepare(g):
        here = slice(g * LANES, (g + 1) * LANES)
        inner = slice(g % halves * LANES, (g % halves + 1) * LANES)
        w_ref, p_ref = (w_a_ref, p_a_ref) if g < halves else (w_b_ref, p_b_ref)
        w = cat([w_ref[i, :, inner] for i in range(3)])
        sums = [cat([same, flag(stat_lane(i, g, row >> 5) == col)]) for i in range(2)]
        stat_here = [(lane >> 2) == i * 4 + g for i in range(2)]
        out = []
        for m in range(images):
            rows = slice(m * WIN, (m + 1) * WIN)
            qkv = mm(cell_ref[rows, :], w)
            q = qkv[:, :LANES] + p_ref[0:1, inner]
            k = qkv[:, LANES : 2 * LANES]
            vl = (qkv[:, 2 * LANES :] + p_ref[1:2, inner]).astype(BF)
            rq = lax.rsqrt(head_sums(q * q, sums[0]) + 1.0)
            rk = lax.rsqrt(head_sums(k * k, sums[1]) + 1.0)
            ql = (q * rq[:, :LANES]).astype(BF)
            kl = (k * rk[:, :LANES]).astype(BF)
            stat = jnp.where(stat_here[0], rq[:, LANES:], stat_ref[rows, :])
            stat_ref[rows, :] = jnp.where(stat_here[1], rk[:, LANES:], stat)
            ql_ref[rows, here] = ql
            kl_ref[rows, here] = kl
            vl_ref[rows, here] = vl
            out.append((cat(split(ql.astype(F32) * (p_ref[2:3, inner] * LOG2E))), kl, vl))
        return out

    def bands_of(head):
        even = jnp.broadcast_to(table_ref[0, head : head + 1, :], (SIDE, WIDE))
        even = pltpu.roll(even, WIDE - SIDE + 1, 1, stride=1, stride_axis=0)
        odd = jnp.broadcast_to(table_ref[1, head : head + 1, :], (SIDE, WIDE))
        odd = pltpu.roll(odd, 1, 1, stride=1, stride_axis=0)
        return jnp.where(lower, even, odd)

    def place_bias(g, pair):
        slot = pair % 2
        one, two = (bands_of(g * PER_GROUP + 2 * pair + i) for i in range(2))
        for r in range(SIDE):
            offset = (SIDE - 1 - r) * SIDE
            pos_ref[slot, r * SIDE : (r + 1) * SIDE, :] = jnp.where(
                left_half, pltpu.roll(one, (WIDE - offset) % WIDE, 1), pltpu.roll(two, (WIDE + WIN - offset) % WIDE, 1)
            )

    pairs = PER_GROUP // 2
    units = [(g, pair, m) for g in range(2 * halves) for pair in range(pairs) for m in range(images)]
    ready = {}

    def score(at):
        g, pair, m = units[at]
        if (g, 0) not in ready:
            for i, operands in enumerate(prepare(g)):
                ready[g, i] = operands
        if m == 0:
            place_bias(g, pair)
        left, kl, _ = ready[g, m]
        keys = cat([kl * mask for mask in masks[2 * pair : 2 * pair + 2]], 0)
        logit_ref[at % 2] = mm_nt(left, cat([keys, keys]))

    def weigh(at):
        g, pair, m = units[at]
        e_ref[g, pair, m] = jnp.exp2(logit_ref[at % 2] + pos_ref[pair % 2]).astype(BF)
        pltpu.make_async_copy(e_ref.at[g, pair, m], e_hbm.at[g, pair, m], sem.at[g, pair, m]).start()

    def mix(at):
        g, pair, m = units[at]
        vl = ready[g, m][2]
        here = masks[2 * pair : 2 * pair + 2]
        values = cat([cat([vl * mask for mask in here], 0), cat([ones * mask for mask in here], 0)])
        mixed = mm(e_ref[g, pair, m], values)
        if pair == 0:
            mix_ref[m] = mixed
        elif pair < pairs - 1:
            mix_ref[m] += mixed
        else:
            mixed = mix_ref[m] + mixed
            rows = slice(m * WIN, (m + 1) * WIN)
            lanes = slice(g * LANES, (g + 1) * LANES)
            inverse = 1.0 / mixed[:, LANES:]
            high, low = split(mixed[:, :LANES] * inverse)
            ctx_ref[rows, lanes] = high
            rest_ref[rows, lanes] = low
            pick = flag(((row & (HEAD - 1)) == 0) & (stat_lane(2, g, row >> 5) == col))
            stat_ref[rows, :] += head_sums(inverse, pick)

    score(0)
    for at in range(len(units)):
        if at + 1 < len(units):
            score(at + 1)
        weigh(at)
        if at > 0:
            mix(at - 1)
    mix(len(units) - 1)
    for g, pair, m in units:
        pltpu.make_async_copy(e_ref.at[g, pair, m], e_hbm.at[g, pair, m], sem.at[g, pair, m]).wait()


def attention_forward(index, x, ws, ps, coords, columns, w2s):
    count, depth = x.shape
    images = count // WIN
    halves = ws[0].shape[2] // LANES
    groups = 2 * halves
    heads = groups * PER_GROUP
    wide = groups * LANES
    pairs = PER_GROUP // 2
    weights = (groups, pairs, images, WIN, 2 * WIN)
    low = jax.ShapeDtypeStruct((count, wide), BF)
    place = jax.ShapeDtypeStruct((WIN, WIN), BF)
    shapes = [low] * 5 + [jax.ShapeDtypeStruct((count, LANES), F32), jax.ShapeDtypeStruct((count, depth), BF), place, place]
    rest = [x, *ws, *ps, coords, columns, *w2s]
    return pl.pallas_call(
        functools.partial(forward_kernel, images, halves),
        grid=(1,),
        in_specs=[pl.BlockSpec((8, WIN), lambda i: (0, 0)), pl.BlockSpec((WIN, LANES), lambda i: (0, 0))]
        + [whole(a.shape) for a in rest],
        out_specs=[pl.BlockSpec(memory_space=pl.ANY)] + [whole(a.shape) for a in shapes],
        out_shape=[jax.ShapeDtypeStruct(weights, BF)] + shapes,
        scratch_shapes=[
            pltpu.VMEM(weights, BF),
            pltpu.VMEM((2, heads, WIDE), F32),
            pltpu.VMEM((2, WIN, 2 * WIN), F32),
            pltpu.VMEM((2, WIN, 2 * WIN), F32),
            pltpu.VMEM((images, WIN, 2 * LANES), F32),
            pltpu.SemaphoreType.DMA((groups, pairs, images)),
        ],
        compiler_params=params(dimension_semantics=("arbitrary",)),
        cost_estimate=cost(8_000_000_000, 40_000_000),
        name="attention_forward",
    )(index, index, *rest)


def norm_stats(values):
    center = values - jnp.mean(values, axis=1, keepdims=True)
    inverse = lax.rsqrt(jnp.mean(center * center, axis=1, keepdims=True) + 1e-05)
    return center * inverse, inverse


def norm_back(grad, unit, inverse, gain):
    scaled = grad * gain
    mean = jnp.mean(scaled, axis=1, keepdims=True)
    along = jnp.mean(scaled * unit, axis=1, keepdims=True)
    return inverse * (scaled - mean - unit * along)


def feed_kernel(
    images, scatter_ref, x_ref, mix_ref, wo_a_ref, wo_b_ref, p_a_ref, p_b_ref,
    bo_ref, g1_ref, s1_ref, b2_ref, g2_ref, s2_ref, w1_a_hbm, w1_b_hbm, w2_a_hbm, w2_b_hbm, og_hbm,
    out_hbm, dmid_hbm, da_hbm, own_hbm, other_hbm, small_ref, gb1_ref,
    w1_ref, w2_ref, og_ref, out_ref, da_ref, pack_ref, mid_ref,
    ctx_ref, low_ref, pre_ref, hid_ref, slope_ref, acc_ref, unit_ref, in_sem, out_sem,
):
    half = w1_ref.shape[2]
    depth = x_ref.shape[1]
    narrow = wo_a_ref.shape[0]
    tiles = 2 * half // TILE
    ps = (p_a_ref, p_b_ref)
    packed = (own_hbm, other_hbm)
    loads = [
        pltpu.make_async_copy(source, target, in_sem.at[i])
        for i, (source, target) in enumerate(
            (
                (w1_a_hbm, w1_ref.at[0]), (w1_b_hbm, w1_ref.at[1]), (w2_a_hbm, w2_ref.at[0]),
                (w2_b_hbm, w2_ref.at[1]), (og_hbm, og_ref),
            )
        )
    ]
    for load in loads:
        load.start()
    stores = []

    def store(source, target):
        copy = pltpu.make_async_copy(source, target, out_sem.at[len(stores)])
        copy.start()
        stores.append(copy)

    def place_of(tile):
        at = tile * TILE
        return at // half, slice(at % half, at % half + TILE)

    inverse_ones = []
    for m in range(images):
        rows = slice(m * WIN, (m + 1) * WIN)
        ctx = mm(scatter_ref[...], mix_ref[rows, :]).astype(BF)
        ctx_ref[rows, :] = ctx
        attn = mm(ctx[:, :narrow], wo_a_ref[...]) + mm(ctx[:, narrow:], wo_b_ref[...]) + bo_ref[...]
        unit_one, inverse = norm_stats(attn)
        inverse_ones.append(inverse)
        unit_ref[rows, :] = unit_one
        middle = x_ref[rows, :].astype(F32) + unit_one * g1_ref[...] + s1_ref[...]
        mid_ref[rows, :] = middle
        low_ref[rows, :] = middle.astype(BF)

    def up(tile):
        which, cols = place_of(tile)
        if cols.start == 0:
            loads[which].wait()
        row = 3 + cols.start // TILE
        pre_ref[tile % 2] = mm(low_ref[...], w1_ref[which, :, cols]) + ps[which][row : row + 1, :]

    def down(tile):
        which, cols = place_of(tile)
        if cols.start == 0:
            loads[2 + which].wait()
        term = mm(hid_ref[which, :, cols], w2_ref[which, cols, :])
        if tile == 0:
            acc_ref[...] = term
        else:
            acc_ref[...] += term

    up(0)
    for tile in range(tiles):
        if tile + 1 < tiles:
            up(tile + 1)
        which, cols = place_of(tile)
        hidden, slope = gelu_with_slope(pre_ref[tile % 2])
        hid_ref[which, :, cols] = hidden.astype(BF)
        slope_ref[which, :, cols] = slope
        if tile > 0:
            down(tile - 1)
    down(tiles - 1)

    loads[4].wait()
    sums = [jnp.zeros((1, depth), F32)] * 3
    for m in range(images):
        rows = slice(m * WIN, (m + 1) * WIN)
        unit_two, inverse_two = norm_stats(acc_ref[rows, :] + b2_ref[...])
        out_ref[rows, :] = (mid_ref[rows, :] + (unit_two * g2_ref[...] + s2_ref[...])).astype(BF)
        grad = og_ref[rows, :].astype(F32)
        d_mlp = norm_back(grad, unit_two, inverse_two, g2_ref[...])
        terms = (column_sums(d_mlp), column_sums(grad * unit_two), column_sums(grad))
        sums = [a + b for a, b in zip(sums, terms)]
        da_ref[rows, :] = d_mlp.astype(BF)
        acc_ref[rows, :] = grad
    store(out_ref, out_hbm)
    for i in range(3):
        small_ref[3 + i : 4 + i, :] = sums[i]

    for tile in range(tiles):
        which, cols = place_of(tile)
        d_pre = mm_nt(da_ref[...], w2_ref[which, cols, :]) * slope_ref[which, :, cols]
        gb1_ref[which : which + 1, cols] = column_sums(d_pre)
        d_pre_low = d_pre.astype(BF)
        at = cols.start
        pack_ref[which, half + at : half + at + TILE, :] = mm_tn(hid_ref[which, :, cols], da_ref[...]).astype(BF)
        rows = slice(at // depth * depth, (at // depth + 1) * depth)
        pack_ref[which, rows, at % depth : at % depth + TILE] = mm_tn(low_ref[...], d_pre_low).astype(BF)
        acc_ref[...] += mm_nt(d_pre_low, w1_ref[which, :, cols])
        if at + TILE == half:
            span = pl.ds(0, 2 * half)
            store(pack_ref.at[which, span], packed[which].at[span])
    store(acc_ref, dmid_hbm)

    sums = [jnp.zeros((1, depth), F32)] * 3
    for m in range(images):
        rows = slice(m * WIN, (m + 1) * WIN)
        d_middle = acc_ref[rows, :]
        unit_one = unit_ref[rows, :]
        d_attn = norm_back(d_middle, unit_one, inverse_ones[m], g1_ref[...])
        terms = (column_sums(d_attn), column_sums(d_middle * unit_one), column_sums(d_middle))
        sums = [a + b for a, b in zip(sums, terms)]
        da_ref[rows, :] = d_attn.astype(BF)
    store(da_ref, da_hbm)
    for i in range(3):
        small_ref[i : i + 1, :] = sums[i]
    span = pl.ds(2 * half, narrow)
    for which in range(2):
        pack_ref[which, 2 * half : 2 * half + narrow, :] = mm_tn(
            ctx_ref[:, which * narrow : (which + 1) * narrow], da_ref[...]
        ).astype(BF)
        store(pack_ref.at[which, span], packed[which].at[span])
    for copy in stores:
        copy.wait()


def feed_forward(scatter, x, ctx, wos, w1s, w2s, ps, vectors, cotangent):
    count, depth = x.shape
    images = count // WIN
    narrow = wos[0].shape[0]
    half = w1s[0].shape[1]
    packed = 2 * half + narrow
    far = pl.BlockSpec(memory_space=pl.ANY)
    near = pl.BlockSpec(memory_space=pltpu.VMEM)
    low = pltpu.VMEM((count, depth), BF)
    full = pltpu.VMEM((count, depth), F32)
    return pl.pallas_call(
        functools.partial(feed_kernel, images),
        in_specs=[near] * 13 + [far] * 5,
        out_specs=[far] * 5 + [near] * 2,
        out_shape=[
            jax.ShapeDtypeStruct((count, depth), BF),
            jax.ShapeDtypeStruct((count, depth), F32),
            jax.ShapeDtypeStruct((count, depth), BF),
            jax.ShapeDtypeStruct((packed, depth), BF),
            jax.ShapeDtypeStruct((packed, depth), BF),
            jax.ShapeDtypeStruct((8, depth), F32),
            jax.ShapeDtypeStruct((2, half), F32),
        ],
        scratch_shapes=[
            pltpu.VMEM((2, depth, half), BF),
            pltpu.VMEM((2, half, depth), BF),
            low, low, low,
            pltpu.VMEM((2, packed, depth), BF),
            full,
            pltpu.VMEM((count, 2 * narrow), BF),
            low,
            pltpu.VMEM((2, count, TILE), F32),
            pltpu.VMEM((2, count, half), BF),
            pltpu.VMEM((2, count, half), F32),
            full, full,
            pltpu.SemaphoreType.DMA((5,)),
            pltpu.SemaphoreType.DMA((7,)),
        ],
        compiler_params=params(),
        cost_estimate=cost(2 * count * depth * (2 * depth + 12 * half), 30_000_000),
        name="feed_forward",
    )(scatter, x, ctx, *wos, *ps, *vectors, *w1s, *w2s, cotangent)


def context_grad_kernel(images, gather_ref, da_ref, wo_a_ref, wo_b_ref, out_ref):
    for m in range(images):
        rows = slice(m * WIN, (m + 1) * WIN)
        grad = cat([mm_nt(da_ref[rows, :], wo_a_ref[...]), mm_nt(da_ref[rows, :], wo_b_ref[...])]).astype(BF)
        out_ref[rows, :] = mm(gather_ref[...], grad).astype(BF)


def context_grad(gather, d_attn, wos):
    return pl.pallas_call(
        functools.partial(context_grad_kernel, d_attn.shape[0] // WIN),
        out_shape=jax.ShapeDtypeStruct((d_attn.shape[0], 2 * wos[0].shape[0]), BF),
        compiler_params=params(),
        cost_estimate=cost(2_000_000_000, 5_000_000),
        name="context_grad",
    )(gather, d_attn, *wos)


def backward_kernel(
    images, first, span, x_ref, p_ref, dctx_ref, ctx_ref, rest_ref, ql_ref, kl_ref, vl_ref, stat_ref, e_hbm,
    gw_ref, dqkv_ref, dm_ref, small_ref,
    e_ref, prob_ref, low_ref, sum_ref, duq_ref, dkt_ref, dvt_ref, sem,
):
    pairs = PER_GROUP // 2
    units = [(g, pair, m) for g in range(span) for pair in range(pairs) for m in range(images)]
    loads = {
        unit: pltpu.make_async_copy(e_hbm.at[first + unit[0], unit[1], unit[2]], e_ref.at[unit], sem.at[unit])
        for unit in units
    }
    for load in loads.values():
        load.start()
    masks = head_masks()
    summing = head_sum_matrix()
    unit_matrix = flag(iota((LANES, LANES), 0) == iota((LANES, LANES), 1))
    shape = (2 * LANES, 3 * LANES)
    col = iota(shape, 1)
    in_head = iota((1, LANES), 1) & (HEAD - 1)
    left_half = iota((1, WIDE), 1) < WIN
    spots = flag(in_head < 2)
    ready = {}
    sums = [[jnp.zeros((1, LANES), F32)] * 3 for _ in range(span)]

    def prepare(g, m):
        here = slice(g * LANES, (g + 1) * LANES)
        rows = slice(m * WIN, (m + 1) * WIN)
        spread = flag((iota(shape, 0) & (LANES - 1)) == stat_lane(col >> 7, first + g, (col & (LANES - 1)) >> 5))
        stats = head_sums(stat_ref[rows, :], spread)
        grad = (dctx_ref[rows, here].astype(F32) * (stats[:, 2 * LANES :] * p_ref[2:3, here])).astype(BF)
        mix = ctx_ref[rows, here].astype(F32) + rest_ref[rows, here].astype(F32)
        d_high, d_low = split(-head_sums(grad.astype(F32) * mix, summing))
        left = cat([grad, jnp.where(in_head == 0, d_high, d_low)])
        q_t = mm_nt(unit_matrix, ql_ref[rows, here]).astype(BF)
        grad_t = mm_nt(unit_matrix, grad).astype(BF)
        return left, q_t, grad_t, stats[:, : 2 * LANES]

    def score(at):
        g, pair, m = units[at]
        if (g, m) not in ready:
            ready[g, m] = prepare(g, m)
        vl = vl_ref[m * WIN : (m + 1) * WIN, g * LANES : (g + 1) * LANES]
        here = masks[2 * pair : 2 * pair + 2]
        right = cat([cat([vl * mask, jnp.broadcast_to(spots * mask, (WIN, LANES))]) for mask in here], 0)
        prob_ref[at % 2] = mm_nt(ready[g, m][0], right)

    def weigh(at):
        g, pair, m = units[at]
        loads[g, pair, m].wait()
        d_cos = e_ref[g, pair, m].astype(F32) * prob_ref[at % 2]
        low_ref[at % 2] = d_cos.astype(BF)
        if m == 0:
            sum_ref[pair % 2] = d_cos
        else:
            sum_ref[pair % 2] += d_cos
        if m == images - 1:
            one, two = None, None
            for r in range(SIDE):
                offset = (SIDE - 1 - r) * SIDE
                band = sum_ref[pair % 2, r * SIDE : (r + 1) * SIDE, :]
                left = pltpu.roll(jnp.where(left_half, band, 0.0), offset, 1)
                right = pltpu.roll(jnp.where(left_half, 0.0, band), (offset + WIN) % WIDE, 1)
                one = left if one is None else one + left
                two = right if two is None else two + right
            dm_ref[g * PER_GROUP + 2 * pair] = one
            dm_ref[g * PER_GROUP + 2 * pair + 1] = two

    def spend(at):
        g, pair, m = units[at]
        rows = slice(m * WIN, (m + 1) * WIN)
        here = slice(g * LANES, (g + 1) * LANES)
        _, q_t, grad_t, stats = ready[g, m]
        kl, ql = kl_ref[rows, here], ql_ref[rows, here]
        d_low = low_ref[at % 2]
        duq = mm(d_low, cat([kl * mask for mask in masks[2 * pair : 2 * pair + 2]], 0))
        head = pair * 2 * HEAD
        for ref, source, factor in ((dkt_ref, q_t, d_low), (dvt_ref, grad_t, e_ref[g, pair, m])):
            both = mm(source[head : head + 2 * HEAD], factor)
            ref[m, head : head + HEAD, :] = both[:HEAD, : ref.shape[2]]
            ref[m, head + HEAD : head + 2 * HEAD, :] = pltpu.roll(both[HEAD:], WIN, 1)[:, : ref.shape[2]]
        if pair == 0:
            duq_ref[m] = duq
        if 0 < pair < pairs - 1:
            duq_ref[m] += duq
        if pair == pairs - 1:
            duq = duq_ref[m] + duq
            uq = ql.astype(F32)
            along_q = head_sums(uq * duq, summing)
            dq = stats[:, :LANES] * (duq - uq * along_q)
            uk = kl.astype(F32)
            duk = jnp.transpose(dkt_ref[m])[:WIN]
            dk = stats[:, LANES:] * (duk - uk * head_sums(uk * duk, summing))
            dv = jnp.transpose(dvt_ref[m])[:WIN] / p_ref[2:3, here]
            sums[g] = [a + column_sums(t) for a, t in zip(sums[g], (dq, dv, along_q))]
            for i, grads in enumerate((dq, dk, dv)):
                lanes = (i * span + g) * LANES
                dqkv_ref[rows, lanes : lanes + LANES] = grads.astype(BF)

    score(0)
    for at in range(len(units)):
        if at + 1 < len(units):
            score(at + 1)
        weigh(at)
        if at > 0:
            spend(at - 1)
    spend(len(units) - 1)
    for g in range(span):
        for i in range(3):
            small_ref[g, i : i + 1, :] = sums[g][i]
    for i in range(3):
        gw = mm_tn(x_ref[...], dqkv_ref[:, i * span * LANES : (i + 1) * span * LANES]).astype(BF)
        for g in range(span):
            gw_ref[g, i] = gw[:, g * LANES : (g + 1) * LANES]


def attention_backward(first, span, x, p, dctx, saved):
    e, *blocks, stat = saved
    count, depth = x.shape
    images = count // WIN
    padded = -(-WIN // LANES) * LANES
    block = pl.BlockSpec((count, span * LANES), lambda i: (0, first // span))
    shapes = [
        jax.ShapeDtypeStruct((span, 3, depth, LANES), BF),
        jax.ShapeDtypeStruct((count, span * 3 * LANES), BF),
        jax.ShapeDtypeStruct((span * PER_GROUP, SIDE, WIDE), F32),
        jax.ShapeDtypeStruct((span, 8, LANES), F32),
    ]
    return pl.pallas_call(
        functools.partial(backward_kernel, images, first, span),
        grid=(1,),
        in_specs=[whole(x.shape), whole(p.shape)] + [block] * 6
        + [whole(stat.shape), pl.BlockSpec(memory_space=pl.ANY)],
        out_specs=[whole(a.shape) for a in shapes],
        out_shape=shapes,
        scratch_shapes=[
            pltpu.VMEM((span,) + e.shape[1:], BF),
            pltpu.VMEM((2, WIN, 2 * WIN), F32),
            pltpu.VMEM((2, WIN, 2 * WIN), BF),
            pltpu.VMEM((2, WIN, 2 * WIN), F32),
            pltpu.VMEM((images, WIN, LANES), F32),
            pltpu.VMEM((images, LANES, padded), F32),
            pltpu.VMEM((images, LANES, padded), F32),
            pltpu.SemaphoreType.DMA((span,) + e.shape[1:3]),
        ],
        compiler_params=params(dimension_semantics=("arbitrary",)),
        cost_estimate=cost(8_000_000_000 * span, 20_000_000 * span),
        name=f"attention_backward_{first}",
    )(x, p, dctx, *blocks, stat, e)


def input_grad_kernel(scatter_ref, dmid_ref, da_ref, db_ref, w_a_ref, w_b_ref, out_ref):
    wide = w_a_ref.shape[2]
    total = None
    for grad_ref, w_ref in ((da_ref, w_a_ref), (db_ref, w_b_ref)):
        for i in range(3):
            term = mm_nt(grad_ref[:, i * wide : (i + 1) * wide], w_ref[i])
            total = term if total is None else total + term
    high, low = split(total)
    out_ref[...] = dmid_ref[...] + mm(scatter_ref[...], high) + mm(scatter_ref[...], low)


def input_grad(scatter, d_middle, grads, ws):
    count, depth = d_middle.shape
    rows = lambda width: pl.BlockSpec((WIN, width), lambda i: (i, 0))
    return pl.pallas_call(
        input_grad_kernel,
        grid=(count // WIN,),
        in_specs=[whole(scatter.shape), rows(depth)] + [rows(g.shape[1]) for g in grads] + [whole(w.shape) for w in ws],
        out_specs=rows(depth),
        out_shape=jax.ShapeDtypeStruct(d_middle.shape, F32),
        compiler_params=params(dimension_semantics=("arbitrary",)),
        cost_estimate=cost(3_000_000_000, 12_000_000),
        name="input_grad",
    )(scatter, d_middle, *grads, *ws)


def table_back_kernel(spans, coord_ref, cols_ref, w2_a_ref, w2_b_ref, scale_ref, vec_ref, gb1_ref, *refs):
    calls = len(spans)
    dms, smalls, (own_ref, other_ref) = refs[:calls], refs[calls : 2 * calls], refs[2 * calls :]
    lower = iota((1, WIDE), 1) % PITCH < SIDE
    even, odd = [], []
    for ref in dms:
        e = jnp.zeros((ref.shape[0], WIDE), F32)
        o = jnp.zeros((ref.shape[0], WIDE), F32)
        for c in range(SIDE):
            slab = ref[:, c, :]
            e = e + pltpu.roll(jnp.where(lower, slab, 0.0), (SIDE - 1 - c) % WIDE, 1)
            o = o + pltpu.roll(jnp.where(lower, 0.0, slab), (-1 - c) % WIDE, 1)
        even.append(e)
        odd.append(o)
    w2s = (w2_a_ref[...], w2_b_ref[...])
    dw2 = None
    dcols = None
    for parity, grads in enumerate((even, odd)):
        hidden, slope = gelu_with_slope(table_pre(coord_ref, cols_ref, parity))
        table = table_of(hidden, w2s)
        dz = cat(grads, 0) * scale_ref[...] * table * (1.0 - table * 0.0625)
        hidden_high, hidden_low = split(hidden)
        dz_high, dz_low = split(dz)
        term = mm_nt(dz_high, hidden_high) + mm_nt(dz_high, hidden_low) + mm_nt(dz_low, hidden_high)
        dw2 = term if dw2 is None else dw2 + term
        w2 = cat(w2s, 0)
        high, low = split((mm_tn(w2, dz_high) + mm_tn(w2, dz_low)) * slope)
        c_high, c_low = split(coord_ref[parity])
        term = mm_nt(c_high, high) + mm_nt(c_high, low) + mm_nt(c_low, high)
        dcols = term if dcols is None else dcols + term
    heads = w2s[0].shape[0]
    groups = [(ref, g) for ref, span in zip(smalls, spans) for g in range(span)]
    for which, out in enumerate((own_ref, other_ref)):
        lines = [(vec_ref, i) for i in range(6)] + [(dcols, i) for i in range(3)] + [(gb1_ref, which)]
        row = 0
        for source, i in lines + [(dw2, which * heads + h) for h in range(heads)]:
            for at in range(0, source.shape[1], LANES):
                out[row : row + 1, :] = source[i : i + 1, at : at + LANES]
                row += 1
        for ref, g in groups[which * len(groups) // 2 : (which + 1) * len(groups) // 2]:
            for i in range(3):
                out[row : row + 1, :] = ref[g, i : i + 1, :]
                row += 1
        out[row:, :] = jnp.zeros((SMALL_ROWS - row, LANES), F32)


def table_back(coords, columns, w2s, inv_scale, vectors, gb1, dms, smalls):
    small = jax.ShapeDtypeStruct((SMALL_ROWS, LANES), F32)
    return pl.pallas_call(
        functools.partial(table_back_kernel, [s.shape[0] for s in smalls]),
        out_shape=(small, small),
        compiler_params=params(),
        cost_estimate=cost(1_000_000_000, 10_000_000),
        name="table_back",
    )(coords, columns, *w2s, inv_scale, vectors, gb1, *dms, *smalls)


def swap(array):
    return lax.ppermute(array, "mp", [(0, 1), (1, 0)])


def tie(*trees):
    leaves, kind = jax.tree.flatten(trees)
    return jax.tree.unflatten(kind, lax.optimization_barrier(leaves))


def send(array, plan, phase, step):
    pairs = []
    for mp, strides in enumerate(plan):
        stride = strides[phase]
        for dp in range(16):
            digit = dp // stride % 4
            pairs.append((2 * dp + mp, 2 * (dp + ((digit + step) % 4 - digit) * stride) + mp))
    return lax.ppermute(array, ("dp", "mp"), pairs)


def rotate_kernel(parts, _, *refs):
    for t in range(4):
        total = refs[t * parts][...].astype(F32)
        for i in range(1, parts):
            total = total + refs[t * parts + i][...].astype(F32)
        refs[4 * parts + t][...] = total.astype(BF)


def rotate_sum(arrays, digit):
    rows, lanes = arrays[0].shape
    rows //= 4
    cuts = 2 if rows % 32 == 0 and rows > 256 else 1
    tall = rows // cuts

    def spec(t):
        return pl.BlockSpec((tall, lanes), lambda i, d: (((d[0] + t) & 3) * cuts + i, 0))

    return pl.pallas_call(
        functools.partial(rotate_kernel, len(arrays)),
        grid_spec=pltpu.PrefetchScalarGridSpec(
            num_scalar_prefetch=1,
            grid=(cuts,),
            in_specs=[spec(t) for t in range(4) for _ in arrays],
            out_specs=[pl.BlockSpec((tall, lanes), lambda i, d: (i, 0))] * 4,
        ),
        out_shape=[jax.ShapeDtypeStruct((rows, lanes), BF)] * 4,
        compiler_params=params(dimension_semantics=("arbitrary",)),
        cost_estimate=cost(1_000_000, 6 * rows * lanes * len(arrays)),
        name="rotate_sum",
    )(digit, *(arrays * 4))


def add_all(blocks):
    total = blocks[0].astype(F32)
    for block in blocks[1:]:
        total = total + block.astype(F32)
    return total


def settle(digit_ref, refs, held_ref):
    quarter = held_ref.shape[0] // 4
    for s, ref in enumerate(refs):
        at = ((digit_ref[0] - s) & 3) * quarter
        held_ref[pl.ds(pl.multiple_of(at, 16), quarter), :] = ref[:quarter, :]


def lay_feed_kernel(digit_ref, a, b, c, d, up_ref, down_ref, proj_ref, held_ref):
    settle(digit_ref, (a, b, c, d), held_ref)
    depth, half = up_ref.shape
    for piece in range(half // depth):
        span = slice(piece * depth, (piece + 1) * depth)
        up_ref[:, span] = held_ref[span, :].astype(F32)
    down_ref[...] = held_ref[half : 2 * half, :].astype(F32)
    proj_ref[...] = held_ref[2 * half :, :].astype(F32)


SMEM = pl.BlockSpec(memory_space=pltpu.SMEM)
VMEM = pl.BlockSpec(memory_space=pltpu.VMEM)


def lay_feed(outer, blocks, depth, half, narrow):
    return pl.pallas_call(
        lay_feed_kernel,
        in_specs=[SMEM] + [VMEM] * 4,
        out_specs=[VMEM] * 3,
        out_shape=[
            jax.ShapeDtypeStruct((depth, half), F32),
            jax.ShapeDtypeStruct((half, depth), F32),
            jax.ShapeDtypeStruct((narrow, depth), F32),
        ],
        scratch_shapes=[pltpu.VMEM((2 * half + narrow, depth), BF)],
        compiler_params=params(),
        cost_estimate=cost(1_000_000, 8_000_000),
        name="lay_feed",
    )(outer, *blocks)


def lay_rest_kernel(
    halves, digit_ref, a, b, c, d,
    gw_ref, shift_ref, scale_ref, w1_ref, b1_ref, w2_ref, gb1_ref, bp_ref, g1_ref, h1_ref, bd_ref, g2_ref, h2_ref, held_ref,
):
    depth = gw_ref.shape[1]
    settle(digit_ref, (a, b, c, d), held_ref)
    quarter = held_ref.shape[0] // 4
    small = add_all([ref[quarter:, :] for ref in (a, b, c, d)])
    for g in range(halves):
        for i in range(3):
            at = (g * 3 + i) * depth
            gw_ref[i, :, g * LANES : (g + 1) * LANES] = held_ref[at : at + depth, :].astype(F32)
    row = 0

    def line(length):
        nonlocal row
        count = length // LANES
        out = cat([small[row + i : row + i + 1, :] for i in range(count)])
        row += count
        return out

    for ref in (bp_ref, g1_ref, h1_ref, bd_ref, g2_ref, h2_ref):
        ref[...] = line(ref.shape[1])
    w1_ref[...] = cat([line(w1_ref.shape[1]) for _ in range(2)], 0)
    b1_ref[...] = line(b1_ref.shape[1])
    gb1_ref[...] = line(gb1_ref.shape[1])
    heads, units = w2_ref.shape
    w2_ref[...] = cat([line(units) for _ in range(heads)], 0)
    groups = [[line(LANES) for _ in range(3)] for _ in range(halves)]
    for i in range(2):
        shift_ref[i : i + 1, :] = cat([group[i] for group in groups])
    scale = cat([group[2] for group in groups])
    pick = iota((1, scale.shape[1]), 1)
    scale_ref[...] = cat(
        [jnp.sum(jnp.where(pick == h * HEAD, scale, 0.0), axis=1, keepdims=True) for h in range(heads)]
    )


def lay_rest(outer, blocks, depth, halves, half, units):
    width = halves * LANES
    heads = halves * PER_GROUP
    shapes = [(3, depth, width), (2, width), (1, heads), (2, units), (1, units), (heads, units), (1, half)]
    shapes += [(1, depth)] * 6
    return pl.pallas_call(
        functools.partial(lay_rest_kernel, halves),
        in_specs=[SMEM] + [VMEM] * 4,
        out_specs=[VMEM] * len(shapes),
        out_shape=[jax.ShapeDtypeStruct(s, F32) for s in shapes],
        scratch_shapes=[pltpu.VMEM((halves * 3 * depth, LANES), BF)],
        compiler_params=params(),
        cost_estimate=cost(1_000_000, 8_000_000),
        name="lay_rest",
    )(outer, *blocks)


def on_device(
    size, tokens, query_key_value_matrix, query_value_bias, head_logit_scale, bias_net_first_weight,
    bias_net_first_bias, bias_net_second_weight, relative_pair_index, attention_out_weight, attention_out_bias,
    attention_norm_weight, attention_norm_bias, ffn_input_weight, hidden_ffn_bias, ffn_output_weight,
    output_ffn_bias, feedforward_norm_weight, feedforward_norm_bias, output_gradient,
):
    depth = tokens.shape[1]
    width = query_key_value_matrix.shape[2]
    halves = width // LANES
    half = ffn_input_weight.shape[1]
    units = bias_net_first_bias.shape[0]

    def pair(array):
        return array, swap(array)

    ws = pair(jnp.transpose(query_key_value_matrix, (1, 0, 2)))
    ps = pair(
        jnp.concatenate(
            [
                query_value_bias.astype(F32),
                jnp.repeat(jnp.exp(head_logit_scale.astype(F32)), HEAD)[None],
                hidden_ffn_bias.astype(F32).reshape(-1, TILE),
                jnp.zeros((5 - half // TILE, width), F32),
            ]
        )
    )
    net_seconds = pair(bias_net_second_weight.T)
    wos = pair(attention_out_weight)
    w1s = pair(ffn_input_weight)
    w2s = pair(ffn_output_weight)

    coords = jnp.asarray(coord_rows())
    columns = jnp.concatenate([bias_net_first_weight, bias_net_first_bias[None]]).T
    *saved, cells, gather, scatter = attention_forward(relative_pair_index, tokens, ws, ps, coords, columns, net_seconds)
    vectors = [
        v.reshape(1, depth)
        for v in (
            attention_out_bias, attention_norm_weight, attention_norm_bias,
            output_ffn_bias, feedforward_norm_weight, feedforward_norm_bias,
        )
    ]
    block_out, d_middle, d_attn, own, other, vector_grads, gb1 = feed_forward(
        scatter, tokens, saved[1], wos, w1s, w2s, ps, vectors, output_gradient
    )
    inv_scale = 1.0 / jnp.concatenate([p[2, ::HEAD] for p in ps])[:, None]

    def backward(which, dctx):
        return attention_backward(which * halves, halves, cells, ps[which], dctx, saved)

    def tail_small(results):
        return table_back(
            coords, columns, net_seconds, inv_scale, vector_grads, gb1,
            [r[2] for r in results], [r[3] for r in results],
        )

    def lines(array):
        return array.reshape(-1, LANES)

    dctx = context_grad(gather, d_attn, wos)
    if size == 16:
        dp, mp = lax.axis_index("dp"), lax.axis_index("mp")
        plan = ((1, 4), (4, 1))
        near, far = dp & 3, dp >> 2
        outer = jnp.where(mp == 0, near, far).reshape(1)

        def spread(blocks, phase):
            return [send(b, plan, phase, t + 1) for t, b in enumerate(blocks)]

        got, dctx = tie(swap(other), dctx)
        blocks = rotate_sum([own, got], outer)
        blocks, dctx = tie(blocks, dctx)
        got = spread(blocks[1:], 0)
        theirs = backward(1, dctx)
        got, theirs, dctx = tie(got, theirs, dctx)
        low = add_all([blocks[0]] + got).astype(BF)
        low, dctx = tie(low, dctx)
        got = spread([low] * 3, 1)
        rest_got = swap(lines(theirs[0]))
        mine = backward(0, dctx)
        got, rest_got, mine = tie(got, rest_got, mine)
        low = add_all([low] + got).astype(BF)
        rest = rotate_sum([lines(mine[0]), rest_got], outer)
        rest, low = tie(rest, low)
        rest_got = spread(rest[1:], 0)
        gathered = spread([low] * 3, 0)
        results = [mine, theirs]
        small_own, small_other = tail_small(results)
        small = small_own + swap(small_other)
        rest_got, small, gathered[0] = tie(rest_got, small, gathered[0])
        message = jnp.concatenate([add_all([rest[0]] + rest_got), small]).astype(BF)
        rest_got = spread([message] * 3, 1)
        tokens_grad = input_grad(scatter, d_middle, [r[1] for r in results], ws)
        rest_got, tokens_grad = tie(rest_got, tokens_grad)
        message = add_all([message] + rest_got).astype(BF)
        rest_got = spread([message] * 3, 0)
        feed = lay_feed(outer, [low] + gathered, depth, half, width)
        rest_got, feed = tie(rest_got, feed)
        final = lay_rest(outer, [message] + rest_got, depth, halves, half, units)
    else:
        results = [backward(0, dctx), backward(1, dctx)]
        small_own, small_other = tail_small(results)
        tokens_grad = input_grad(scatter, d_middle, [r[1] for r in results], ws)
        outer = jnp.zeros((1,), jnp.int32)

        def total(array):
            return lax.psum(array, "dp").astype(BF)

        def quarters(array):
            rows = array.shape[0] // 4
            return [array[(-s % 4) * rows : (-s % 4 + 1) * rows] for s in range(4)]

        feed = lay_feed(outer, quarters(total(own.astype(F32) + swap(other).astype(F32))), depth, half, width)
        rest = total(lines(results[0][0]).astype(F32) + swap(lines(results[1][0])).astype(F32))
        small = total(small_own + swap(small_other))
        none = jnp.zeros_like(small)
        blocks = [jnp.concatenate([block, none if s else small]) for s, block in enumerate(quarters(rest))]
        final = lay_rest(outer, blocks, depth, halves, half, units)

    grad_up, grad_down, grad_proj = feed
    grad_qkv, grad_shift, grad_scale, grad_w1, grad_b1, grad_w2, grad_hidden, *vec = final
    vec = [v.reshape(-1) for v in vec]
    return (
        block_out, tokens_grad, jnp.transpose(grad_qkv, (1, 0, 2)), grad_shift, grad_scale.reshape(-1),
        grad_w1, grad_b1.reshape(-1), grad_w2.T, grad_proj, vec[0], vec[1], vec[2],
        grad_up, grad_hidden.reshape(-1), grad_down, vec[3], vec[4], vec[5],
    )


def solution(mesh):
    in_specs = (
        P(("dp", "mp"), None), P(None, None, "mp"), P(None, "mp"), P("mp"), P(), P(), P(None, "mp"), P(),
        P("mp", None), P(), P(), P(), P(None, "mp"), P("mp"), P("mp", None), P(), P(), P(), P(("dp", "mp"), None),
    )
    out_specs = (
        P(("dp", "mp"), None), P(("dp", "mp"), None), P(None, None, "mp"), P(None, "mp"), P("mp"), P(), P(),
        P(None, "mp"), P("mp", None), P(), P(), P(), P(None, "mp"), P("mp"), P("mp", None), P(), P(), P(),
    )
    return jax.shard_map(
        functools.partial(on_device, mesh.shape["dp"]),
        mesh=mesh, in_specs=in_specs, out_specs=out_specs, check_vma=False,
    )
```

```python
import functools

import jax
import jax.numpy as jnp
import numpy as np
from jax import lax
from jax.experimental import pallas as pl
from jax.experimental.pallas import tpu as pltpu
from jax.sharding import PartitionSpec as P

SIDE = 24
WIN = SIDE * SIDE
TABLE_SIDE = 2 * SIDE - 1
PITCH = 2 * SIDE
WIDE = SIDE * PITCH
HEAD = 32
LANES = 128
PER_GROUP = LANES // HEAD
TILE = 256
SMALL_ROWS = 96
LOG2E = 1.4426950408889634
MIB = 1024 * 1024
BF = jnp.bfloat16
F32 = jnp.float32
FAR = pl.BlockSpec(memory_space=pl.ANY)
NEAR = pl.BlockSpec(memory_space=pltpu.VMEM)
SCALARS = pl.BlockSpec(memory_space=pltpu.SMEM)


def mm(left, right):
    return lax.dot_general(left, right, (((1,), (0,)), ((), ())), preferred_element_type=F32)


def mm_nt(left, right):
    return lax.dot_general(left, right, (((1,), (1,)), ((), ())), preferred_element_type=F32)


def mm_tn(left, right):
    return lax.dot_general(left, right, (((0,), (0,)), ((), ())), preferred_element_type=F32)


def split(values):
    high = values.astype(BF)
    return high, (values - high.astype(F32)).astype(BF)


def iota(shape, axis):
    return lax.broadcasted_iota(jnp.int32, shape, axis)


def cat(parts, axis=1):
    return jnp.concatenate(parts, axis=axis)


def flag(condition):
    return jnp.where(condition, 1.0, 0.0).astype(BF)


def column_sums(values):
    return jnp.sum(values, axis=0, keepdims=True)


def gelu_with_slope(values):
    cdf = 0.5 + 0.5 * lax.erf(values * 0.7071067811865476)
    bell = jnp.exp2(values * values * (-0.5 * LOG2E)) * 0.3989422804014327
    return values * cdf, cdf + values * bell


def cell_of_places(index_line, axis):
    row_part = (index_line * 22311) >> 20
    col_part = index_line - row_part * TABLE_SIDE
    if axis == 1:
        rows = jnp.max(row_part, axis=1, keepdims=True) - row_part
        cols = jnp.max(col_part, axis=1, keepdims=True) - col_part
    else:
        rows = row_part - jnp.min(row_part, axis=0, keepdims=True)
        cols = col_part - jnp.min(col_part, axis=0, keepdims=True)
    return rows * SIDE + cols


def head_sum_matrix():
    row = iota((2 * LANES, LANES), 0)
    col = iota((2 * LANES, LANES), 1)
    return flag(((row >> 5) & 3) == (col >> 5))


def head_sums(values, matrix):
    return mm(cat(split(values)), matrix)


def whole(shape):
    return pl.BlockSpec(shape, lambda *_: (0,) * len(shape))


def params(mib=58, **more):
    return pltpu.CompilerParams(vmem_limit_bytes=mib * MIB, **more)


def cost(flops, moved):
    return pl.CostEstimate(flops=flops, bytes_accessed=moved, transcendentals=0)


def coord_rows():
    def u(offset):
        c = np.float32(offset) * np.float32(8.0 / 15.0)
        return np.sign(c) * np.log2(np.abs(c) + np.float32(1.0)) / np.float32(3.0)

    lane = np.arange(WIDE)
    out = []
    for parity in range(2):
        e = 2 * (lane // PITCH) + parity
        k = lane % PITCH
        out.append(np.stack([u(SIDE - 1 - e), u(SIDE - 1 - k)] + [np.ones(WIDE)] + [np.zeros(WIDE)] * 5))
    return np.stack(out).astype(np.float32)


def net_columns(w1_ref, b1_ref):
    units = w1_ref.shape[1]
    return jnp.transpose(cat([w1_ref[...], b1_ref[...], jnp.zeros((5, units), F32)], 0))


def table_pre(coord_ref, cols, parity):
    pre = cols[:, 0:1] * coord_ref[parity, 0:1, :] + cols[:, 1:2] * coord_ref[parity, 1:2, :]
    return pre + cols[:, 2:3]


def table_of(hidden, w2s):
    parts = split(hidden)
    z = cat([mm(w2, parts[0]) + mm(w2, parts[1]) for w2 in w2s], 0)
    return 16.0 / (1.0 + jnp.exp(-z))


def stat_lane(kind, group, head):
    return kind * 16 + group * PER_GROUP + head


def head_masks():
    lane = iota((1, LANES), 1) >> 5
    return [flag(lane == h) for h in range(PER_GROUP)]


def forward_kernel(
    images, halves, row_ref, col_ref, p_a_ref, p_b_ref, coord_ref, w1_ref, b1_ref, w2_a_ref, w2_b_ref,
    x_hbm, w_a_hbm, w_b_hbm,
    stat_ref, scale_ref, e_hbm, ctx_hbm, rest_hbm, ql_hbm, kl_hbm, vl_hbm, cell_hbm, gather_hbm, scatter_hbm,
    x_ref, w_a_ref, w_b_ref, e_ref, ctx_ref, rest_ref, ql_ref, kl_ref, vl_ref, cell_ref, gather_ref, scatter_ref,
    table_ref, pos_ref, logit_ref, mix_ref, in_sem, sem, out_sem,
):
    loads = [
        pltpu.make_async_copy(source, target, in_sem.at[i])
        for i, (source, target) in enumerate(((x_hbm, x_ref), (w_a_hbm, w_a_ref), (w_b_hbm, w_b_ref)))
    ]
    for load in loads:
        load.start()
    stores = []

    def store(source, target):
        copy = pltpu.make_async_copy(source, target, out_sem.at[len(stores)])
        copy.start()
        stores.append(copy)

    scatter_ref[...] = flag(iota((WIN, WIN), 1) == cell_of_places(col_ref[:, 0:1], 0))
    store(scatter_ref, scatter_hbm)
    gather = flag(iota((WIN, WIN), 0) == cell_of_places(row_ref[0:1, :], 1))
    gather_ref[...] = gather
    store(gather_ref, gather_hbm)
    stat_ref[...] = jnp.zeros_like(stat_ref)
    for which, ref in enumerate((p_a_ref, p_b_ref)):
        scale_ref[which : which + 1, :] = ref[2:3, :]
    columns = net_columns(w1_ref, b1_ref)
    for parity in range(2):
        hidden, _ = gelu_with_slope(table_pre(coord_ref, columns, parity))
        table_ref[parity] = table_of(hidden, (w2_a_ref[...], w2_b_ref[...])) * LOG2E
    loads[0].wait()
    for m in range(images):
        rows = slice(m * WIN, (m + 1) * WIN)
        cell_ref[rows, :] = mm(gather, x_ref[rows, :]).astype(BF)
    store(cell_ref, cell_hbm)

    masks = head_masks()
    lane = iota((1, LANES), 1)
    row = iota((2 * LANES, LANES), 0) & (LANES - 1)
    col = iota((2 * LANES, LANES), 1)
    same = flag((row >> 5) == (col >> 5))
    lower = iota((1, WIDE), 1) % PITCH < SIDE
    left_half = iota((1, WIDE), 1) < WIN
    ones = jnp.ones((WIN, LANES), BF)

    def prepare(g):
        here = slice(g * LANES, (g + 1) * LANES)
        inner = slice(g % halves * LANES, (g % halves + 1) * LANES)
        which = g // halves
        w_ref, p_ref = ((w_a_ref, p_a_ref), (w_b_ref, p_b_ref))[which]
        if g % halves == 0:
            loads[1 + which].wait()
        w = cat([w_ref[i, :, inner] for i in range(3)])
        sums = [cat([same, flag(stat_lane(i, g, row >> 5) == col)]) for i in range(2)]
        stat_here = [(lane >> 2) == i * 4 + g for i in range(2)]
        out = []
        for m in range(images):
            rows = slice(m * WIN, (m + 1) * WIN)
            qkv = mm(cell_ref[rows, :], w)
            q = qkv[:, :LANES] + p_ref[0:1, inner]
            k = qkv[:, LANES : 2 * LANES]
            vl = (qkv[:, 2 * LANES :] + p_ref[1:2, inner]).astype(BF)
            rq = lax.rsqrt(head_sums(q * q, sums[0]) + 1.0)
            rk = lax.rsqrt(head_sums(k * k, sums[1]) + 1.0)
            ql = (q * rq[:, :LANES]).astype(BF)
            kl = (k * rk[:, :LANES]).astype(BF)
            stat = jnp.where(stat_here[0], rq[:, LANES:], stat_ref[rows, :])
            stat_ref[rows, :] = jnp.where(stat_here[1], rk[:, LANES:], stat)
            ql_ref[rows, here] = ql
            kl_ref[rows, here] = kl
            vl_ref[rows, here] = vl
            out.append((cat(split(ql.astype(F32) * (p_ref[2:3, inner] * LOG2E))), kl, vl))
        for source, target in ((ql_ref, ql_hbm), (kl_ref, kl_hbm), (vl_ref, vl_hbm)):
            store(source.at[:, pl.ds(g * LANES, LANES)], target.at[:, pl.ds(g * LANES, LANES)])
        return out

    def bands_of(head):
        even = jnp.broadcast_to(table_ref[0, head : head + 1, :], (SIDE, WIDE))
        even = pltpu.roll(even, WIDE - SIDE + 1, 1, stride=1, stride_axis=0)
        odd = jnp.broadcast_to(table_ref[1, head : head + 1, :], (SIDE, WIDE))
        odd = pltpu.roll(odd, 1, 1, stride=1, stride_axis=0)
        return jnp.where(lower, even, odd)

    def place_bias(g, pair):
        slot = pair % 2
        one, two = (bands_of(g * PER_GROUP + 2 * pair + i) for i in range(2))
        for r in range(SIDE):
            offset = (SIDE - 1 - r) * SIDE
            pos_ref[slot, r * SIDE : (r + 1) * SIDE, :] = jnp.where(
                left_half, pltpu.roll(one, (WIDE - offset) % WIDE, 1), pltpu.roll(two, (WIDE + WIN - offset) % WIDE, 1)
            )

    pairs = PER_GROUP // 2
    units = [(g, pair, m) for g in range(2 * halves) for pair in range(pairs) for m in range(images)]
    ready = {}

    def score(at):
        g, pair, m = units[at]
        if (g, 0) not in ready:
            for i, operands in enumerate(prepare(g)):
                ready[g, i] = operands
        if m == 0:
            place_bias(g, pair)
        left, kl, _ = ready[g, m]
        keys = cat([kl * mask for mask in masks[2 * pair : 2 * pair + 2]], 0)
        logit_ref[at % 2] = mm_nt(left, cat([keys, keys]))

    def weigh(at):
        g, pair, m = units[at]
        e_ref[g, pair, m] = jnp.exp2(logit_ref[at % 2] + pos_ref[pair % 2]).astype(BF)
        pltpu.make_async_copy(e_ref.at[g, pair, m], e_hbm.at[g, pair, m], sem.at[g, pair, m]).start()

    def mix(at):
        g, pair, m = units[at]
        vl = ready[g, m][2]
        here = masks[2 * pair : 2 * pair + 2]
        values = cat([cat([vl * mask for mask in here], 0), cat([ones * mask for mask in here], 0)])
        mixed = mm(e_ref[g, pair, m], values)
        if pair == 0:
            mix_ref[m] = mixed
        elif pair < pairs - 1:
            mix_ref[m] += mixed
        else:
            mixed = mix_ref[m] + mixed
            rows = slice(m * WIN, (m + 1) * WIN)
            lanes = slice(g * LANES, (g + 1) * LANES)
            inverse = 1.0 / mixed[:, LANES:]
            high, low = split(mixed[:, :LANES] * inverse)
            ctx_ref[rows, lanes] = high
            rest_ref[rows, lanes] = low
            pick = flag(((row & (HEAD - 1)) == 0) & (stat_lane(2, g, row >> 5) == col))
            stat_ref[rows, :] += head_sums(inverse, pick)
            if m == images - 1:
                for source, target in ((ctx_ref, ctx_hbm), (rest_ref, rest_hbm)):
                    store(source.at[:, pl.ds(g * LANES, LANES)], target.at[:, pl.ds(g * LANES, LANES)])

    score(0)
    for at in range(len(units)):
        if at + 1 < len(units):
            score(at + 1)
        weigh(at)
        if at > 0:
            mix(at - 1)
    mix(len(units) - 1)
    for g, pair, m in units:
        pltpu.make_async_copy(e_ref.at[g, pair, m], e_hbm.at[g, pair, m], sem.at[g, pair, m]).wait()
    for copy in stores:
        copy.wait()


def attention_forward(index, x, ws, ps, coords, net_first, net_seconds):
    count, depth = x.shape
    images = count // WIN
    halves = ws[0].shape[2] // LANES
    groups = 2 * halves
    heads = groups * PER_GROUP
    wide = groups * LANES
    pairs = PER_GROUP // 2
    weights = (groups, pairs, images, WIN, 2 * WIN)
    near = [*ps, coords, *net_first, *net_seconds]
    far_out = [weights] + [(count, wide)] * 5 + [(count, depth), (WIN, WIN), (WIN, WIN)]
    near_out = [jax.ShapeDtypeStruct((count, LANES), F32), jax.ShapeDtypeStruct((2, wide // 2), F32)]
    return pl.pallas_call(
        functools.partial(forward_kernel, images, halves),
        grid=(1,),
        in_specs=[pl.BlockSpec((8, WIN), lambda i: (0, 0)), pl.BlockSpec((WIN, LANES), lambda i: (0, 0))]
        + [whole(a.shape) for a in near] + [FAR] * 3,
        out_specs=[whole(a.shape) for a in near_out] + [FAR] * len(far_out),
        out_shape=near_out + [jax.ShapeDtypeStruct(shape, BF) for shape in far_out],
        scratch_shapes=[pltpu.VMEM(x.shape, BF)] + [pltpu.VMEM(w.shape, BF) for w in ws]
        + [pltpu.VMEM(shape, BF) for shape in far_out]
        + [
            pltpu.VMEM((2, heads, WIDE), F32),
            pltpu.VMEM((2, WIN, 2 * WIN), F32),
            pltpu.VMEM((2, WIN, 2 * WIN), F32),
            pltpu.VMEM((images, WIN, 2 * LANES), F32),
            pltpu.SemaphoreType.DMA((3,)),
            pltpu.SemaphoreType.DMA((groups, pairs, images)),
            pltpu.SemaphoreType.DMA((5 * groups + 3,)),
        ],
        compiler_params=params(mib=54, dimension_semantics=("arbitrary",)),
        cost_estimate=cost(8_000_000_000, 40_000_000),
        name="attention_forward",
    )(index, index, *near, x, *ws)


def norm_stats(values):
    center = values - jnp.mean(values, axis=1, keepdims=True)
    inverse = lax.rsqrt(jnp.mean(center * center, axis=1, keepdims=True) + 1e-05)
    return center * inverse, inverse


def norm_back(grad, unit, inverse, gain):
    scaled = grad * gain
    mean = jnp.mean(scaled, axis=1, keepdims=True)
    along = jnp.mean(scaled * unit, axis=1, keepdims=True)
    return inverse * (scaled - mean - unit * along)


def feed_kernel(
    images, scatter_ref, x_ref, mix_ref, p_a_ref, p_b_ref,
    bo_ref, g1_ref, s1_ref, b2_ref, g2_ref, s2_ref, w1_a_hbm, w1_b_hbm, w2_a_hbm, w2_b_hbm, og_hbm,
    wo_a_hbm, wo_b_hbm,
    out_hbm, dmid_hbm, da_hbm, own_hbm, other_hbm, small_ref, gb1_ref,
    w1_ref, w2_ref, og_ref, wo_ref, out_ref, da_ref, dm_ref, pack_ref, mid_ref,
    ctx_ref, low_ref, pre_ref, hid_ref, slope_ref, grad_ref, acc_ref, unit_ref, in_sem, out_sem,
):
    half = w1_ref.shape[2]
    depth = x_ref.shape[1]
    narrow = wo_ref.shape[1]
    tiles = 2 * half // TILE
    ps = (p_a_ref, p_b_ref)
    packed = (own_hbm, other_hbm)
    loads = [
        pltpu.make_async_copy(source, target, in_sem.at[i])
        for i, (source, target) in enumerate(
            (
                (w1_a_hbm, w1_ref.at[0]), (w1_b_hbm, w1_ref.at[1]), (w2_a_hbm, w2_ref.at[0]),
                (w2_b_hbm, w2_ref.at[1]), (og_hbm, og_ref), (wo_a_hbm, wo_ref.at[0]), (wo_b_hbm, wo_ref.at[1]),
            )
        )
    ]
    for load in loads[5:] + loads[:5]:
        load.start()
    stores = []

    def store(source, target):
        copy = pltpu.make_async_copy(source, target, out_sem.at[len(stores)])
        copy.start()
        stores.append(copy)

    def place_of(tile):
        at = tile * TILE
        return at // half, slice(at % half, at % half + TILE)

    inverse_ones = []
    for m in range(images):
        rows = slice(m * WIN, (m + 1) * WIN)
        ctx = mm(scatter_ref[...], mix_ref[rows, :]).astype(BF)
        ctx_ref[rows, :] = ctx
        if m == 0:
            loads[5].wait()
            loads[6].wait()
        attn = mm(ctx[:, :narrow], wo_ref[0]) + mm(ctx[:, narrow:], wo_ref[1]) + bo_ref[...]
        unit_one, inverse = norm_stats(attn)
        inverse_ones.append(inverse)
        unit_ref[rows, :] = unit_one
        middle = x_ref[rows, :].astype(F32) + unit_one * g1_ref[...] + s1_ref[...]
        mid_ref[rows, :] = middle
        low_ref[rows, :] = middle.astype(BF)

    def up(tile):
        which, cols = place_of(tile)
        if cols.start == 0:
            loads[which].wait()
        row = 3 + cols.start // TILE
        pre_ref[tile % 2] = mm(low_ref[...], w1_ref[which, :, cols]) + ps[which][row : row + 1, :]

    def down(tile):
        which, cols = place_of(tile)
        if cols.start == 0:
            loads[2 + which].wait()
        term = mm(hid_ref[which, :, cols], w2_ref[which, cols, :])
        if tile == 0:
            acc_ref[...] = term
        else:
            acc_ref[...] += term

    up(0)
    for tile in range(tiles):
        if tile + 1 < tiles:
            up(tile + 1)
        which, cols = place_of(tile)
        hidden, slope = gelu_with_slope(pre_ref[tile % 2])
        hid_ref[which, :, cols] = hidden.astype(BF)
        slope_ref[which, :, cols] = slope
        if tile > 0:
            down(tile - 1)
    down(tiles - 1)

    loads[4].wait()
    sums = [jnp.zeros((1, depth), F32)] * 3
    for m in range(images):
        rows = slice(m * WIN, (m + 1) * WIN)
        unit_two, inverse_two = norm_stats(acc_ref[rows, :] + b2_ref[...])
        out_ref[rows, :] = (mid_ref[rows, :] + (unit_two * g2_ref[...] + s2_ref[...])).astype(BF)
        grad = og_ref[rows, :].astype(F32)
        d_mlp = norm_back(grad, unit_two, inverse_two, g2_ref[...])
        terms = (column_sums(d_mlp), column_sums(grad * unit_two), column_sums(grad))
        sums = [a + b for a, b in zip(sums, terms)]
        dm_ref[rows, :] = d_mlp.astype(BF)
        acc_ref[rows, :] = grad
    store(out_ref, out_hbm)
    for i in range(3):
        small_ref[3 + i : 4 + i, :] = sums[i]

    for tile in range(tiles):
        which, cols = place_of(tile)
        d_pre = mm_nt(dm_ref[...], w2_ref[which, cols, :]) * slope_ref[which, :, cols]
        gb1_ref[which : which + 1, cols] = column_sums(d_pre)
        d_pre_low = d_pre.astype(BF)
        grad_ref[which, :, cols] = d_pre_low
        acc_ref[...] += mm_nt(d_pre_low, w1_ref[which, :, cols])
    store(acc_ref, dmid_hbm)

    def weight_grads(tile):
        which, cols = place_of(tile)
        at = cols.start
        pack_ref[which, half + at : half + at + TILE, :] = mm_tn(hid_ref[which, :, cols], dm_ref[...]).astype(BF)
        rows = slice(at // depth * depth, (at // depth + 1) * depth)
        grads = mm_tn(low_ref[...], grad_ref[which, :, cols]).astype(BF)
        pack_ref[which, rows, at % depth : at % depth + TILE] = grads
        if at + TILE == half:
            span = pl.ds(0, 2 * half)
            store(pack_ref.at[which, span], packed[which].at[span])

    sums = [jnp.zeros((1, depth), F32)] * 3
    for tile in range(tiles):
        weight_grads(tile)
        if tile < images:
            rows = slice(tile * WIN, (tile + 1) * WIN)
            d_middle = acc_ref[rows, :]
            unit_one = unit_ref[rows, :]
            d_attn = norm_back(d_middle, unit_one, inverse_ones[tile], g1_ref[...])
            terms = (column_sums(d_attn), column_sums(d_middle * unit_one), column_sums(d_middle))
            sums = [a + b for a, b in zip(sums, terms)]
            da_ref[rows, :] = d_attn.astype(BF)
        if tile == images - 1:
            store(da_ref, da_hbm)
    for i in range(3):
        small_ref[i : i + 1, :] = sums[i]
    span = pl.ds(2 * half, narrow)
    for which in range(2):
        pack_ref[which, 2 * half : 2 * half + narrow, :] = mm_tn(
            ctx_ref[:, which * narrow : (which + 1) * narrow], da_ref[...]
        ).astype(BF)
        store(pack_ref.at[which, span], packed[which].at[span])
    for copy in stores:
        copy.wait()


def feed_forward(scatter, x, ctx, wos, w1s, w2s, ps, vectors, cotangent):
    count, depth = x.shape
    images = count // WIN
    narrow = wos[0].shape[0]
    half = w1s[0].shape[1]
    packed = 2 * half + narrow
    low = pltpu.VMEM((count, depth), BF)
    full = pltpu.VMEM((count, depth), F32)
    return pl.pallas_call(
        functools.partial(feed_kernel, images),
        in_specs=[NEAR] * 11 + [FAR] * 7,
        out_specs=[FAR] * 5 + [NEAR] * 2,
        out_shape=[
            jax.ShapeDtypeStruct((count, depth), BF),
            jax.ShapeDtypeStruct((count, depth), F32),
            jax.ShapeDtypeStruct((count, depth), BF),
            jax.ShapeDtypeStruct((packed, depth), BF),
            jax.ShapeDtypeStruct((packed, depth), BF),
            jax.ShapeDtypeStruct((8, depth), F32),
            jax.ShapeDtypeStruct((2, half), F32),
        ],
        scratch_shapes=[
            pltpu.VMEM((2, depth, half), BF),
            pltpu.VMEM((2, half, depth), BF),
            low,
            pltpu.VMEM((2, narrow, depth), BF),
            low, low, low,
            pltpu.VMEM((2, packed, depth), BF),
            full,
            pltpu.VMEM((count, 2 * narrow), BF),
            low,
            pltpu.VMEM((2, count, TILE), F32),
            pltpu.VMEM((2, count, half), BF),
            pltpu.VMEM((2, count, half), F32),
            pltpu.VMEM((2, count, half), BF),
            full, full,
            pltpu.SemaphoreType.DMA((7,)),
            pltpu.SemaphoreType.DMA((7,)),
        ],
        compiler_params=params(mib=56),
        cost_estimate=cost(2 * count * depth * (2 * depth + 12 * half), 30_000_000),
        name="feed_forward",
    )(scatter, x, ctx, *ps, *vectors, *w1s, *w2s, cotangent, *wos)


def context_grad_kernel(images, gather_ref, da_ref, wo_a_ref, wo_b_ref, out_ref):
    for m in range(images):
        rows = slice(m * WIN, (m + 1) * WIN)
        grad = cat([mm_nt(da_ref[rows, :], wo_a_ref[...]), mm_nt(da_ref[rows, :], wo_b_ref[...])]).astype(BF)
        out_ref[rows, :] = mm(gather_ref[...], grad).astype(BF)


def context_grad(gather, d_attn, wos):
    return pl.pallas_call(
        functools.partial(context_grad_kernel, d_attn.shape[0] // WIN),
        out_shape=jax.ShapeDtypeStruct((d_attn.shape[0], 2 * wos[0].shape[0]), BF),
        compiler_params=params(),
        cost_estimate=cost(2_000_000_000, 5_000_000),
        name="context_grad",
    )(gather, d_attn, *wos)


def backward_kernel(
    images, first, span, x_ref, scale_ref, dctx_ref, ctx_ref, rest_ref, ql_ref, kl_ref, vl_ref, stat_ref, e_hbm,
    gw_ref, dqkv_ref, dm_ref, small_ref,
    e_ref, prob_ref, low_ref, sum_ref, duq_ref, dkt_ref, dvt_ref, sem,
):
    pairs = PER_GROUP // 2
    which = first // span
    units = [(g, pair, m) for g in range(span) for pair in range(pairs) for m in range(images)]
    loads = {
        unit: pltpu.make_async_copy(e_hbm.at[first + unit[0], unit[1], unit[2]], e_ref.at[unit], sem.at[unit])
        for unit in units
    }
    for load in loads.values():
        load.start()
    masks = head_masks()
    summing = head_sum_matrix()
    unit_matrix = flag(iota((LANES, LANES), 0) == iota((LANES, LANES), 1))
    shape = (2 * LANES, 3 * LANES)
    col = iota(shape, 1)
    in_head = iota((1, LANES), 1) & (HEAD - 1)
    left_half = iota((1, WIDE), 1) < WIN
    spots = flag(in_head < 2)
    ready = {}
    sums = [[jnp.zeros((1, LANES), F32)] * 3 for _ in range(span)]

    def prepare(g, m):
        here = slice(g * LANES, (g + 1) * LANES)
        rows = slice(m * WIN, (m + 1) * WIN)
        spread = flag((iota(shape, 0) & (LANES - 1)) == stat_lane(col >> 7, first + g, (col & (LANES - 1)) >> 5))
        stats = head_sums(stat_ref[rows, :], spread)
        grad = (dctx_ref[rows, here].astype(F32) * (stats[:, 2 * LANES :] * scale_ref[which : which + 1, here])).astype(BF)
        mix = ctx_ref[rows, here].astype(F32) + rest_ref[rows, here].astype(F32)
        d_high, d_low = split(-head_sums(grad.astype(F32) * mix, summing))
        left = cat([grad, jnp.where(in_head == 0, d_high, d_low)])
        q_t = mm_nt(unit_matrix, ql_ref[rows, here]).astype(BF)
        grad_t = mm_nt(unit_matrix, grad).astype(BF)
        return left, q_t, grad_t, stats[:, : 2 * LANES]

    def score(at):
        g, pair, m = units[at]
        if (g, m) not in ready:
            ready[g, m] = prepare(g, m)
        vl = vl_ref[m * WIN : (m + 1) * WIN, g * LANES : (g + 1) * LANES]
        here = masks[2 * pair : 2 * pair + 2]
        right = cat([cat([vl * mask, jnp.broadcast_to(spots * mask, (WIN, LANES))]) for mask in here], 0)
        prob_ref[at % 2] = mm_nt(ready[g, m][0], right)

    def weigh(at):
        g, pair, m = units[at]
        loads[g, pair, m].wait()
        d_cos = e_ref[g, pair, m].astype(F32) * prob_ref[at % 2]
        low_ref[at % 2] = d_cos.astype(BF)
        if m == 0:
            sum_ref[pair % 2] = d_cos
        else:
            sum_ref[pair % 2] += d_cos
        if m == images - 1:
            one, two = None, None
            for r in range(SIDE):
                offset = (SIDE - 1 - r) * SIDE
                band = sum_ref[pair % 2, r * SIDE : (r + 1) * SIDE, :]
                left = pltpu.roll(jnp.where(left_half, band, 0.0), offset, 1)
                right = pltpu.roll(jnp.where(left_half, 0.0, band), (offset + WIN) % WIDE, 1)
                one = left if one is None else one + left
                two = right if two is None else two + right
            dm_ref[g * PER_GROUP + 2 * pair] = one
            dm_ref[g * PER_GROUP + 2 * pair + 1] = two

    def spend(at):
        g, pair, m = units[at]
        rows = slice(m * WIN, (m + 1) * WIN)
        here = slice(g * LANES, (g + 1) * LANES)
        _, q_t, grad_t, stats = ready[g, m]
        kl, ql = kl_ref[rows, here], ql_ref[rows, here]
        d_low = low_ref[at % 2]
        duq = mm(d_low, cat([kl * mask for mask in masks[2 * pair : 2 * pair + 2]], 0))
        head = pair * 2 * HEAD
        for ref, source, factor in ((dkt_ref, q_t, d_low), (dvt_ref, grad_t, e_ref[g, pair, m])):
            both = mm(source[head : head + 2 * HEAD], factor)
            ref[m, head : head + HEAD, :] = both[:HEAD, : ref.shape[2]]
            ref[m, head + HEAD : head + 2 * HEAD, :] = pltpu.roll(both[HEAD:], WIN, 1)[:, : ref.shape[2]]
        if pair == 0:
            duq_ref[m] = duq
        if 0 < pair < pairs - 1:
            duq_ref[m] += duq
        if pair == pairs - 1:
            duq = duq_ref[m] + duq
            uq = ql.astype(F32)
            along_q = head_sums(uq * duq, summing)
            dq = stats[:, :LANES] * (duq - uq * along_q)
            uk = kl.astype(F32)
            duk = jnp.transpose(dkt_ref[m])[:WIN]
            dk = stats[:, LANES:] * (duk - uk * head_sums(uk * duk, summing))
            dv = jnp.transpose(dvt_ref[m])[:WIN] / scale_ref[which : which + 1, here]
            sums[g] = [a + column_sums(t) for a, t in zip(sums[g], (dq, dv, along_q))]
            for i, grads in enumerate((dq, dk, dv)):
                lanes = (i * span + g) * LANES
                dqkv_ref[rows, lanes : lanes + LANES] = grads.astype(BF)

    score(0)
    for at in range(len(units)):
        if at + 1 < len(units):
            score(at + 1)
        weigh(at)
        if at > 0:
            spend(at - 1)
    spend(len(units) - 1)
    for g in range(span):
        for i in range(3):
            small_ref[g, i : i + 1, :] = sums[g][i]
    for i in range(3):
        gw = mm_tn(x_ref[...], dqkv_ref[:, i * span * LANES : (i + 1) * span * LANES]).astype(BF)
        for g in range(span):
            gw_ref[g, i] = gw[:, g * LANES : (g + 1) * LANES]


def attention_backward(first, span, x, scales, dctx, saved):
    e, *blocks, stat = saved
    count, depth = x.shape
    images = count // WIN
    padded = -(-WIN // LANES) * LANES
    block = pl.BlockSpec((count, span * LANES), lambda i: (0, first // span))
    shapes = [
        jax.ShapeDtypeStruct((span, 3, depth, LANES), BF),
        jax.ShapeDtypeStruct((count, span * 3 * LANES), BF),
        jax.ShapeDtypeStruct((span * PER_GROUP, SIDE, WIDE), F32),
        jax.ShapeDtypeStruct((span, 8, LANES), F32),
    ]
    return pl.pallas_call(
        functools.partial(backward_kernel, images, first, span),
        grid=(1,),
        in_specs=[whole(x.shape), whole(scales.shape)] + [block] * 6
        + [whole(stat.shape), FAR],
        out_specs=[whole(a.shape) for a in shapes],
        out_shape=shapes,
        scratch_shapes=[
            pltpu.VMEM((span,) + e.shape[1:], BF),
            pltpu.VMEM((2, WIN, 2 * WIN), F32),
            pltpu.VMEM((2, WIN, 2 * WIN), BF),
            pltpu.VMEM((2, WIN, 2 * WIN), F32),
            pltpu.VMEM((images, WIN, LANES), F32),
            pltpu.VMEM((images, LANES, padded), F32),
            pltpu.VMEM((images, LANES, padded), F32),
            pltpu.SemaphoreType.DMA((span,) + e.shape[1:3]),
        ],
        compiler_params=params(mib=46, dimension_semantics=("arbitrary",)),
        cost_estimate=cost(8_000_000_000 * span, 20_000_000 * span),
        name=f"attention_backward_{first}",
    )(x, scales, dctx, *blocks, stat, e)


def input_grad_kernel(scatter_ref, dmid_ref, da_ref, db_ref, w_a_ref, w_b_ref, out_ref):
    wide = w_a_ref.shape[2]
    total = None
    for grad_ref, w_ref in ((da_ref, w_a_ref), (db_ref, w_b_ref)):
        for i in range(3):
            term = mm_nt(grad_ref[:, i * wide : (i + 1) * wide], w_ref[i])
            total = term if total is None else total + term
    high, low = split(total)
    out_ref[...] = dmid_ref[...] + mm(scatter_ref[...], high) + mm(scatter_ref[...], low)


def input_grad(scatter, d_middle, grads, ws):
    count, depth = d_middle.shape
    rows = lambda width: pl.BlockSpec((WIN, width), lambda i: (i, 0))
    return pl.pallas_call(
        input_grad_kernel,
        grid=(count // WIN,),
        in_specs=[whole(scatter.shape), rows(depth)] + [rows(g.shape[1]) for g in grads] + [whole(w.shape) for w in ws],
        out_specs=rows(depth),
        out_shape=jax.ShapeDtypeStruct(d_middle.shape, F32),
        compiler_params=params(mib=14, dimension_semantics=("arbitrary",)),
        cost_estimate=cost(3_000_000_000, 12_000_000),
        name="input_grad",
    )(scatter, d_middle, *grads, *ws)


def table_back_kernel(spans, coord_ref, w1_ref, b1_ref, w2_a_ref, w2_b_ref, scale_ref, vec_ref, gb1_ref, *refs):
    calls = len(spans)
    dms, smalls, (own_ref, other_ref) = refs[:calls], refs[calls : 2 * calls], refs[2 * calls :]
    lower = iota((1, WIDE), 1) % PITCH < SIDE
    even, odd = [], []
    for ref in dms:
        e = jnp.zeros((ref.shape[0], WIDE), F32)
        o = jnp.zeros((ref.shape[0], WIDE), F32)
        for c in range(SIDE):
            slab = ref[:, c, :]
            e = e + pltpu.roll(jnp.where(lower, slab, 0.0), (SIDE - 1 - c) % WIDE, 1)
            o = o + pltpu.roll(jnp.where(lower, 0.0, slab), (-1 - c) % WIDE, 1)
        even.append(e)
        odd.append(o)
    w2s = (w2_a_ref[...], w2_b_ref[...])
    columns = net_columns(w1_ref, b1_ref)
    shape = (w2s[0].shape[0], scale_ref.shape[1])
    diagonal = iota(shape, 0) * HEAD == iota(shape, 1)
    inverses = [
        1.0 / jnp.sum(jnp.where(diagonal, scale_ref[i : i + 1, :], 0.0), axis=1, keepdims=True) for i in range(2)
    ]
    inverse = cat(inverses, 0)
    dw2 = None
    dcols = None
    for parity, grads in enumerate((even, odd)):
        hidden, slope = gelu_with_slope(table_pre(coord_ref, columns, parity))
        table = table_of(hidden, w2s)
        dz = cat(grads, 0) * inverse * table * (1.0 - table * 0.0625)
        hidden_high, hidden_low = split(hidden)
        dz_high, dz_low = split(dz)
        term = mm_nt(dz_high, hidden_high) + mm_nt(dz_high, hidden_low) + mm_nt(dz_low, hidden_high)
        dw2 = term if dw2 is None else dw2 + term
        w2 = cat(w2s, 0)
        high, low = split((mm_tn(w2, dz_high) + mm_tn(w2, dz_low)) * slope)
        c_high, c_low = split(coord_ref[parity])
        term = mm_nt(c_high, high) + mm_nt(c_high, low) + mm_nt(c_low, high)
        dcols = term if dcols is None else dcols + term
    heads = w2s[0].shape[0]
    groups = [(ref, g) for ref, span in zip(smalls, spans) for g in range(span)]
    for which, out in enumerate((own_ref, other_ref)):
        lines = [(vec_ref, i) for i in range(6)] + [(dcols, i) for i in range(3)] + [(gb1_ref, which)]
        row = 0
        for source, i in lines + [(dw2, which * heads + h) for h in range(heads)]:
            for at in range(0, source.shape[1], LANES):
                out[row : row + 1, :] = source[i : i + 1, at : at + LANES]
                row += 1
        for ref, g in groups[which * len(groups) // 2 : (which + 1) * len(groups) // 2]:
            for i in range(3):
                out[row : row + 1, :] = ref[g, i : i + 1, :]
                row += 1
        out[row:, :] = jnp.zeros((SMALL_ROWS - row, LANES), F32)


def table_back(coords, net_first, w2s, scales, vectors, gb1, dms, smalls):
    small = jax.ShapeDtypeStruct((SMALL_ROWS, LANES), F32)
    return pl.pallas_call(
        functools.partial(table_back_kernel, [s.shape[0] for s in smalls]),
        out_shape=(small, small),
        compiler_params=params(mib=22),
        cost_estimate=cost(1_000_000_000, 10_000_000),
        name="table_back",
    )(coords, *net_first, *w2s, scales, vectors, gb1, *dms, *smalls)


def swap(array):
    return lax.ppermute(array, "mp", [(0, 1), (1, 0)])


def tie(*trees):
    leaves, kind = jax.tree.flatten(trees)
    return jax.tree.unflatten(kind, lax.optimization_barrier(leaves))


def send(array, plan, phase, step):
    pairs = []
    for mp, strides in enumerate(plan):
        stride = strides[phase]
        for dp in range(16):
            digit = dp // stride % 4
            pairs.append((2 * dp + mp, 2 * (dp + ((digit + step) % 4 - digit) * stride) + mp))
    return lax.ppermute(array, ("dp", "mp"), pairs)


def rotate_kernel(count, digit_ref, *refs):
    sources, targets = refs[:count], refs[count : count + 4]
    in_ref, out_ref, in_sem, out_sem = refs[count + 4 :]
    rows = out_ref.shape[1]
    order = (1, 2, 3, 0)
    loads, stores = {}, []
    for t in order:
        at = pl.multiple_of(((digit_ref[0] + t) & 3) * rows, 16)
        for i, source in enumerate(sources):
            loads[t, i] = pltpu.make_async_copy(source.at[pl.ds(at, rows)], in_ref.at[i, t], in_sem.at[i, t])
            loads[t, i].start()
    for t in order:
        total = None
        for i in range(count):
            loads[t, i].wait()
            term = in_ref[i, t].astype(F32)
            total = term if total is None else total + term
        out_ref[t] = total.astype(BF)
        stores.append(pltpu.make_async_copy(out_ref.at[t], targets[t], out_sem.at[t]))
        stores[-1].start()
    for store in stores:
        store.wait()


def rotate_sum(arrays, digit):
    rows, lanes = arrays[0].shape
    rows //= 4
    count = len(arrays)
    return pl.pallas_call(
        functools.partial(rotate_kernel, count),
        in_specs=[SCALARS] + [FAR] * count,
        out_specs=[FAR] * 4,
        out_shape=[jax.ShapeDtypeStruct((rows, lanes), BF)] * 4,
        scratch_shapes=[
            pltpu.VMEM((count, 4, rows, lanes), BF),
            pltpu.VMEM((4, rows, lanes), BF),
            pltpu.SemaphoreType.DMA((count, 4)),
            pltpu.SemaphoreType.DMA((4,)),
        ],
        compiler_params=params(mib=12),
        cost_estimate=cost(1_000_000, 6 * rows * lanes * count),
        name="rotate_sum",
    )(digit, *arrays)


def add_all(blocks):
    total = blocks[0].astype(F32)
    for block in blocks[1:]:
        total = total + block.astype(F32)
    return total


def fetch(sources, buffer_ref, sem):
    loads = [pltpu.make_async_copy(ref, buffer_ref.at[i], sem.at[i]) for i, ref in enumerate(sources)]
    for load in loads:
        load.start()
    return loads


def lay_feed_kernel(digit_ref, a, b, c, d, up_ref, down_ref, proj_ref, in_ref, held_ref, in_sem, out_sem):
    rows = in_ref.shape[1]
    for s, load in enumerate(fetch((a, b, c, d), in_ref, in_sem)):
        at = ((digit_ref[0] - s) & 3) * rows
        load.wait()
        held_ref[pl.ds(pl.multiple_of(at, 16), rows), :] = in_ref[s].astype(F32)
    depth, half = up_ref.shape
    parts = [
        (held_ref.at[pl.ds(at, depth)], up_ref.at[:, pl.ds(at, depth)]) for at in range(0, half, depth)
    ]
    parts.append((held_ref.at[pl.ds(half, half)], down_ref))
    parts.append((held_ref.at[pl.ds(2 * half, proj_ref.shape[0])], proj_ref))
    stores = [pltpu.make_async_copy(x, y, out_sem.at[i]) for i, (x, y) in enumerate(parts)]
    for store in stores:
        store.start()
    for store in stores:
        store.wait()


def lay_feed(outer, blocks, depth, half, narrow):
    rows = 2 * half + narrow
    return pl.pallas_call(
        lay_feed_kernel,
        in_specs=[SCALARS] + [FAR] * 4,
        out_specs=[FAR] * 3,
        out_shape=[
            jax.ShapeDtypeStruct((depth, half), F32),
            jax.ShapeDtypeStruct((half, depth), F32),
            jax.ShapeDtypeStruct((narrow, depth), F32),
        ],
        scratch_shapes=[
            pltpu.VMEM((4, rows // 4, depth), BF),
            pltpu.VMEM((rows, depth), F32),
            pltpu.SemaphoreType.DMA((4,)),
            pltpu.SemaphoreType.DMA((half // depth + 2,)),
        ],
        compiler_params=params(mib=12),
        cost_estimate=cost(1_000_000, 8_000_000),
        name="lay_feed",
    )(outer, *blocks)


def lay_rest_kernel(
    halves, digit_ref, a, b, c, d,
    gw_ref, shift_ref, scale_ref, w1_ref, b1_ref, w2_ref, gb1_ref, bp_ref, g1_ref, h1_ref, bd_ref, g2_ref, h2_ref,
    in_ref, held_ref, in_sem,
):
    depth = gw_ref.shape[1]
    quarter = held_ref.shape[0] // 4
    for s, load in enumerate(fetch((a, b, c, d), in_ref, in_sem)):
        at = ((digit_ref[0] - s) & 3) * quarter
        load.wait()
        held_ref[pl.ds(pl.multiple_of(at, 16), quarter), :] = in_ref[s, :quarter, :]
    small = add_all([in_ref[s, quarter:, :] for s in range(4)])
    for g in range(halves):
        for i in range(3):
            at = (g * 3 + i) * depth
            gw_ref[i, :, g * LANES : (g + 1) * LANES] = held_ref[at : at + depth, :].astype(F32)
    row = 0

    def line(length):
        nonlocal row
        count = length // LANES
        out = cat([small[row + i : row + i + 1, :] for i in range(count)])
        row += count
        return out

    for ref in (bp_ref, g1_ref, h1_ref, bd_ref, g2_ref, h2_ref):
        ref[...] = line(ref.shape[1])
    w1_ref[...] = cat([line(w1_ref.shape[1]) for _ in range(2)], 0)
    b1_ref[...] = line(b1_ref.shape[1])
    gb1_ref[...] = line(gb1_ref.shape[1])
    heads, units = w2_ref.shape
    w2_ref[...] = cat([line(units) for _ in range(heads)], 0)
    groups = [[line(LANES) for _ in range(3)] for _ in range(halves)]
    for i in range(2):
        shift_ref[i : i + 1, :] = cat([group[i] for group in groups])
    scale = cat([group[2] for group in groups])
    pick = iota((1, scale.shape[1]), 1)
    scale_ref[...] = cat(
        [jnp.sum(jnp.where(pick == h * HEAD, scale, 0.0), axis=1, keepdims=True) for h in range(heads)]
    )


def lay_rest(outer, blocks, depth, halves, half, units):
    width = halves * LANES
    heads = halves * PER_GROUP
    shapes = [(3, depth, width), (2, width), (1, heads), (2, units), (1, units), (heads, units), (1, half)]
    shapes += [(1, depth)] * 6
    return pl.pallas_call(
        functools.partial(lay_rest_kernel, halves),
        in_specs=[SCALARS] + [FAR] * 4,
        out_specs=[NEAR] * len(shapes),
        out_shape=[jax.ShapeDtypeStruct(s, F32) for s in shapes],
        scratch_shapes=[
            pltpu.VMEM((4,) + blocks[0].shape, BF),
            pltpu.VMEM((halves * 3 * depth, LANES), BF),
            pltpu.SemaphoreType.DMA((4,)),
        ],
        compiler_params=params(mib=16),
        cost_estimate=cost(1_000_000, 8_000_000),
        name="lay_rest",
    )(outer, *blocks)


def on_device(
    size, tokens, query_key_value_matrix, query_value_bias, head_logit_scale, bias_net_first_weight,
    bias_net_first_bias, bias_net_second_weight, relative_pair_index, attention_out_weight, attention_out_bias,
    attention_norm_weight, attention_norm_bias, ffn_input_weight, hidden_ffn_bias, ffn_output_weight,
    output_ffn_bias, feedforward_norm_weight, feedforward_norm_bias, output_gradient,
):
    depth = tokens.shape[1]
    width = query_key_value_matrix.shape[2]
    halves = width // LANES
    half = ffn_input_weight.shape[1]
    units = bias_net_first_bias.shape[0]

    def pair(array):
        return array, swap(array)

    ws = pair(jnp.transpose(query_key_value_matrix, (1, 0, 2)))
    ps = pair(
        jnp.concatenate(
            [
                query_value_bias.astype(F32),
                jnp.repeat(jnp.exp(head_logit_scale.astype(F32)), HEAD)[None],
                hidden_ffn_bias.astype(F32).reshape(-1, TILE),
                jnp.zeros((5 - half // TILE, width), F32),
            ]
        )
    )
    net_seconds = pair(bias_net_second_weight.T)
    wos = pair(attention_out_weight)
    w1s = pair(ffn_input_weight)
    w2s = pair(ffn_output_weight)

    coords = jnp.asarray(coord_rows())
    net_first = (bias_net_first_weight, bias_net_first_bias.reshape(1, units))
    stat, scale_lanes, *saved, cells, gather, scatter = attention_forward(
        relative_pair_index, tokens, ws, ps, coords, net_first, net_seconds
    )
    saved.append(stat)
    vectors = [
        v.reshape(1, depth)
        for v in (
            attention_out_bias, attention_norm_weight, attention_norm_bias,
            output_ffn_bias, feedforward_norm_weight, feedforward_norm_bias,
        )
    ]
    block_out, d_middle, d_attn, own, other, vector_grads, gb1 = feed_forward(
        scatter, tokens, saved[1], wos, w1s, w2s, ps, vectors, output_gradient
    )

    def backward(which, dctx):
        return attention_backward(which * halves, halves, cells, scale_lanes, dctx, saved)

    def tail_small(results):
        return table_back(
            coords, net_first, net_seconds, scale_lanes, vector_grads, gb1,
            [r[2] for r in results], [r[3] for r in results],
        )

    def lines(array):
        return array.reshape(-1, LANES)

    dctx = context_grad(gather, d_attn, wos)
    if size == 16:
        dp, mp = lax.axis_index("dp"), lax.axis_index("mp")
        plan = ((1, 4), (4, 1))
        near, far = dp & 3, dp >> 2
        outer = jnp.where(mp == 0, near, far).reshape(1)

        def spread(blocks, phase):
            return [send(b, plan, phase, t + 1) for t, b in enumerate(blocks)]

        got, dctx = tie(swap(other), dctx)
        blocks = rotate_sum([own, got], outer)
        blocks, dctx = tie(blocks, dctx)
        got = spread(blocks[1:], 0)
        theirs = backward(1, dctx)
        got, theirs, dctx = tie(got, theirs, dctx)
        low = add_all([blocks[0]] + got).astype(BF)
        low, dctx = tie(low, dctx)
        got = spread([low] * 3, 1)
        rest_got = swap(lines(theirs[0]))
        mine = backward(0, dctx)
        got, rest_got, mine = tie(got, rest_got, mine)
        low = add_all([low] + got).astype(BF)
        rest = rotate_sum([lines(mine[0]), rest_got], outer)
        rest, low = tie(rest, low)
        rest_got = spread(rest[1:], 0)
        gathered = spread([low] * 3, 0)
        results = [mine, theirs]
        small_own, small_other = tail_small(results)
        small = small_own + swap(small_other)
        rest_got, small, gathered[0] = tie(rest_got, small, gathered[0])
        message = jnp.concatenate([add_all([rest[0]] + rest_got), small]).astype(BF)
        rest_got = spread([message] * 3, 1)
        tokens_grad = input_grad(scatter, d_middle, [r[1] for r in results], ws)
        rest_got, tokens_grad = tie(rest_got, tokens_grad)
        message = add_all([message] + rest_got).astype(BF)
        rest_got = spread([message] * 3, 0)
        feed = lay_feed(outer, [low] + gathered, depth, half, width)
        rest_got, feed = tie(rest_got, feed)
        final = lay_rest(outer, [message] + rest_got, depth, halves, half, units)
    else:
        results = [backward(0, dctx), backward(1, dctx)]
        small_own, small_other = tail_small(results)
        tokens_grad = input_grad(scatter, d_middle, [r[1] for r in results], ws)
        outer = jnp.zeros((1,), jnp.int32)

        def total(array):
            return lax.psum(array, "dp").astype(BF)

        def quarters(array):
            rows = array.shape[0] // 4
            return [array[(-s % 4) * rows : (-s % 4 + 1) * rows] for s in range(4)]

        feed = lay_feed(outer, quarters(total(own.astype(F32) + swap(other).astype(F32))), depth, half, width)
        rest = total(lines(results[0][0]).astype(F32) + swap(lines(results[1][0])).astype(F32))
        small = total(small_own + swap(small_other))
        none = jnp.zeros_like(small)
        blocks = [jnp.concatenate([block, none if s else small]) for s, block in enumerate(quarters(rest))]
        final = lay_rest(outer, blocks, depth, halves, half, units)

    grad_up, grad_down, grad_proj = feed
    grad_qkv, grad_shift, grad_scale, grad_w1, grad_b1, grad_w2, grad_hidden, *vec = final
    vec = [v.reshape(-1) for v in vec]
    return (
        block_out, tokens_grad, jnp.transpose(grad_qkv, (1, 0, 2)), grad_shift, grad_scale.reshape(-1),
        grad_w1, grad_b1.reshape(-1), grad_w2.T, grad_proj, vec[0], vec[1], vec[2],
        grad_up, grad_hidden.reshape(-1), grad_down, vec[3], vec[4], vec[5],
    )


def solution(mesh):
    in_specs = (
        P(("dp", "mp"), None), P(None, None, "mp"), P(None, "mp"), P("mp"), P(), P(), P(None, "mp"), P(),
        P("mp", None), P(), P(), P(), P(None, "mp"), P("mp"), P("mp", None), P(), P(), P(), P(("dp", "mp"), None),
    )
    out_specs = (
        P(("dp", "mp"), None), P(("dp", "mp"), None), P(None, None, "mp"), P(None, "mp"), P("mp"), P(), P(),
        P(None, "mp"), P("mp", None), P(), P(), P(), P(None, "mp"), P("mp"), P("mp", None), P(), P(), P(),
    )
    return jax.shard_map(
        functools.partial(on_device, mesh.shape["dp"]),
        mesh=mesh, in_specs=in_specs, out_specs=out_specs, check_vma=False,
    )
```

```python
import functools

import jax
import jax.numpy as jnp
import numpy as np
from jax import lax
from jax.experimental import pallas as pl
from jax.experimental.pallas import tpu as pltpu
from jax.sharding import PartitionSpec as P

SIDE = 24
WIN = SIDE * SIDE
TABLE_SIDE = 2 * SIDE - 1
PITCH = 2 * SIDE
WIDE = SIDE * PITCH
HEAD = 32
LANES = 128
PER_GROUP = LANES // HEAD
TILE = 256
SMALL_ROWS = 96
LOG2E = 1.4426950408889634
MIB = 1024 * 1024
BF = jnp.bfloat16
F32 = jnp.float32
FAR = pl.BlockSpec(memory_space=pl.ANY)
NEAR = pl.BlockSpec(memory_space=pltpu.VMEM)
SCALARS = pl.BlockSpec(memory_space=pltpu.SMEM)


def mm(left, right):
    return lax.dot_general(left, right, (((1,), (0,)), ((), ())), preferred_element_type=F32)


def mm_nt(left, right):
    return lax.dot_general(left, right, (((1,), (1,)), ((), ())), preferred_element_type=F32)


def mm_tn(left, right):
    return lax.dot_general(left, right, (((0,), (0,)), ((), ())), preferred_element_type=F32)


def split(values):
    high = values.astype(BF)
    return high, (values - high.astype(F32)).astype(BF)


def iota(shape, axis):
    return lax.broadcasted_iota(jnp.int32, shape, axis)


def cat(parts, axis=1):
    return jnp.concatenate(parts, axis=axis)


def flag(condition):
    return jnp.where(condition, 1.0, 0.0).astype(BF)


def column_sums(values):
    return jnp.sum(values, axis=0, keepdims=True)


def gelu_with_slope(values):
    cdf = 0.5 + 0.5 * lax.erf(values * 0.7071067811865476)
    bell = jnp.exp2(values * values * (-0.5 * LOG2E)) * 0.3989422804014327
    return values * cdf, cdf + values * bell


def cell_of_places(index_line, axis):
    row_part = (index_line * 22311) >> 20
    col_part = index_line - row_part * TABLE_SIDE
    if axis == 1:
        rows = jnp.max(row_part, axis=1, keepdims=True) - row_part
        cols = jnp.max(col_part, axis=1, keepdims=True) - col_part
    else:
        rows = row_part - jnp.min(row_part, axis=0, keepdims=True)
        cols = col_part - jnp.min(col_part, axis=0, keepdims=True)
    return rows * SIDE + cols


def head_sum_matrix():
    row = iota((2 * LANES, LANES), 0)
    col = iota((2 * LANES, LANES), 1)
    return flag(((row >> 5) & 3) == (col >> 5))


def head_sums(values, matrix):
    return mm(cat(split(values)), matrix)


def whole(shape):
    return pl.BlockSpec(shape, lambda *_: (0,) * len(shape))


def params(mib=58, **more):
    return pltpu.CompilerParams(vmem_limit_bytes=mib * MIB, **more)


def cost(flops, moved):
    return pl.CostEstimate(flops=flops, bytes_accessed=moved, transcendentals=0)


def coord_rows():
    def u(offset):
        c = np.float32(offset) * np.float32(8.0 / 15.0)
        return np.sign(c) * np.log2(np.abs(c) + np.float32(1.0)) / np.float32(3.0)

    lane = np.arange(WIDE)
    out = []
    for parity in range(2):
        e = 2 * (lane // PITCH) + parity
        k = lane % PITCH
        out.append(np.stack([u(SIDE - 1 - e), u(SIDE - 1 - k)] + [np.ones(WIDE)] + [np.zeros(WIDE)] * 5))
    return np.stack(out).astype(np.float32)


def net_columns(w1_ref, b1_ref):
    units = w1_ref.shape[1]
    return jnp.transpose(cat([w1_ref[...], b1_ref[...], jnp.zeros((5, units), F32)], 0))


def table_pre(coord_ref, cols, parity):
    pre = cols[:, 0:1] * coord_ref[parity, 0:1, :] + cols[:, 1:2] * coord_ref[parity, 1:2, :]
    return pre + cols[:, 2:3]


def table_of(hidden, w2s):
    parts = split(hidden)
    z = cat([mm(w2, parts[0]) + mm(w2, parts[1]) for w2 in w2s], 0)
    return 16.0 / (1.0 + jnp.exp(-z))


def stat_lane(kind, group, head):
    return kind * 16 + group * PER_GROUP + head


def head_masks():
    lane = iota((1, LANES), 1) >> 5
    return [flag(lane == h) for h in range(PER_GROUP)]


def forward_kernel(
    images, halves, row_ref, col_ref, p_a_ref, p_b_ref, coord_ref, w1_ref, b1_ref, w2_a_ref, w2_b_ref,
    x_hbm, w_a_hbm, w_b_hbm,
    stat_ref, scale_ref, e_hbm, ctx_hbm, rest_hbm, ql_hbm, kl_hbm, vl_hbm, cell_hbm, gather_hbm, scatter_hbm,
    x_ref, w_a_ref, w_b_ref, e_ref, ctx_ref, rest_ref, ql_ref, kl_ref, vl_ref, cell_ref, gather_ref, scatter_ref,
    table_ref, pos_ref, logit_ref, mix_ref, in_sem, sem, out_sem,
):
    loads = [
        pltpu.make_async_copy(source, target, in_sem.at[i])
        for i, (source, target) in enumerate(((x_hbm, x_ref), (w_a_hbm, w_a_ref), (w_b_hbm, w_b_ref)))
    ]
    for load in loads:
        load.start()
    stores = []

    def store(source, target):
        copy = pltpu.make_async_copy(source, target, out_sem.at[len(stores)])
        copy.start()
        stores.append(copy)

    scatter_ref[...] = flag(iota((WIN, WIN), 1) == cell_of_places(col_ref[:, 0:1], 0))
    store(scatter_ref, scatter_hbm)
    gather = flag(iota((WIN, WIN), 0) == cell_of_places(row_ref[0:1, :], 1))
    gather_ref[...] = gather
    store(gather_ref, gather_hbm)
    stat_ref[...] = jnp.zeros_like(stat_ref)
    for which, ref in enumerate((p_a_ref, p_b_ref)):
        scale_ref[which : which + 1, :] = ref[2:3, :]
    columns = net_columns(w1_ref, b1_ref)
    for parity in range(2):
        hidden, _ = gelu_with_slope(table_pre(coord_ref, columns, parity))
        table_ref[parity] = table_of(hidden, (w2_a_ref[...], w2_b_ref[...])) * LOG2E
    loads[0].wait()
    for m in range(images):
        rows = slice(m * WIN, (m + 1) * WIN)
        cell_ref[rows, :] = mm(gather, x_ref[rows, :]).astype(BF)
    store(cell_ref, cell_hbm)

    masks = head_masks()
    lane = iota((1, LANES), 1)
    row = iota((2 * LANES, LANES), 0) & (LANES - 1)
    col = iota((2 * LANES, LANES), 1)
    same = flag((row >> 5) == (col >> 5))
    lower = iota((1, WIDE), 1) % PITCH < SIDE
    left_half = iota((1, WIDE), 1) < WIN
    ones = jnp.ones((WIN, LANES), BF)

    def prepare(g):
        here = slice(g * LANES, (g + 1) * LANES)
        inner = slice(g % halves * LANES, (g % halves + 1) * LANES)
        which = g // halves
        w_ref, p_ref = ((w_a_ref, p_a_ref), (w_b_ref, p_b_ref))[which]
        if g % halves == 0:
            loads[1 + which].wait()
        w = cat([w_ref[i, :, inner] for i in range(3)])
        sums = [cat([same, flag(stat_lane(i, g, row >> 5) == col)]) for i in range(2)]
        stat_here = [(lane >> 2) == i * 4 + g for i in range(2)]
        out = []
        for m in range(images):
            rows = slice(m * WIN, (m + 1) * WIN)
            qkv = mm(cell_ref[rows, :], w)
            q = qkv[:, :LANES] + p_ref[0:1, inner]
            k = qkv[:, LANES : 2 * LANES]
            vl = (qkv[:, 2 * LANES :] + p_ref[1:2, inner]).astype(BF)
            rq = lax.rsqrt(head_sums(q * q, sums[0]) + 1.0)
            rk = lax.rsqrt(head_sums(k * k, sums[1]) + 1.0)
            ql = (q * rq[:, :LANES]).astype(BF)
            kl = (k * rk[:, :LANES]).astype(BF)
            stat = jnp.where(stat_here[0], rq[:, LANES:], stat_ref[rows, :])
            stat_ref[rows, :] = jnp.where(stat_here[1], rk[:, LANES:], stat)
            ql_ref[rows, here] = ql
            kl_ref[rows, here] = kl
            vl_ref[rows, here] = vl
            out.append((cat(split(ql.astype(F32) * (p_ref[2:3, inner] * LOG2E))), kl, vl))
        for source, target in ((ql_ref, ql_hbm), (kl_ref, kl_hbm), (vl_ref, vl_hbm)):
            store(source.at[:, pl.ds(g * LANES, LANES)], target.at[:, pl.ds(g * LANES, LANES)])
        return out

    def bands_of(head):
        even = jnp.broadcast_to(table_ref[0, head : head + 1, :], (SIDE, WIDE))
        even = pltpu.roll(even, WIDE - SIDE + 1, 1, stride=1, stride_axis=0)
        odd = jnp.broadcast_to(table_ref[1, head : head + 1, :], (SIDE, WIDE))
        odd = pltpu.roll(odd, 1, 1, stride=1, stride_axis=0)
        return jnp.where(lower, even, odd)

    def place_bias(g, pair):
        slot = pair % 2
        one, two = (bands_of(g * PER_GROUP + 2 * pair + i) for i in range(2))
        for r in range(SIDE):
            offset = (SIDE - 1 - r) * SIDE
            pos_ref[slot, r * SIDE : (r + 1) * SIDE, :] = jnp.where(
                left_half, pltpu.roll(one, (WIDE - offset) % WIDE, 1), pltpu.roll(two, (WIDE + WIN - offset) % WIDE, 1)
            )

    pairs = PER_GROUP // 2
    units = [(g, pair, m) for g in range(2 * halves) for pair in range(pairs) for m in range(images)]
    ready = {}

    def score(at):
        g, pair, m = units[at]
        if (g, 0) not in ready:
            for i, operands in enumerate(prepare(g)):
                ready[g, i] = operands
        if m == 0:
            place_bias(g, pair)
        left, kl, _ = ready[g, m]
        keys = cat([kl * mask for mask in masks[2 * pair : 2 * pair + 2]], 0)
        logit_ref[at % 2] = mm_nt(left, cat([keys, keys]))

    def weigh(at):
        g, pair, m = units[at]
        e_ref[g, pair, m] = jnp.exp2(logit_ref[at % 2] + pos_ref[pair % 2]).astype(BF)
        pltpu.make_async_copy(e_ref.at[g, pair, m], e_hbm.at[g, pair, m], sem.at[g, pair, m]).start()

    def mix(at):
        g, pair, m = units[at]
        vl = ready[g, m][2]
        here = masks[2 * pair : 2 * pair + 2]
        values = cat([cat([vl * mask for mask in here], 0), cat([ones * mask for mask in here], 0)])
        mixed = mm(e_ref[g, pair, m], values)
        if pair == 0:
            mix_ref[m] = mixed
        elif pair < pairs - 1:
            mix_ref[m] += mixed
        else:
            mixed = mix_ref[m] + mixed
            rows = slice(m * WIN, (m + 1) * WIN)
            lanes = slice(g * LANES, (g + 1) * LANES)
            inverse = 1.0 / mixed[:, LANES:]
            high, low = split(mixed[:, :LANES] * inverse)
            ctx_ref[rows, lanes] = high
            rest_ref[rows, lanes] = low
            pick = flag(((row & (HEAD - 1)) == 0) & (stat_lane(2, g, row >> 5) == col))
            stat_ref[rows, :] += head_sums(inverse, pick)
            if m == images - 1:
                for source, target in ((ctx_ref, ctx_hbm), (rest_ref, rest_hbm)):
                    store(source.at[:, pl.ds(g * LANES, LANES)], target.at[:, pl.ds(g * LANES, LANES)])

    score(0)
    for at in range(len(units)):
        if at + 1 < len(units):
            score(at + 1)
        weigh(at)
        if at > 0:
            mix(at - 1)
    mix(len(units) - 1)
    for g, pair, m in units:
        pltpu.make_async_copy(e_ref.at[g, pair, m], e_hbm.at[g, pair, m], sem.at[g, pair, m]).wait()
    for copy in stores:
        copy.wait()


def attention_forward(index, x, ws, ps, coords, net_first, net_seconds):
    count, depth = x.shape
    images = count // WIN
    halves = ws[0].shape[2] // LANES
    groups = 2 * halves
    heads = groups * PER_GROUP
    wide = groups * LANES
    pairs = PER_GROUP // 2
    weights = (groups, pairs, images, WIN, 2 * WIN)
    near = [*ps, coords, *net_first, *net_seconds]
    far_out = [weights] + [(count, wide)] * 5 + [(count, depth), (WIN, WIN), (WIN, WIN)]
    near_out = [jax.ShapeDtypeStruct((count, LANES), F32), jax.ShapeDtypeStruct((2, wide // 2), F32)]
    return pl.pallas_call(
        functools.partial(forward_kernel, images, halves),
        grid=(1,),
        in_specs=[pl.BlockSpec((8, WIN), lambda i: (0, 0)), pl.BlockSpec((WIN, LANES), lambda i: (0, 0))]
        + [whole(a.shape) for a in near] + [FAR] * 3,
        out_specs=[whole(a.shape) for a in near_out] + [FAR] * len(far_out),
        out_shape=near_out + [jax.ShapeDtypeStruct(shape, BF) for shape in far_out],
        scratch_shapes=[pltpu.VMEM(x.shape, BF)] + [pltpu.VMEM(w.shape, BF) for w in ws]
        + [pltpu.VMEM(shape, BF) for shape in far_out]
        + [
            pltpu.VMEM((2, heads, WIDE), F32),
            pltpu.VMEM((2, WIN, 2 * WIN), F32),
            pltpu.VMEM((2, WIN, 2 * WIN), F32),
            pltpu.VMEM((images, WIN, 2 * LANES), F32),
            pltpu.SemaphoreType.DMA((3,)),
            pltpu.SemaphoreType.DMA((groups, pairs, images)),
            pltpu.SemaphoreType.DMA((5 * groups + 3,)),
        ],
        compiler_params=params(mib=54, dimension_semantics=("arbitrary",)),
        cost_estimate=cost(8_000_000_000, 40_000_000),
        name="attention_forward",
    )(index, index, *near, x, *ws)


def norm_stats(values):
    center = values - jnp.mean(values, axis=1, keepdims=True)
    inverse = lax.rsqrt(jnp.mean(center * center, axis=1, keepdims=True) + 1e-05)
    return center * inverse, inverse


def norm_back(grad, unit, inverse, gain):
    scaled = grad * gain
    mean = jnp.mean(scaled, axis=1, keepdims=True)
    along = jnp.mean(scaled * unit, axis=1, keepdims=True)
    return inverse * (scaled - mean - unit * along)


def feed_kernel(
    images, scatter_ref, x_ref, mix_ref, wo_a_ref, wo_b_ref, p_a_ref, p_b_ref,
    bo_ref, g1_ref, s1_ref, b2_ref, g2_ref, s2_ref, w1_a_hbm, w1_b_hbm, w2_a_hbm, w2_b_hbm, og_hbm,
    out_hbm, dmid_hbm, da_hbm, own_hbm, other_hbm, small_ref, gb1_ref,
    w1_ref, w2_ref, og_ref, out_ref, da_ref, dm_ref, pack_ref, mid_ref,
    ctx_ref, low_ref, pre_ref, hid_ref, slope_ref, grad_ref, acc_ref, unit_ref, in_sem, out_sem,
):
    half = w1_ref.shape[2]
    depth = x_ref.shape[1]
    narrow = wo_a_ref.shape[0]
    tiles = 2 * half // TILE
    ps = (p_a_ref, p_b_ref)
    packed = (own_hbm, other_hbm)
    loads = [
        pltpu.make_async_copy(source, target, in_sem.at[i])
        for i, (source, target) in enumerate(
            (
                (w1_a_hbm, w1_ref.at[0]), (w1_b_hbm, w1_ref.at[1]), (w2_a_hbm, w2_ref.at[0]),
                (w2_b_hbm, w2_ref.at[1]), (og_hbm, og_ref),
            )
        )
    ]
    for load in loads:
        load.start()
    stores = []

    def store(source, target):
        copy = pltpu.make_async_copy(source, target, out_sem.at[len(stores)])
        copy.start()
        stores.append(copy)

    def place_of(tile):
        at = tile * TILE
        return at // half, slice(at % half, at % half + TILE)

    inverse_ones = []
    for m in range(images):
        rows = slice(m * WIN, (m + 1) * WIN)
        ctx = mm(scatter_ref[...], mix_ref[rows, :]).astype(BF)
        ctx_ref[rows, :] = ctx
        attn = mm(ctx[:, :narrow], wo_a_ref[...]) + mm(ctx[:, narrow:], wo_b_ref[...]) + bo_ref[...]
        unit_one, inverse = norm_stats(attn)
        inverse_ones.append(inverse)
        unit_ref[rows, :] = unit_one
        middle = x_ref[rows, :].astype(F32) + unit_one * g1_ref[...] + s1_ref[...]
        mid_ref[rows, :] = middle
        low_ref[rows, :] = middle.astype(BF)

    def up(tile):
        which, cols = place_of(tile)
        if cols.start == 0:
            loads[which].wait()
        row = 3 + cols.start // TILE
        pre_ref[tile % 2] = mm(low_ref[...], w1_ref[which, :, cols]) + ps[which][row : row + 1, :]

    def down(tile):
        which, cols = place_of(tile)
        if cols.start == 0:
            loads[2 + which].wait()
        term = mm(hid_ref[which, :, cols], w2_ref[which, cols, :])
        if tile == 0:
            acc_ref[...] = term
        else:
            acc_ref[...] += term

    up(0)
    for tile in range(tiles):
        if tile + 1 < tiles:
            up(tile + 1)
        which, cols = place_of(tile)
        hidden, slope = gelu_with_slope(pre_ref[tile % 2])
        hid_ref[which, :, cols] = hidden.astype(BF)
        slope_ref[which, :, cols] = slope
        if tile > 0:
            down(tile - 1)
    down(tiles - 1)

    loads[4].wait()
    sums = [jnp.zeros((1, depth), F32)] * 3
    for m in range(images):
        rows = slice(m * WIN, (m + 1) * WIN)
        unit_two, inverse_two = norm_stats(acc_ref[rows, :] + b2_ref[...])
        out_ref[rows, :] = (mid_ref[rows, :] + (unit_two * g2_ref[...] + s2_ref[...])).astype(BF)
        grad = og_ref[rows, :].astype(F32)
        d_mlp = norm_back(grad, unit_two, inverse_two, g2_ref[...])
        terms = (column_sums(d_mlp), column_sums(grad * unit_two), column_sums(grad))
        sums = [a + b for a, b in zip(sums, terms)]
        dm_ref[rows, :] = d_mlp.astype(BF)
        acc_ref[rows, :] = grad
    store(out_ref, out_hbm)
    for i in range(3):
        small_ref[3 + i : 4 + i, :] = sums[i]

    for tile in range(tiles):
        which, cols = place_of(tile)
        d_pre = mm_nt(dm_ref[...], w2_ref[which, cols, :]) * slope_ref[which, :, cols]
        gb1_ref[which : which + 1, cols] = column_sums(d_pre)
        d_pre_low = d_pre.astype(BF)
        grad_ref[which, :, cols] = d_pre_low
        acc_ref[...] += mm_nt(d_pre_low, w1_ref[which, :, cols])
    store(acc_ref, dmid_hbm)

    def weight_grads(tile):
        which, cols = place_of(tile)
        at = cols.start
        pack_ref[which, half + at : half + at + TILE, :] = mm_tn(hid_ref[which, :, cols], dm_ref[...]).astype(BF)
        rows = slice(at // depth * depth, (at // depth + 1) * depth)
        grads = mm_tn(low_ref[...], grad_ref[which, :, cols]).astype(BF)
        pack_ref[which, rows, at % depth : at % depth + TILE] = grads
        if at + TILE == half:
            span = pl.ds(0, 2 * half)
            store(pack_ref.at[which, span], packed[which].at[span])

    sums = [jnp.zeros((1, depth), F32)] * 3
    for tile in range(tiles):
        weight_grads(tile)
        if tile < images:
            rows = slice(tile * WIN, (tile + 1) * WIN)
            d_middle = acc_ref[rows, :]
            unit_one = unit_ref[rows, :]
            d_attn = norm_back(d_middle, unit_one, inverse_ones[tile], g1_ref[...])
            terms = (column_sums(d_attn), column_sums(d_middle * unit_one), column_sums(d_middle))
            sums = [a + b for a, b in zip(sums, terms)]
            da_ref[rows, :] = d_attn.astype(BF)
        if tile == images - 1:
            store(da_ref, da_hbm)
    for i in range(3):
        small_ref[i : i + 1, :] = sums[i]
    span = pl.ds(2 * half, narrow)
    for which in range(2):
        pack_ref[which, 2 * half : 2 * half + narrow, :] = mm_tn(
            ctx_ref[:, which * narrow : (which + 1) * narrow], da_ref[...]
        ).astype(BF)
        store(pack_ref.at[which, span], packed[which].at[span])
    for copy in stores:
        copy.wait()


def feed_forward(scatter, x, ctx, wos, w1s, w2s, ps, vectors, cotangent):
    count, depth = x.shape
    images = count // WIN
    narrow = wos[0].shape[0]
    half = w1s[0].shape[1]
    packed = 2 * half + narrow
    low = pltpu.VMEM((count, depth), BF)
    full = pltpu.VMEM((count, depth), F32)
    return pl.pallas_call(
        functools.partial(feed_kernel, images),
        in_specs=[NEAR] * 13 + [FAR] * 5,
        out_specs=[FAR] * 5 + [NEAR] * 2,
        out_shape=[
            jax.ShapeDtypeStruct((count, depth), BF),
            jax.ShapeDtypeStruct((count, depth), F32),
            jax.ShapeDtypeStruct((count, depth), BF),
            jax.ShapeDtypeStruct((packed, depth), BF),
            jax.ShapeDtypeStruct((packed, depth), BF),
            jax.ShapeDtypeStruct((8, depth), F32),
            jax.ShapeDtypeStruct((2, half), F32),
        ],
        scratch_shapes=[
            pltpu.VMEM((2, depth, half), BF),
            pltpu.VMEM((2, half, depth), BF),
            low, low, low, low,
            pltpu.VMEM((2, packed, depth), BF),
            full,
            pltpu.VMEM((count, 2 * narrow), BF),
            low,
            pltpu.VMEM((2, count, TILE), F32),
            pltpu.VMEM((2, count, half), BF),
            pltpu.VMEM((2, count, half), F32),
            pltpu.VMEM((2, count, half), BF),
            full, full,
            pltpu.SemaphoreType.DMA((5,)),
            pltpu.SemaphoreType.DMA((7,)),
        ],
        compiler_params=params(mib=56),
        cost_estimate=cost(2 * count * depth * (2 * depth + 12 * half), 30_000_000),
        name="feed_forward",
    )(scatter, x, ctx, *wos, *ps, *vectors, *w1s, *w2s, cotangent)


def context_grad_kernel(images, gather_ref, da_ref, wo_a_ref, wo_b_ref, out_ref):
    for m in range(images):
        rows = slice(m * WIN, (m + 1) * WIN)
        grad = cat([mm_nt(da_ref[rows, :], wo_a_ref[...]), mm_nt(da_ref[rows, :], wo_b_ref[...])]).astype(BF)
        out_ref[rows, :] = mm(gather_ref[...], grad).astype(BF)


def context_grad(gather, d_attn, wos):
    return pl.pallas_call(
        functools.partial(context_grad_kernel, d_attn.shape[0] // WIN),
        out_shape=jax.ShapeDtypeStruct((d_attn.shape[0], 2 * wos[0].shape[0]), BF),
        compiler_params=params(),
        cost_estimate=cost(2_000_000_000, 5_000_000),
        name="context_grad",
    )(gather, d_attn, *wos)


def backward_kernel(
    images, first, span, x_ref, scale_ref, dctx_ref, ctx_ref, rest_ref, ql_ref, kl_ref, vl_ref, stat_ref, e_hbm,
    gw_ref, dqkv_ref, dm_ref, small_ref,
    e_ref, prob_ref, low_ref, sum_ref, duq_ref, dkt_ref, dvt_ref, sem,
):
    pairs = PER_GROUP // 2
    which = first // span
    units = [(g, pair, m) for g in range(span) for pair in range(pairs) for m in range(images)]
    loads = {
        unit: pltpu.make_async_copy(e_hbm.at[first + unit[0], unit[1], unit[2]], e_ref.at[unit], sem.at[unit])
        for unit in units
    }
    for load in loads.values():
        load.start()
    masks = head_masks()
    summing = head_sum_matrix()
    unit_matrix = flag(iota((LANES, LANES), 0) == iota((LANES, LANES), 1))
    shape = (2 * LANES, 3 * LANES)
    col = iota(shape, 1)
    in_head = iota((1, LANES), 1) & (HEAD - 1)
    left_half = iota((1, WIDE), 1) < WIN
    spots = flag(in_head < 2)
    ready = {}
    sums = [[jnp.zeros((1, LANES), F32)] * 3 for _ in range(span)]

    def prepare(g, m):
        here = slice(g * LANES, (g + 1) * LANES)
        rows = slice(m * WIN, (m + 1) * WIN)
        spread = flag((iota(shape, 0) & (LANES - 1)) == stat_lane(col >> 7, first + g, (col & (LANES - 1)) >> 5))
        stats = head_sums(stat_ref[rows, :], spread)
        grad = (dctx_ref[rows, here].astype(F32) * (stats[:, 2 * LANES :] * scale_ref[which : which + 1, here])).astype(BF)
        mix = ctx_ref[rows, here].astype(F32) + rest_ref[rows, here].astype(F32)
        d_high, d_low = split(-head_sums(grad.astype(F32) * mix, summing))
        left = cat([grad, jnp.where(in_head == 0, d_high, d_low)])
        q_t = mm_nt(unit_matrix, ql_ref[rows, here]).astype(BF)
        grad_t = mm_nt(unit_matrix, grad).astype(BF)
        return left, q_t, grad_t, stats[:, : 2 * LANES]

    def score(at):
        g, pair, m = units[at]
        if (g, m) not in ready:
            ready[g, m] = prepare(g, m)
        vl = vl_ref[m * WIN : (m + 1) * WIN, g * LANES : (g + 1) * LANES]
        here = masks[2 * pair : 2 * pair + 2]
        right = cat([cat([vl * mask, jnp.broadcast_to(spots * mask, (WIN, LANES))]) for mask in here], 0)
        prob_ref[at % 2] = mm_nt(ready[g, m][0], right)

    def weigh(at):
        g, pair, m = units[at]
        loads[g, pair, m].wait()
        d_cos = e_ref[g, pair, m].astype(F32) * prob_ref[at % 2]
        low_ref[at % 2] = d_cos.astype(BF)
        if m == 0:
            sum_ref[pair % 2] = d_cos
        else:
            sum_ref[pair % 2] += d_cos
        if m == images - 1:
            one, two = None, None
            for r in range(SIDE):
                offset = (SIDE - 1 - r) * SIDE
                band = sum_ref[pair % 2, r * SIDE : (r + 1) * SIDE, :]
                left = pltpu.roll(jnp.where(left_half, band, 0.0), offset, 1)
                right = pltpu.roll(jnp.where(left_half, 0.0, band), (offset + WIN) % WIDE, 1)
                one = left if one is None else one + left
                two = right if two is None else two + right
            dm_ref[g * PER_GROUP + 2 * pair] = one
            dm_ref[g * PER_GROUP + 2 * pair + 1] = two

    def spend(at):
        g, pair, m = units[at]
        rows = slice(m * WIN, (m + 1) * WIN)
        here = slice(g * LANES, (g + 1) * LANES)
        _, q_t, grad_t, stats = ready[g, m]
        kl, ql = kl_ref[rows, here], ql_ref[rows, here]
        d_low = low_ref[at % 2]
        duq = mm(d_low, cat([kl * mask for mask in masks[2 * pair : 2 * pair + 2]], 0))
        head = pair * 2 * HEAD
        for ref, source, factor in ((dkt_ref, q_t, d_low), (dvt_ref, grad_t, e_ref[g, pair, m])):
            both = mm(source[head : head + 2 * HEAD], factor)
            ref[m, head : head + HEAD, :] = both[:HEAD, : ref.shape[2]]
            ref[m, head + HEAD : head + 2 * HEAD, :] = pltpu.roll(both[HEAD:], WIN, 1)[:, : ref.shape[2]]
        if pair == 0:
            duq_ref[m] = duq
        if 0 < pair < pairs - 1:
            duq_ref[m] += duq
        if pair == pairs - 1:
            duq = duq_ref[m] + duq
            uq = ql.astype(F32)
            along_q = head_sums(uq * duq, summing)
            dq = stats[:, :LANES] * (duq - uq * along_q)
            uk = kl.astype(F32)
            duk = jnp.transpose(dkt_ref[m])[:WIN]
            dk = stats[:, LANES:] * (duk - uk * head_sums(uk * duk, summing))
            dv = jnp.transpose(dvt_ref[m])[:WIN] / scale_ref[which : which + 1, here]
            sums[g] = [a + column_sums(t) for a, t in zip(sums[g], (dq, dv, along_q))]
            for i, grads in enumerate((dq, dk, dv)):
                lanes = (i * span + g) * LANES
                dqkv_ref[rows, lanes : lanes + LANES] = grads.astype(BF)

    score(0)
    for at in range(len(units)):
        if at + 1 < len(units):
            score(at + 1)
        weigh(at)
        if at > 0:
            spend(at - 1)
    spend(len(units) - 1)
    for g in range(span):
        for i in range(3):
            small_ref[g, i : i + 1, :] = sums[g][i]
    for i in range(3):
        gw = mm_tn(x_ref[...], dqkv_ref[:, i * span * LANES : (i + 1) * span * LANES]).astype(BF)
        for g in range(span):
            gw_ref[g, i] = gw[:, g * LANES : (g + 1) * LANES]


def attention_backward(first, span, x, scales, dctx, saved):
    e, *blocks, stat = saved
    count, depth = x.shape
    images = count // WIN
    padded = -(-WIN // LANES) * LANES
    block = pl.BlockSpec((count, span * LANES), lambda i: (0, first // span))
    shapes = [
        jax.ShapeDtypeStruct((span, 3, depth, LANES), BF),
        jax.ShapeDtypeStruct((count, span * 3 * LANES), BF),
        jax.ShapeDtypeStruct((span * PER_GROUP, SIDE, WIDE), F32),
        jax.ShapeDtypeStruct((span, 8, LANES), F32),
    ]
    return pl.pallas_call(
        functools.partial(backward_kernel, images, first, span),
        grid=(1,),
        in_specs=[whole(x.shape), whole(scales.shape)] + [block] * 6
        + [whole(stat.shape), FAR],
        out_specs=[whole(a.shape) for a in shapes],
        out_shape=shapes,
        scratch_shapes=[
            pltpu.VMEM((span,) + e.shape[1:], BF),
            pltpu.VMEM((2, WIN, 2 * WIN), F32),
            pltpu.VMEM((2, WIN, 2 * WIN), BF),
            pltpu.VMEM((2, WIN, 2 * WIN), F32),
            pltpu.VMEM((images, WIN, LANES), F32),
            pltpu.VMEM((images, LANES, padded), F32),
            pltpu.VMEM((images, LANES, padded), F32),
            pltpu.SemaphoreType.DMA((span,) + e.shape[1:3]),
        ],
        compiler_params=params(mib=56, dimension_semantics=("arbitrary",)),
        cost_estimate=cost(8_000_000_000 * span, 20_000_000 * span),
        name=f"attention_backward_{first}",
    )(x, scales, dctx, *blocks, stat, e)


def input_grad_kernel(scatter_ref, dmid_ref, da_ref, db_ref, w_a_ref, w_b_ref, out_ref):
    wide = w_a_ref.shape[2]
    total = None
    for grad_ref, w_ref in ((da_ref, w_a_ref), (db_ref, w_b_ref)):
        for i in range(3):
            term = mm_nt(grad_ref[:, i * wide : (i + 1) * wide], w_ref[i])
            total = term if total is None else total + term
    high, low = split(total)
    out_ref[...] = dmid_ref[...] + mm(scatter_ref[...], high) + mm(scatter_ref[...], low)


def input_grad(scatter, d_middle, grads, ws):
    count, depth = d_middle.shape
    rows = lambda width: pl.BlockSpec((WIN, width), lambda i: (i, 0))
    return pl.pallas_call(
        input_grad_kernel,
        grid=(count // WIN,),
        in_specs=[whole(scatter.shape), rows(depth)] + [rows(g.shape[1]) for g in grads] + [whole(w.shape) for w in ws],
        out_specs=rows(depth),
        out_shape=jax.ShapeDtypeStruct(d_middle.shape, F32),
        compiler_params=params(mib=14, dimension_semantics=("arbitrary",)),
        cost_estimate=cost(3_000_000_000, 12_000_000),
        name="input_grad",
    )(scatter, d_middle, *grads, *ws)


def table_back_kernel(spans, coord_ref, w1_ref, b1_ref, w2_a_ref, w2_b_ref, scale_ref, vec_ref, gb1_ref, *refs):
    calls = len(spans)
    dms, smalls, (own_ref, other_ref) = refs[:calls], refs[calls : 2 * calls], refs[2 * calls :]
    lower = iota((1, WIDE), 1) % PITCH < SIDE
    even, odd = [], []
    for ref in dms:
        e = jnp.zeros((ref.shape[0], WIDE), F32)
        o = jnp.zeros((ref.shape[0], WIDE), F32)
        for c in range(SIDE):
            slab = ref[:, c, :]
            e = e + pltpu.roll(jnp.where(lower, slab, 0.0), (SIDE - 1 - c) % WIDE, 1)
            o = o + pltpu.roll(jnp.where(lower, 0.0, slab), (-1 - c) % WIDE, 1)
        even.append(e)
        odd.append(o)
    w2s = (w2_a_ref[...], w2_b_ref[...])
    columns = net_columns(w1_ref, b1_ref)
    shape = (w2s[0].shape[0], scale_ref.shape[1])
    diagonal = iota(shape, 0) * HEAD == iota(shape, 1)
    inverses = [
        1.0 / jnp.sum(jnp.where(diagonal, scale_ref[i : i + 1, :], 0.0), axis=1, keepdims=True) for i in range(2)
    ]
    inverse = cat(inverses, 0)
    dw2 = None
    dcols = None
    for parity, grads in enumerate((even, odd)):
        hidden, slope = gelu_with_slope(table_pre(coord_ref, columns, parity))
        table = table_of(hidden, w2s)
        dz = cat(grads, 0) * inverse * table * (1.0 - table * 0.0625)
        hidden_high, hidden_low = split(hidden)
        dz_high, dz_low = split(dz)
        term = mm_nt(dz_high, hidden_high) + mm_nt(dz_high, hidden_low) + mm_nt(dz_low, hidden_high)
        dw2 = term if dw2 is None else dw2 + term
        w2 = cat(w2s, 0)
        high, low = split((mm_tn(w2, dz_high) + mm_tn(w2, dz_low)) * slope)
        c_high, c_low = split(coord_ref[parity])
        term = mm_nt(c_high, high) + mm_nt(c_high, low) + mm_nt(c_low, high)
        dcols = term if dcols is None else dcols + term
    heads = w2s[0].shape[0]
    groups = [(ref, g) for ref, span in zip(smalls, spans) for g in range(span)]
    for which, out in enumerate((own_ref, other_ref)):
        lines = [(vec_ref, i) for i in range(6)] + [(dcols, i) for i in range(3)] + [(gb1_ref, which)]
        row = 0
        for source, i in lines + [(dw2, which * heads + h) for h in range(heads)]:
            for at in range(0, source.shape[1], LANES):
                out[row : row + 1, :] = source[i : i + 1, at : at + LANES]
                row += 1
        for ref, g in groups[which * len(groups) // 2 : (which + 1) * len(groups) // 2]:
            for i in range(3):
                out[row : row + 1, :] = ref[g, i : i + 1, :]
                row += 1
        out[row:, :] = jnp.zeros((SMALL_ROWS - row, LANES), F32)


def table_back(coords, net_first, w2s, scales, vectors, gb1, dms, smalls):
    small = jax.ShapeDtypeStruct((SMALL_ROWS, LANES), F32)
    return pl.pallas_call(
        functools.partial(table_back_kernel, [s.shape[0] for s in smalls]),
        out_shape=(small, small),
        compiler_params=params(mib=22),
        cost_estimate=cost(1_000_000_000, 10_000_000),
        name="table_back",
    )(coords, *net_first, *w2s, scales, vectors, gb1, *dms, *smalls)


def swap(array):
    return lax.ppermute(array, "mp", [(0, 1), (1, 0)])


def tie(*trees):
    leaves, kind = jax.tree.flatten(trees)
    return jax.tree.unflatten(kind, lax.optimization_barrier(leaves))


def send(array, plan, phase, step):
    pairs = []
    for mp, strides in enumerate(plan):
        stride = strides[phase]
        for dp in range(16):
            digit = dp // stride % 4
            pairs.append((2 * dp + mp, 2 * (dp + ((digit ^ step) - digit) * stride) + mp))
    return lax.ppermute(array, ("dp", "mp"), pairs)


def rotate_kernel(count, digit_ref, *refs):
    sources, targets = refs[:count], refs[count : count + 4]
    in_ref, out_ref, in_sem, out_sem = refs[count + 4 :]
    rows = out_ref.shape[1]
    order = (1, 2, 3, 0)
    loads, stores = {}, []
    for t in order:
        at = pl.multiple_of((digit_ref[0] ^ t) * rows, 16)
        for i, source in enumerate(sources):
            loads[t, i] = pltpu.make_async_copy(source.at[pl.ds(at, rows)], in_ref.at[i, t], in_sem.at[i, t])
            loads[t, i].start()
    for t in order:
        total = None
        for i in range(count):
            loads[t, i].wait()
            term = in_ref[i, t].astype(F32)
            total = term if total is None else total + term
        out_ref[t] = total.astype(BF)
        stores.append(pltpu.make_async_copy(out_ref.at[t], targets[t], out_sem.at[t]))
        stores[-1].start()
    for store in stores:
        store.wait()


def rotate_sum(arrays, digit):
    rows, lanes = arrays[0].shape
    rows //= 4
    count = len(arrays)
    return pl.pallas_call(
        functools.partial(rotate_kernel, count),
        in_specs=[SCALARS] + [FAR] * count,
        out_specs=[FAR] * 4,
        out_shape=[jax.ShapeDtypeStruct((rows, lanes), BF)] * 4,
        scratch_shapes=[
            pltpu.VMEM((count, 4, rows, lanes), BF),
            pltpu.VMEM((4, rows, lanes), BF),
            pltpu.SemaphoreType.DMA((count, 4)),
            pltpu.SemaphoreType.DMA((4,)),
        ],
        compiler_params=params(mib=12),
        cost_estimate=cost(1_000_000, 6 * rows * lanes * count),
        name="rotate_sum",
    )(digit, *arrays)


def add_all(blocks):
    total = blocks[0].astype(F32)
    for block in blocks[1:]:
        total = total + block.astype(F32)
    return total


def fetch(sources, buffer_ref, sem):
    loads = [pltpu.make_async_copy(ref, buffer_ref.at[i], sem.at[i]) for i, ref in enumerate(sources)]
    for load in loads:
        load.start()
    return loads


def lay_feed_kernel(digit_ref, a, b, c, d, up_ref, down_ref, proj_ref, in_ref, held_ref, in_sem, out_sem):
    rows = in_ref.shape[1]
    for s, load in enumerate(fetch((a, b, c, d), in_ref, in_sem)):
        at = (digit_ref[0] ^ s) * rows
        load.wait()
        held_ref[pl.ds(pl.multiple_of(at, 16), rows), :] = in_ref[s].astype(F32)
    depth, half = up_ref.shape
    parts = [
        (held_ref.at[pl.ds(at, depth)], up_ref.at[:, pl.ds(at, depth)]) for at in range(0, half, depth)
    ]
    parts.append((held_ref.at[pl.ds(half, half)], down_ref))
    parts.append((held_ref.at[pl.ds(2 * half, proj_ref.shape[0])], proj_ref))
    stores = [pltpu.make_async_copy(x, y, out_sem.at[i]) for i, (x, y) in enumerate(parts)]
    for store in stores:
        store.start()
    for store in stores:
        store.wait()


def lay_feed(outer, blocks, depth, half, narrow):
    rows = 2 * half + narrow
    return pl.pallas_call(
        lay_feed_kernel,
        in_specs=[SCALARS] + [FAR] * 4,
        out_specs=[FAR] * 3,
        out_shape=[
            jax.ShapeDtypeStruct((depth, half), F32),
            jax.ShapeDtypeStruct((half, depth), F32),
            jax.ShapeDtypeStruct((narrow, depth), F32),
        ],
        scratch_shapes=[
            pltpu.VMEM((4, rows // 4, depth), BF),
            pltpu.VMEM((rows, depth), F32),
            pltpu.SemaphoreType.DMA((4,)),
            pltpu.SemaphoreType.DMA((half // depth + 2,)),
        ],
        compiler_params=params(mib=12),
        cost_estimate=cost(1_000_000, 8_000_000),
        name="lay_feed",
    )(outer, *blocks)


def lay_rest_kernel(
    halves, digit_ref, a, b, c, d,
    gw_ref, shift_ref, scale_ref, w1_ref, b1_ref, w2_ref, gb1_ref, bp_ref, g1_ref, h1_ref, bd_ref, g2_ref, h2_ref,
    in_ref, held_ref, in_sem,
):
    depth = gw_ref.shape[1]
    quarter = held_ref.shape[0] // 4
    for s, load in enumerate(fetch((a, b, c, d), in_ref, in_sem)):
        at = (digit_ref[0] ^ s) * quarter
        load.wait()
        held_ref[pl.ds(pl.multiple_of(at, 16), quarter), :] = in_ref[s, :quarter, :]
    small = add_all([in_ref[s, quarter:, :] for s in range(4)])
    for g in range(halves):
        for i in range(3):
            at = (g * 3 + i) * depth
            gw_ref[i, :, g * LANES : (g + 1) * LANES] = held_ref[at : at + depth, :].astype(F32)
    row = 0

    def line(length):
        nonlocal row
        count = length // LANES
        out = cat([small[row + i : row + i + 1, :] for i in range(count)])
        row += count
        return out

    for ref in (bp_ref, g1_ref, h1_ref, bd_ref, g2_ref, h2_ref):
        ref[...] = line(ref.shape[1])
    w1_ref[...] = cat([line(w1_ref.shape[1]) for _ in range(2)], 0)
    b1_ref[...] = line(b1_ref.shape[1])
    gb1_ref[...] = line(gb1_ref.shape[1])
    heads, units = w2_ref.shape
    w2_ref[...] = cat([line(units) for _ in range(heads)], 0)
    groups = [[line(LANES) for _ in range(3)] for _ in range(halves)]
    for i in range(2):
        shift_ref[i : i + 1, :] = cat([group[i] for group in groups])
    scale = cat([group[2] for group in groups])
    pick = iota((1, scale.shape[1]), 1)
    scale_ref[...] = cat(
        [jnp.sum(jnp.where(pick == h * HEAD, scale, 0.0), axis=1, keepdims=True) for h in range(heads)]
    )


def lay_rest(outer, blocks, depth, halves, half, units):
    width = halves * LANES
    heads = halves * PER_GROUP
    shapes = [(3, depth, width), (2, width), (1, heads), (2, units), (1, units), (heads, units), (1, half)]
    shapes += [(1, depth)] * 6
    return pl.pallas_call(
        functools.partial(lay_rest_kernel, halves),
        in_specs=[SCALARS] + [FAR] * 4,
        out_specs=[NEAR] * len(shapes),
        out_shape=[jax.ShapeDtypeStruct(s, F32) for s in shapes],
        scratch_shapes=[
            pltpu.VMEM((4,) + blocks[0].shape, BF),
            pltpu.VMEM((halves * 3 * depth, LANES), BF),
            pltpu.SemaphoreType.DMA((4,)),
        ],
        compiler_params=params(mib=16),
        cost_estimate=cost(1_000_000, 8_000_000),
        name="lay_rest",
    )(outer, *blocks)


def on_device(
    size, tokens, query_key_value_matrix, query_value_bias, head_logit_scale, bias_net_first_weight,
    bias_net_first_bias, bias_net_second_weight, relative_pair_index, attention_out_weight, attention_out_bias,
    attention_norm_weight, attention_norm_bias, ffn_input_weight, hidden_ffn_bias, ffn_output_weight,
    output_ffn_bias, feedforward_norm_weight, feedforward_norm_bias, output_gradient,
):
    depth = tokens.shape[1]
    width = query_key_value_matrix.shape[2]
    halves = width // LANES
    half = ffn_input_weight.shape[1]
    units = bias_net_first_bias.shape[0]

    def pair(array):
        return array, swap(array)

    ws = pair(jnp.transpose(query_key_value_matrix, (1, 0, 2)))
    ps = pair(
        jnp.concatenate(
            [
                query_value_bias.astype(F32),
                jnp.repeat(jnp.exp(head_logit_scale.astype(F32)), HEAD)[None],
                hidden_ffn_bias.astype(F32).reshape(-1, TILE),
                jnp.zeros((5 - half // TILE, width), F32),
            ]
        )
    )
    net_seconds = pair(bias_net_second_weight.T)
    wos = pair(attention_out_weight)
    w1s = pair(ffn_input_weight)
    w2s = pair(ffn_output_weight)

    coords = jnp.asarray(coord_rows())
    net_first = (bias_net_first_weight, bias_net_first_bias.reshape(1, units))
    stat, scale_lanes, *saved, cells, gather, scatter = attention_forward(
        relative_pair_index, tokens, ws, ps, coords, net_first, net_seconds
    )
    saved.append(stat)
    vectors = [
        v.reshape(1, depth)
        for v in (
            attention_out_bias, attention_norm_weight, attention_norm_bias,
            output_ffn_bias, feedforward_norm_weight, feedforward_norm_bias,
        )
    ]
    block_out, d_middle, d_attn, own, other, vector_grads, gb1 = feed_forward(
        scatter, tokens, saved[1], wos, w1s, w2s, ps, vectors, output_gradient
    )

    def backward(which, dctx):
        return attention_backward(which * halves, halves, cells, scale_lanes, dctx, saved)

    def tail_small(results):
        return table_back(
            coords, net_first, net_seconds, scale_lanes, vector_grads, gb1,
            [r[2] for r in results], [r[3] for r in results],
        )

    def lines(array):
        return array.reshape(-1, LANES)

    dctx = context_grad(gather, d_attn, wos)
    if size == 16:
        dp, mp = lax.axis_index("dp"), lax.axis_index("mp")
        plan, rest_plan = ((1, 4), (4, 1)), ((1, 4), (1, 4))
        near, far = dp & 3, dp >> 2
        outer = jnp.where(mp == 0, near, far).reshape(1)

        def spread(blocks, phase, plan=plan):
            return [send(b, plan, phase, t + 1) for t, b in enumerate(blocks)]

        got, dctx = tie(swap(other), dctx)
        blocks = rotate_sum([own, got], outer)
        blocks, dctx = tie(blocks, dctx)
        got = spread(blocks[1:], 0)
        theirs = backward(1, dctx)
        got, theirs, dctx = tie(got, theirs, dctx)
        low = add_all([blocks[0]] + got).astype(BF)
        low, dctx = tie(low, dctx)
        got = spread([low] * 3, 1)
        rest_got = swap(lines(theirs[0]))
        mine = backward(0, dctx)
        got, rest_got, mine = tie(got, rest_got, mine)
        low = add_all([low] + got).astype(BF)
        rest = rotate_sum([lines(mine[0]), rest_got], near.reshape(1))
        rest, low = tie(rest, low)
        rest_got = spread(rest[1:], 0, rest_plan)
        gathered = spread([low] * 2, 0)
        results = [mine, theirs]
        small_own, small_other = tail_small(results)
        small = small_own + swap(small_other)
        rest_got, small, gathered[1] = tie(rest_got, small, gathered[1])
        gathered += spread([gathered[1]], 0)
        message = jnp.concatenate([add_all([rest[0]] + rest_got), small]).astype(BF)
        rest_got = spread([message] * 3, 1, rest_plan)
        tokens_grad = input_grad(scatter, d_middle, [r[1] for r in results], ws)
        rest_got, tokens_grad = tie(rest_got, tokens_grad)
        message = add_all([message] + rest_got).astype(BF)
        rest_got = spread([message] * 3, 0, rest_plan)
        feed = lay_feed(outer, [low] + gathered, depth, half, width)
        rest_got, feed = tie(rest_got, feed)
        final = lay_rest(near.reshape(1), [message] + rest_got, depth, halves, half, units)
    else:
        results = [backward(0, dctx), backward(1, dctx)]
        small_own, small_other = tail_small(results)
        tokens_grad = input_grad(scatter, d_middle, [r[1] for r in results], ws)
        outer = jnp.zeros((1,), jnp.int32)

        def total(array):
            return lax.psum(array, "dp").astype(BF)

        def quarters(array):
            rows = array.shape[0] // 4
            return [array[s * rows : (s + 1) * rows] for s in range(4)]

        feed = lay_feed(outer, quarters(total(own.astype(F32) + swap(other).astype(F32))), depth, half, width)
        rest = total(lines(results[0][0]).astype(F32) + swap(lines(results[1][0])).astype(F32))
        small = total(small_own + swap(small_other))
        none = jnp.zeros_like(small)
        blocks = [jnp.concatenate([block, none if s else small]) for s, block in enumerate(quarters(rest))]
        final = lay_rest(outer, blocks, depth, halves, half, units)

    grad_up, grad_down, grad_proj = feed
    grad_qkv, grad_shift, grad_scale, grad_w1, grad_b1, grad_w2, grad_hidden, *vec = final
    vec = [v.reshape(-1) for v in vec]
    return (
        block_out, tokens_grad, jnp.transpose(grad_qkv, (1, 0, 2)), grad_shift, grad_scale.reshape(-1),
        grad_w1, grad_b1.reshape(-1), grad_w2.T, grad_proj, vec[0], vec[1], vec[2],
        grad_up, grad_hidden.reshape(-1), grad_down, vec[3], vec[4], vec[5],
    )


def solution(mesh):
    in_specs = (
        P(("dp", "mp"), None), P(None, None, "mp"), P(None, "mp"), P("mp"), P(), P(), P(None, "mp"), P(),
        P("mp", None), P(), P(), P(), P(None, "mp"), P("mp"), P("mp", None), P(), P(), P(), P(("dp", "mp"), None),
    )
    out_specs = (
        P(("dp", "mp"), None), P(("dp", "mp"), None), P(None, None, "mp"), P(None, "mp"), P("mp"), P(), P(),
        P(None, "mp"), P("mp", None), P(), P(), P(), P(None, "mp"), P("mp"), P("mp", None), P(), P(), P(),
    )
    return jax.shard_map(
        functools.partial(on_device, mesh.shape["dp"]),
        mesh=mesh, in_specs=in_specs, out_specs=out_specs, check_vma=False,
    )
```

```python
import functools

import jax
import jax.numpy as jnp
import numpy as np
from jax import lax
from jax.experimental import pallas as pl
from jax.experimental.pallas import tpu as pltpu
from jax.sharding import PartitionSpec as P

SIDE = 24
WIN = SIDE * SIDE
TABLE_SIDE = 2 * SIDE - 1
PITCH = 2 * SIDE
WIDE = SIDE * PITCH
HEAD = 32
LANES = 128
PER_GROUP = LANES // HEAD
TILE = 256
SMALL_ROWS = 96
LOG2E = 1.4426950408889634
MIB = 1024 * 1024
BF = jnp.bfloat16
F32 = jnp.float32
FAR = pl.BlockSpec(memory_space=pl.ANY)
NEAR = pl.BlockSpec(memory_space=pltpu.VMEM)
SCALARS = pl.BlockSpec(memory_space=pltpu.SMEM)


def mm(left, right):
    return lax.dot_general(left, right, (((1,), (0,)), ((), ())), preferred_element_type=F32)


def mm_nt(left, right):
    return lax.dot_general(left, right, (((1,), (1,)), ((), ())), preferred_element_type=F32)


def mm_tn(left, right):
    return lax.dot_general(left, right, (((0,), (0,)), ((), ())), preferred_element_type=F32)


def split(values):
    high = values.astype(BF)
    return high, (values - high.astype(F32)).astype(BF)


def iota(shape, axis):
    return lax.broadcasted_iota(jnp.int32, shape, axis)


def cat(parts, axis=1):
    return jnp.concatenate(parts, axis=axis)


def flag(condition):
    return jnp.where(condition, 1.0, 0.0).astype(BF)


def column_sums(values):
    return jnp.sum(values, axis=0, keepdims=True)


def gelu_with_slope(values):
    cdf = 0.5 + 0.5 * lax.erf(values * 0.7071067811865476)
    bell = jnp.exp2(values * values * (-0.5 * LOG2E)) * 0.3989422804014327
    return values * cdf, cdf + values * bell


def cell_of_places(index_line, axis):
    row_part = (index_line * 22311) >> 20
    col_part = index_line - row_part * TABLE_SIDE
    if axis == 1:
        rows = jnp.max(row_part, axis=1, keepdims=True) - row_part
        cols = jnp.max(col_part, axis=1, keepdims=True) - col_part
    else:
        rows = row_part - jnp.min(row_part, axis=0, keepdims=True)
        cols = col_part - jnp.min(col_part, axis=0, keepdims=True)
    return rows * SIDE + cols


def head_sum_matrix():
    row = iota((2 * LANES, LANES), 0)
    col = iota((2 * LANES, LANES), 1)
    return flag(((row >> 5) & 3) == (col >> 5))


def head_sums(values, matrix):
    return mm(cat(split(values)), matrix)


def whole(shape):
    return pl.BlockSpec(shape, lambda *_: (0,) * len(shape))


def params(mib=58, **more):
    return pltpu.CompilerParams(vmem_limit_bytes=mib * MIB, **more)


def cost(flops, moved):
    return pl.CostEstimate(flops=flops, bytes_accessed=moved, transcendentals=0)


def coord_rows():
    def u(offset):
        c = np.float32(offset) * np.float32(8.0 / 15.0)
        return np.sign(c) * np.log2(np.abs(c) + np.float32(1.0)) / np.float32(3.0)

    lane = np.arange(WIDE)
    out = []
    for parity in range(2):
        e = 2 * (lane // PITCH) + parity
        k = lane % PITCH
        out.append(np.stack([u(SIDE - 1 - e), u(SIDE - 1 - k)] + [np.ones(WIDE)] + [np.zeros(WIDE)] * 5))
    return np.stack(out).astype(np.float32)


def net_columns(w1_ref, b1_ref):
    units = w1_ref.shape[1]
    return jnp.transpose(cat([w1_ref[...], b1_ref[...], jnp.zeros((5, units), F32)], 0))


def table_pre(coord_ref, cols, parity):
    pre = cols[:, 0:1] * coord_ref[parity, 0:1, :] + cols[:, 1:2] * coord_ref[parity, 1:2, :]
    return pre + cols[:, 2:3]


def table_of(hidden, w2s):
    parts = split(hidden)
    z = cat([mm(w2, parts[0]) + mm(w2, parts[1]) for w2 in w2s], 0)
    return 16.0 / (1.0 + jnp.exp(-z))


def stat_lane(kind, group, head):
    return kind * 16 + group * PER_GROUP + head


def head_masks():
    lane = iota((1, LANES), 1) >> 5
    return [flag(lane == h) for h in range(PER_GROUP)]


def forward_kernel(
    images, halves, row_ref, col_ref, p_a_ref, p_b_ref, coord_ref, w1_ref, b1_ref, w2_a_ref, w2_b_ref,
    x_hbm, w_a_hbm, w_b_hbm,
    stat_ref, scale_ref, e_hbm, ctx_hbm, rest_hbm, ql_hbm, kl_hbm, vl_hbm, cell_hbm, gather_hbm, scatter_hbm,
    x_ref, w_a_ref, w_b_ref, e_ref, ctx_ref, rest_ref, ql_ref, kl_ref, vl_ref, cell_ref, gather_ref, scatter_ref,
    table_ref, pos_ref, logit_ref, mix_ref, in_sem, sem, out_sem,
):
    loads = [
        pltpu.make_async_copy(source, target, in_sem.at[i])
        for i, (source, target) in enumerate(((x_hbm, x_ref), (w_a_hbm, w_a_ref), (w_b_hbm, w_b_ref)))
    ]
    for load in loads:
        load.start()
    stores = []

    def store(source, target):
        copy = pltpu.make_async_copy(source, target, out_sem.at[len(stores)])
        copy.start()
        stores.append(copy)

    scatter_ref[...] = flag(iota((WIN, WIN), 1) == cell_of_places(col_ref[:, 0:1], 0))
    store(scatter_ref, scatter_hbm)
    gather = flag(iota((WIN, WIN), 0) == cell_of_places(row_ref[0:1, :], 1))
    gather_ref[...] = gather
    store(gather_ref, gather_hbm)
    stat_ref[...] = jnp.zeros_like(stat_ref)
    for which, ref in enumerate((p_a_ref, p_b_ref)):
        scale_ref[which : which + 1, :] = ref[2:3, :]
    columns = net_columns(w1_ref, b1_ref)
    for parity in range(2):
        hidden, _ = gelu_with_slope(table_pre(coord_ref, columns, parity))
        table_ref[parity] = table_of(hidden, (w2_a_ref[...], w2_b_ref[...])) * LOG2E
    loads[0].wait()
    for m in range(images):
        rows = slice(m * WIN, (m + 1) * WIN)
        cell_ref[rows, :] = mm(gather, x_ref[rows, :]).astype(BF)
    store(cell_ref, cell_hbm)

    masks = head_masks()
    lane = iota((1, LANES), 1)
    row = iota((2 * LANES, LANES), 0) & (LANES - 1)
    col = iota((2 * LANES, LANES), 1)
    same = flag((row >> 5) == (col >> 5))
    lower = iota((1, WIDE), 1) % PITCH < SIDE
    left_half = iota((1, WIDE), 1) < WIN
    ones = jnp.ones((WIN, LANES), BF)

    def prepare(g):
        here = slice(g * LANES, (g + 1) * LANES)
        inner = slice(g % halves * LANES, (g % halves + 1) * LANES)
        which = g // halves
        w_ref, p_ref = ((w_a_ref, p_a_ref), (w_b_ref, p_b_ref))[which]
        if g % halves == 0:
            loads[1 + which].wait()
        w = cat([w_ref[i, :, inner] for i in range(3)])
        sums = [cat([same, flag(stat_lane(i, g, row >> 5) == col)]) for i in range(2)]
        stat_here = [(lane >> 2) == i * 4 + g for i in range(2)]
        out = []
        for m in range(images):
            rows = slice(m * WIN, (m + 1) * WIN)
            qkv = mm(cell_ref[rows, :], w)
            q = qkv[:, :LANES] + p_ref[0:1, inner]
            k = qkv[:, LANES : 2 * LANES]
            vl = (qkv[:, 2 * LANES :] + p_ref[1:2, inner]).astype(BF)
            rq = lax.rsqrt(head_sums(q * q, sums[0]) + 1.0)
            rk = lax.rsqrt(head_sums(k * k, sums[1]) + 1.0)
            ql = (q * rq[:, :LANES]).astype(BF)
            kl = (k * rk[:, :LANES]).astype(BF)
            stat = jnp.where(stat_here[0], rq[:, LANES:], stat_ref[rows, :])
            stat_ref[rows, :] = jnp.where(stat_here[1], rk[:, LANES:], stat)
            ql_ref[rows, here] = ql
            kl_ref[rows, here] = kl
            vl_ref[rows, here] = vl
            out.append((cat(split(ql.astype(F32) * (p_ref[2:3, inner] * LOG2E))), kl, vl))
        for source, target in ((ql_ref, ql_hbm), (kl_ref, kl_hbm), (vl_ref, vl_hbm)):
            store(source.at[:, pl.ds(g * LANES, LANES)], target.at[:, pl.ds(g * LANES, LANES)])
        return out

    def bands_of(head):
        even = jnp.broadcast_to(table_ref[0, head : head + 1, :], (SIDE, WIDE))
        even = pltpu.roll(even, WIDE - SIDE + 1, 1, stride=1, stride_axis=0)
        odd = jnp.broadcast_to(table_ref[1, head : head + 1, :], (SIDE, WIDE))
        odd = pltpu.roll(odd, 1, 1, stride=1, stride_axis=0)
        return jnp.where(lower, even, odd)

    def place_bias(g, pair):
        slot = pair % 2
        one, two = (bands_of(g * PER_GROUP + 2 * pair + i) for i in range(2))
        for r in range(SIDE):
            offset = (SIDE - 1 - r) * SIDE
            pos_ref[slot, r * SIDE : (r + 1) * SIDE, :] = jnp.where(
                left_half, pltpu.roll(one, (WIDE - offset) % WIDE, 1), pltpu.roll(two, (WIDE + WIN - offset) % WIDE, 1)
            )

    pairs = PER_GROUP // 2
    units = [(g, pair, m) for g in range(2 * halves) for pair in range(pairs) for m in range(images)]
    ready = {}

    def score(at):
        g, pair, m = units[at]
        if (g, 0) not in ready:
            for i, operands in enumerate(prepare(g)):
                ready[g, i] = operands
        if m == 0:
            place_bias(g, pair)
        left, kl, _ = ready[g, m]
        keys = cat([kl * mask for mask in masks[2 * pair : 2 * pair + 2]], 0)
        logit_ref[at % 2] = mm_nt(left, cat([keys, keys]))

    def weigh(at):
        g, pair, m = units[at]
        e_ref[g, pair, m] = jnp.exp2(logit_ref[at % 2] + pos_ref[pair % 2]).astype(BF)
        pltpu.make_async_copy(e_ref.at[g, pair, m], e_hbm.at[g, pair, m], sem.at[g, pair, m]).start()

    def mix(at):
        g, pair, m = units[at]
        vl = ready[g, m][2]
        here = masks[2 * pair : 2 * pair + 2]
        values = cat([cat([vl * mask for mask in here], 0), cat([ones * mask for mask in here], 0)])
        mixed = mm(e_ref[g, pair, m], values)
        if pair == 0:
            mix_ref[m] = mixed
        elif pair < pairs - 1:
            mix_ref[m] += mixed
        else:
            mixed = mix_ref[m] + mixed
            rows = slice(m * WIN, (m + 1) * WIN)
            lanes = slice(g * LANES, (g + 1) * LANES)
            inverse = 1.0 / mixed[:, LANES:]
            high, low = split(mixed[:, :LANES] * inverse)
            ctx_ref[rows, lanes] = high
            rest_ref[rows, lanes] = low
            pick = flag(((row & (HEAD - 1)) == 0) & (stat_lane(2, g, row >> 5) == col))
            stat_ref[rows, :] += head_sums(inverse, pick)
            if m == images - 1:
                for source, target in ((ctx_ref, ctx_hbm), (rest_ref, rest_hbm)):
                    store(source.at[:, pl.ds(g * LANES, LANES)], target.at[:, pl.ds(g * LANES, LANES)])

    score(0)
    for at in range(len(units)):
        if at + 1 < len(units):
            score(at + 1)
        weigh(at)
        if at > 0:
            mix(at - 1)
    mix(len(units) - 1)
    for g, pair, m in units:
        pltpu.make_async_copy(e_ref.at[g, pair, m], e_hbm.at[g, pair, m], sem.at[g, pair, m]).wait()
    for copy in stores:
        copy.wait()


def attention_forward(index, x, ws, ps, coords, net_first, net_seconds):
    count, depth = x.shape
    images = count // WIN
    halves = ws[0].shape[2] // LANES
    groups = 2 * halves
    heads = groups * PER_GROUP
    wide = groups * LANES
    pairs = PER_GROUP // 2
    weights = (groups, pairs, images, WIN, 2 * WIN)
    near = [*ps, coords, *net_first, *net_seconds]
    far_out = [weights] + [(count, wide)] * 5 + [(count, depth), (WIN, WIN), (WIN, WIN)]
    near_out = [jax.ShapeDtypeStruct((count, LANES), F32), jax.ShapeDtypeStruct((2, wide // 2), F32)]
    return pl.pallas_call(
        functools.partial(forward_kernel, images, halves),
        grid=(1,),
        in_specs=[pl.BlockSpec((8, WIN), lambda i: (0, 0)), pl.BlockSpec((WIN, LANES), lambda i: (0, 0))]
        + [whole(a.shape) for a in near] + [FAR] * 3,
        out_specs=[whole(a.shape) for a in near_out] + [FAR] * len(far_out),
        out_shape=near_out + [jax.ShapeDtypeStruct(shape, BF) for shape in far_out],
        scratch_shapes=[pltpu.VMEM(x.shape, BF)] + [pltpu.VMEM(w.shape, BF) for w in ws]
        + [pltpu.VMEM(shape, BF) for shape in far_out]
        + [
            pltpu.VMEM((2, heads, WIDE), F32),
            pltpu.VMEM((2, WIN, 2 * WIN), F32),
            pltpu.VMEM((2, WIN, 2 * WIN), F32),
            pltpu.VMEM((images, WIN, 2 * LANES), F32),
            pltpu.SemaphoreType.DMA((3,)),
            pltpu.SemaphoreType.DMA((groups, pairs, images)),
            pltpu.SemaphoreType.DMA((5 * groups + 3,)),
        ],
        compiler_params=params(mib=54, dimension_semantics=("arbitrary",)),
        cost_estimate=cost(8_000_000_000, 40_000_000),
        name="attention_forward",
    )(index, index, *near, x, *ws)


def norm_stats(values):
    center = values - jnp.mean(values, axis=1, keepdims=True)
    inverse = lax.rsqrt(jnp.mean(center * center, axis=1, keepdims=True) + 1e-05)
    return center * inverse, inverse


def norm_back(grad, unit, inverse, gain):
    scaled = grad * gain
    mean = jnp.mean(scaled, axis=1, keepdims=True)
    along = jnp.mean(scaled * unit, axis=1, keepdims=True)
    return inverse * (scaled - mean - unit * along)


def feed_kernel(
    images, scatter_ref, x_ref, mix_ref, wo_a_ref, wo_b_ref, p_a_ref, p_b_ref,
    bo_ref, g1_ref, s1_ref, b2_ref, g2_ref, s2_ref, w1_a_hbm, w1_b_hbm, w2_a_hbm, w2_b_hbm, og_hbm,
    out_hbm, dmid_hbm, da_hbm, own_hbm, other_hbm, small_ref, gb1_ref,
    w1_ref, w2_ref, og_ref, out_ref, da_ref, dm_ref, pack_ref, mid_ref,
    ctx_ref, low_ref, pre_ref, hid_ref, slope_ref, grad_ref, acc_ref, unit_ref, in_sem, out_sem,
):
    half = w1_ref.shape[2]
    depth = x_ref.shape[1]
    narrow = wo_a_ref.shape[0]
    tiles = 2 * half // TILE
    ps = (p_a_ref, p_b_ref)
    packed = (own_hbm, other_hbm)
    loads = [
        pltpu.make_async_copy(source, target, in_sem.at[i])
        for i, (source, target) in enumerate(
            (
                (w1_a_hbm, w1_ref.at[0]), (w1_b_hbm, w1_ref.at[1]), (w2_a_hbm, w2_ref.at[0]),
                (w2_b_hbm, w2_ref.at[1]), (og_hbm, og_ref),
            )
        )
    ]
    for load in loads:
        load.start()
    stores = []

    def store(source, target):
        copy = pltpu.make_async_copy(source, target, out_sem.at[len(stores)])
        copy.start()
        stores.append(copy)

    def place_of(tile):
        at = tile * TILE
        return at // half, slice(at % half, at % half + TILE)

    inverse_ones = []
    for m in range(images):
        rows = slice(m * WIN, (m + 1) * WIN)
        ctx = mm(scatter_ref[...], mix_ref[rows, :]).astype(BF)
        ctx_ref[rows, :] = ctx
        attn = mm(ctx[:, :narrow], wo_a_ref[...]) + mm(ctx[:, narrow:], wo_b_ref[...]) + bo_ref[...]
        unit_one, inverse = norm_stats(attn)
        inverse_ones.append(inverse)
        unit_ref[rows, :] = unit_one
        middle = x_ref[rows, :].astype(F32) + unit_one * g1_ref[...] + s1_ref[...]
        mid_ref[rows, :] = middle
        low_ref[rows, :] = middle.astype(BF)

    def up(tile):
        which, cols = place_of(tile)
        if cols.start == 0:
            loads[which].wait()
        row = 3 + cols.start // TILE
        pre_ref[tile % 2] = mm(low_ref[...], w1_ref[which, :, cols]) + ps[which][row : row + 1, :]

    def down(tile):
        which, cols = place_of(tile)
        if cols.start == 0:
            loads[2 + which].wait()
        term = mm(hid_ref[which, :, cols], w2_ref[which, cols, :])
        if tile == 0:
            acc_ref[...] = term
        else:
            acc_ref[...] += term

    up(0)
    for tile in range(tiles):
        if tile + 1 < tiles:
            up(tile + 1)
        which, cols = place_of(tile)
        hidden, slope = gelu_with_slope(pre_ref[tile % 2])
        hid_ref[which, :, cols] = hidden.astype(BF)
        slope_ref[which, :, cols] = slope
        if tile > 0:
            down(tile - 1)
    down(tiles - 1)

    loads[4].wait()
    sums = [jnp.zeros((1, depth), F32)] * 3
    for m in range(images):
        rows = slice(m * WIN, (m + 1) * WIN)
        unit_two, inverse_two = norm_stats(acc_ref[rows, :] + b2_ref[...])
        out_ref[rows, :] = (mid_ref[rows, :] + (unit_two * g2_ref[...] + s2_ref[...])).astype(BF)
        grad = og_ref[rows, :].astype(F32)
        d_mlp = norm_back(grad, unit_two, inverse_two, g2_ref[...])
        terms = (column_sums(d_mlp), column_sums(grad * unit_two), column_sums(grad))
        sums = [a + b for a, b in zip(sums, terms)]
        dm_ref[rows, :] = d_mlp.astype(BF)
        acc_ref[rows, :] = grad
    store(out_ref, out_hbm)
    for i in range(3):
        small_ref[3 + i : 4 + i, :] = sums[i]

    for tile in range(tiles):
        which, cols = place_of(tile)
        d_pre = mm_nt(dm_ref[...], w2_ref[which, cols, :]) * slope_ref[which, :, cols]
        gb1_ref[which : which + 1, cols] = column_sums(d_pre)
        d_pre_low = d_pre.astype(BF)
        grad_ref[which, :, cols] = d_pre_low
        acc_ref[...] += mm_nt(d_pre_low, w1_ref[which, :, cols])
    store(acc_ref, dmid_hbm)

    def weight_grads(tile):
        which, cols = place_of(tile)
        at = cols.start
        pack_ref[which, half + at : half + at + TILE, :] = mm_tn(hid_ref[which, :, cols], dm_ref[...]).astype(BF)
        rows = slice(at // depth * depth, (at // depth + 1) * depth)
        grads = mm_tn(low_ref[...], grad_ref[which, :, cols]).astype(BF)
        pack_ref[which, rows, at % depth : at % depth + TILE] = grads
        if at + TILE == half:
            span = pl.ds(0, 2 * half)
            store(pack_ref.at[which, span], packed[which].at[span])

    sums = [jnp.zeros((1, depth), F32)] * 3
    for tile in range(tiles):
        weight_grads(tile)
        if tile < images:
            rows = slice(tile * WIN, (tile + 1) * WIN)
            d_middle = acc_ref[rows, :]
            unit_one = unit_ref[rows, :]
            d_attn = norm_back(d_middle, unit_one, inverse_ones[tile], g1_ref[...])
            terms = (column_sums(d_attn), column_sums(d_middle * unit_one), column_sums(d_middle))
            sums = [a + b for a, b in zip(sums, terms)]
            da_ref[rows, :] = d_attn.astype(BF)
        if tile == images - 1:
            store(da_ref, da_hbm)
    for i in range(3):
        small_ref[i : i + 1, :] = sums[i]
    span = pl.ds(2 * half, narrow)
    for which in range(2):
        pack_ref[which, 2 * half : 2 * half + narrow, :] = mm_tn(
            ctx_ref[:, which * narrow : (which + 1) * narrow], da_ref[...]
        ).astype(BF)
        store(pack_ref.at[which, span], packed[which].at[span])
    for copy in stores:
        copy.wait()


def feed_forward(scatter, x, ctx, wos, w1s, w2s, ps, vectors, cotangent):
    count, depth = x.shape
    images = count // WIN
    narrow = wos[0].shape[0]
    half = w1s[0].shape[1]
    packed = 2 * half + narrow
    low = pltpu.VMEM((count, depth), BF)
    full = pltpu.VMEM((count, depth), F32)
    return pl.pallas_call(
        functools.partial(feed_kernel, images),
        in_specs=[NEAR] * 13 + [FAR] * 5,
        out_specs=[FAR] * 5 + [NEAR] * 2,
        out_shape=[
            jax.ShapeDtypeStruct((count, depth), BF),
            jax.ShapeDtypeStruct((count, depth), F32),
            jax.ShapeDtypeStruct((count, depth), BF),
            jax.ShapeDtypeStruct((packed, depth), BF),
            jax.ShapeDtypeStruct((packed, depth), BF),
            jax.ShapeDtypeStruct((8, depth), F32),
            jax.ShapeDtypeStruct((2, half), F32),
        ],
        scratch_shapes=[
            pltpu.VMEM((2, depth, half), BF),
            pltpu.VMEM((2, half, depth), BF),
            low, low, low, low,
            pltpu.VMEM((2, packed, depth), BF),
            full,
            pltpu.VMEM((count, 2 * narrow), BF),
            low,
            pltpu.VMEM((2, count, TILE), F32),
            pltpu.VMEM((2, count, half), BF),
            pltpu.VMEM((2, count, half), F32),
            pltpu.VMEM((2, count, half), BF),
            full, full,
            pltpu.SemaphoreType.DMA((5,)),
            pltpu.SemaphoreType.DMA((7,)),
        ],
        compiler_params=params(mib=56),
        cost_estimate=cost(2 * count * depth * (2 * depth + 12 * half), 30_000_000),
        name="feed_forward",
    )(scatter, x, ctx, *wos, *ps, *vectors, *w1s, *w2s, cotangent)


def context_grad_kernel(images, gather_ref, da_ref, wo_a_ref, wo_b_ref, out_ref):
    for m in range(images):
        rows = slice(m * WIN, (m + 1) * WIN)
        grad = cat([mm_nt(da_ref[rows, :], wo_a_ref[...]), mm_nt(da_ref[rows, :], wo_b_ref[...])]).astype(BF)
        out_ref[rows, :] = mm(gather_ref[...], grad).astype(BF)


def context_grad(gather, d_attn, wos):
    return pl.pallas_call(
        functools.partial(context_grad_kernel, d_attn.shape[0] // WIN),
        out_shape=jax.ShapeDtypeStruct((d_attn.shape[0], 2 * wos[0].shape[0]), BF),
        compiler_params=params(),
        cost_estimate=cost(2_000_000_000, 5_000_000),
        name="context_grad",
    )(gather, d_attn, *wos)


def backward_kernel(
    images, first, span, x_ref, scale_ref, dctx_ref, ctx_ref, rest_ref, ql_ref, kl_ref, vl_ref, stat_ref, e_hbm,
    gw_ref, dqkv_ref, dm_ref, small_ref,
    e_ref, prob_ref, low_ref, sum_ref, duq_ref, dkt_ref, dvt_ref, sem,
):
    pairs = PER_GROUP // 2
    which = first // span
    units = [(g, pair, m) for g in range(span) for pair in range(pairs) for m in range(images)]
    loads = {
        unit: pltpu.make_async_copy(e_hbm.at[first + unit[0], unit[1], unit[2]], e_ref.at[unit], sem.at[unit])
        for unit in units
    }
    for load in loads.values():
        load.start()
    masks = head_masks()
    summing = head_sum_matrix()
    unit_matrix = flag(iota((LANES, LANES), 0) == iota((LANES, LANES), 1))
    shape = (2 * LANES, 3 * LANES)
    col = iota(shape, 1)
    in_head = iota((1, LANES), 1) & (HEAD - 1)
    left_half = iota((1, WIDE), 1) < WIN
    spots = flag(in_head < 2)
    ready = {}
    sums = [[jnp.zeros((1, LANES), F32)] * 3 for _ in range(span)]

    def prepare(g, m):
        here = slice(g * LANES, (g + 1) * LANES)
        rows = slice(m * WIN, (m + 1) * WIN)
        spread = flag((iota(shape, 0) & (LANES - 1)) == stat_lane(col >> 7, first + g, (col & (LANES - 1)) >> 5))
        stats = head_sums(stat_ref[rows, :], spread)
        grad = (dctx_ref[rows, here].astype(F32) * (stats[:, 2 * LANES :] * scale_ref[which : which + 1, here])).astype(BF)
        mix = ctx_ref[rows, here].astype(F32) + rest_ref[rows, here].astype(F32)
        d_high, d_low = split(-head_sums(grad.astype(F32) * mix, summing))
        left = cat([grad, jnp.where(in_head == 0, d_high, d_low)])
        q_t = mm_nt(unit_matrix, ql_ref[rows, here]).astype(BF)
        grad_t = mm_nt(unit_matrix, grad).astype(BF)
        return left, q_t, grad_t, stats[:, : 2 * LANES]

    def score(at):
        g, pair, m = units[at]
        if (g, m) not in ready:
            ready[g, m] = prepare(g, m)
        vl = vl_ref[m * WIN : (m + 1) * WIN, g * LANES : (g + 1) * LANES]
        here = masks[2 * pair : 2 * pair + 2]
        right = cat([cat([vl * mask, jnp.broadcast_to(spots * mask, (WIN, LANES))]) for mask in here], 0)
        prob_ref[at % 2] = mm_nt(ready[g, m][0], right)

    def weigh(at):
        g, pair, m = units[at]
        loads[g, pair, m].wait()
        d_cos = e_ref[g, pair, m].astype(F32) * prob_ref[at % 2]
        low_ref[at % 2] = d_cos.astype(BF)
        if m == 0:
            sum_ref[pair % 2] = d_cos
        else:
            sum_ref[pair % 2] += d_cos
        if m == images - 1:
            one, two = None, None
            for r in range(SIDE):
                offset = (SIDE - 1 - r) * SIDE
                band = sum_ref[pair % 2, r * SIDE : (r + 1) * SIDE, :]
                left = pltpu.roll(jnp.where(left_half, band, 0.0), offset, 1)
                right = pltpu.roll(jnp.where(left_half, 0.0, band), (offset + WIN) % WIDE, 1)
                one = left if one is None else one + left
                two = right if two is None else two + right
            dm_ref[g * PER_GROUP + 2 * pair] = one
            dm_ref[g * PER_GROUP + 2 * pair + 1] = two

    def spend(at):
        g, pair, m = units[at]
        rows = slice(m * WIN, (m + 1) * WIN)
        here = slice(g * LANES, (g + 1) * LANES)
        _, q_t, grad_t, stats = ready[g, m]
        kl, ql = kl_ref[rows, here], ql_ref[rows, here]
        d_low = low_ref[at % 2]
        duq = mm(d_low, cat([kl * mask for mask in masks[2 * pair : 2 * pair + 2]], 0))
        head = pair * 2 * HEAD
        for ref, source, factor in ((dkt_ref, q_t, d_low), (dvt_ref, grad_t, e_ref[g, pair, m])):
            both = mm(source[head : head + 2 * HEAD], factor)
            ref[m, head : head + HEAD, :] = both[:HEAD, : ref.shape[2]]
            ref[m, head + HEAD : head + 2 * HEAD, :] = pltpu.roll(both[HEAD:], WIN, 1)[:, : ref.shape[2]]
        if pair == 0:
            duq_ref[m] = duq
        if 0 < pair < pairs - 1:
            duq_ref[m] += duq
        if pair == pairs - 1:
            duq = duq_ref[m] + duq
            uq = ql.astype(F32)
            along_q = head_sums(uq * duq, summing)
            dq = stats[:, :LANES] * (duq - uq * along_q)
            uk = kl.astype(F32)
            duk = jnp.transpose(dkt_ref[m])[:WIN]
            dk = stats[:, LANES:] * (duk - uk * head_sums(uk * duk, summing))
            dv = jnp.transpose(dvt_ref[m])[:WIN] / scale_ref[which : which + 1, here]
            sums[g] = [a + column_sums(t) for a, t in zip(sums[g], (dq, dv, along_q))]
            for i, grads in enumerate((dq, dk, dv)):
                lanes = (i * span + g) * LANES
                dqkv_ref[rows, lanes : lanes + LANES] = grads.astype(BF)

    score(0)
    for at in range(len(units)):
        if at + 1 < len(units):
            score(at + 1)
        weigh(at)
        if at > 0:
            spend(at - 1)
    spend(len(units) - 1)
    for g in range(span):
        for i in range(3):
            small_ref[g, i : i + 1, :] = sums[g][i]
    for i in range(3):
        gw = mm_tn(x_ref[...], dqkv_ref[:, i * span * LANES : (i + 1) * span * LANES]).astype(BF)
        for g in range(span):
            gw_ref[g, i] = gw[:, g * LANES : (g + 1) * LANES]


def attention_backward(first, span, x, scales, dctx, saved):
    e, *blocks, stat = saved
    count, depth = x.shape
    images = count // WIN
    padded = -(-WIN // LANES) * LANES
    block = pl.BlockSpec((count, span * LANES), lambda i: (0, first // span))
    shapes = [
        jax.ShapeDtypeStruct((span, 3, depth, LANES), BF),
        jax.ShapeDtypeStruct((count, span * 3 * LANES), BF),
        jax.ShapeDtypeStruct((span * PER_GROUP, SIDE, WIDE), F32),
        jax.ShapeDtypeStruct((span, 8, LANES), F32),
    ]
    return pl.pallas_call(
        functools.partial(backward_kernel, images, first, span),
        grid=(1,),
        in_specs=[whole(x.shape), whole(scales.shape)] + [block] * 6
        + [whole(stat.shape), FAR],
        out_specs=[whole(a.shape) for a in shapes],
        out_shape=shapes,
        scratch_shapes=[
            pltpu.VMEM((span,) + e.shape[1:], BF),
            pltpu.VMEM((2, WIN, 2 * WIN), F32),
            pltpu.VMEM((2, WIN, 2 * WIN), BF),
            pltpu.VMEM((2, WIN, 2 * WIN), F32),
            pltpu.VMEM((images, WIN, LANES), F32),
            pltpu.VMEM((images, LANES, padded), F32),
            pltpu.VMEM((images, LANES, padded), F32),
            pltpu.SemaphoreType.DMA((span,) + e.shape[1:3]),
        ],
        compiler_params=params(mib=56 if first else 46, dimension_semantics=("arbitrary",)),
        cost_estimate=cost(8_000_000_000 * span, 20_000_000 * span),
        name=f"attention_backward_{first}",
    )(x, scales, dctx, *blocks, stat, e)


def input_grad_kernel(scatter_ref, dmid_ref, da_ref, db_ref, w_a_ref, w_b_ref, out_ref):
    wide = w_a_ref.shape[2]
    total = None
    for grad_ref, w_ref in ((da_ref, w_a_ref), (db_ref, w_b_ref)):
        for i in range(3):
            term = mm_nt(grad_ref[:, i * wide : (i + 1) * wide], w_ref[i])
            total = term if total is None else total + term
    high, low = split(total)
    out_ref[...] = dmid_ref[...] + mm(scatter_ref[...], high) + mm(scatter_ref[...], low)


def input_grad(scatter, d_middle, grads, ws):
    count, depth = d_middle.shape
    rows = lambda width: pl.BlockSpec((WIN, width), lambda i: (i, 0))
    return pl.pallas_call(
        input_grad_kernel,
        grid=(count // WIN,),
        in_specs=[whole(scatter.shape), rows(depth)] + [rows(g.shape[1]) for g in grads] + [whole(w.shape) for w in ws],
        out_specs=rows(depth),
        out_shape=jax.ShapeDtypeStruct(d_middle.shape, F32),
        compiler_params=params(mib=14, dimension_semantics=("arbitrary",)),
        cost_estimate=cost(3_000_000_000, 12_000_000),
        name="input_grad",
    )(scatter, d_middle, *grads, *ws)


def table_back_kernel(spans, coord_ref, w1_ref, b1_ref, w2_a_ref, w2_b_ref, scale_ref, vec_ref, gb1_ref, *refs):
    calls = len(spans)
    dms, smalls, (own_ref, other_ref) = refs[:calls], refs[calls : 2 * calls], refs[2 * calls :]
    lower = iota((1, WIDE), 1) % PITCH < SIDE
    even, odd = [], []
    for ref in dms:
        e = jnp.zeros((ref.shape[0], WIDE), F32)
        o = jnp.zeros((ref.shape[0], WIDE), F32)
        for c in range(SIDE):
            slab = ref[:, c, :]
            e = e + pltpu.roll(jnp.where(lower, slab, 0.0), (SIDE - 1 - c) % WIDE, 1)
            o = o + pltpu.roll(jnp.where(lower, 0.0, slab), (-1 - c) % WIDE, 1)
        even.append(e)
        odd.append(o)
    w2s = (w2_a_ref[...], w2_b_ref[...])
    columns = net_columns(w1_ref, b1_ref)
    shape = (w2s[0].shape[0], scale_ref.shape[1])
    diagonal = iota(shape, 0) * HEAD == iota(shape, 1)
    inverses = [
        1.0 / jnp.sum(jnp.where(diagonal, scale_ref[i : i + 1, :], 0.0), axis=1, keepdims=True) for i in range(2)
    ]
    inverse = cat(inverses, 0)
    dw2 = None
    dcols = None
    for parity, grads in enumerate((even, odd)):
        hidden, slope = gelu_with_slope(table_pre(coord_ref, columns, parity))
        table = table_of(hidden, w2s)
        dz = cat(grads, 0) * inverse * table * (1.0 - table * 0.0625)
        hidden_high, hidden_low = split(hidden)
        dz_high, dz_low = split(dz)
        term = mm_nt(dz_high, hidden_high) + mm_nt(dz_high, hidden_low) + mm_nt(dz_low, hidden_high)
        dw2 = term if dw2 is None else dw2 + term
        w2 = cat(w2s, 0)
        high, low = split((mm_tn(w2, dz_high) + mm_tn(w2, dz_low)) * slope)
        c_high, c_low = split(coord_ref[parity])
        term = mm_nt(c_high, high) + mm_nt(c_high, low) + mm_nt(c_low, high)
        dcols = term if dcols is None else dcols + term
    heads = w2s[0].shape[0]
    groups = [(ref, g) for ref, span in zip(smalls, spans) for g in range(span)]
    for which, out in enumerate((own_ref, other_ref)):
        lines = [(vec_ref, i) for i in range(6)] + [(dcols, i) for i in range(3)] + [(gb1_ref, which)]
        row = 0
        for source, i in lines + [(dw2, which * heads + h) for h in range(heads)]:
            for at in range(0, source.shape[1], LANES):
                out[row : row + 1, :] = source[i : i + 1, at : at + LANES]
                row += 1
        for ref, g in groups[which * len(groups) // 2 : (which + 1) * len(groups) // 2]:
            for i in range(3):
                out[row : row + 1, :] = ref[g, i : i + 1, :]
                row += 1
        out[row:, :] = jnp.zeros((SMALL_ROWS - row, LANES), F32)


def table_back(coords, net_first, w2s, scales, vectors, gb1, dms, smalls):
    small = jax.ShapeDtypeStruct((SMALL_ROWS, LANES), F32)
    return pl.pallas_call(
        functools.partial(table_back_kernel, [s.shape[0] for s in smalls]),
        out_shape=(small, small),
        compiler_params=params(mib=22),
        cost_estimate=cost(1_000_000_000, 10_000_000),
        name="table_back",
    )(coords, *net_first, *w2s, scales, vectors, gb1, *dms, *smalls)


def swap(array):
    return lax.ppermute(array, "mp", [(0, 1), (1, 0)])


def tie(*trees):
    leaves, kind = jax.tree.flatten(trees)
    return jax.tree.unflatten(kind, lax.optimization_barrier(leaves))


def send(array, plan, phase, step):
    pairs = []
    for mp, strides in enumerate(plan):
        stride = strides[phase]
        for dp in range(16):
            digit = dp // stride % 4
            pairs.append((2 * dp + mp, 2 * (dp + ((digit ^ step) - digit) * stride) + mp))
    return lax.ppermute(array, ("dp", "mp"), pairs)


def rotate_kernel(count, digit_ref, *refs):
    sources, targets = refs[:count], refs[count : count + 4]
    in_ref, out_ref, in_sem, out_sem = refs[count + 4 :]
    rows = out_ref.shape[1]
    order = (1, 2, 3, 0)
    loads, stores = {}, []
    for t in order:
        at = pl.multiple_of((digit_ref[0] ^ t) * rows, 16)
        for i, source in enumerate(sources):
            loads[t, i] = pltpu.make_async_copy(source.at[pl.ds(at, rows)], in_ref.at[i, t], in_sem.at[i, t])
            loads[t, i].start()
    for t in order:
        total = None
        for i in range(count):
            loads[t, i].wait()
            term = in_ref[i, t].astype(F32)
            total = term if total is None else total + term
        out_ref[t] = total.astype(BF)
        stores.append(pltpu.make_async_copy(out_ref.at[t], targets[t], out_sem.at[t]))
        stores[-1].start()
    for store in stores:
        store.wait()


def rotate_sum(arrays, digit):
    rows, lanes = arrays[0].shape
    rows //= 4
    count = len(arrays)
    return pl.pallas_call(
        functools.partial(rotate_kernel, count),
        in_specs=[SCALARS] + [FAR] * count,
        out_specs=[FAR] * 4,
        out_shape=[jax.ShapeDtypeStruct((rows, lanes), BF)] * 4,
        scratch_shapes=[
            pltpu.VMEM((count, 4, rows, lanes), BF),
            pltpu.VMEM((4, rows, lanes), BF),
            pltpu.SemaphoreType.DMA((count, 4)),
            pltpu.SemaphoreType.DMA((4,)),
        ],
        compiler_params=params(mib=12),
        cost_estimate=cost(1_000_000, 6 * rows * lanes * count),
        name="rotate_sum",
    )(digit, *arrays)


def add_all(blocks):
    total = blocks[0].astype(F32)
    for block in blocks[1:]:
        total = total + block.astype(F32)
    return total


def fetch(sources, buffer_ref, sem):
    loads = [pltpu.make_async_copy(ref, buffer_ref.at[i], sem.at[i]) for i, ref in enumerate(sources)]
    for load in loads:
        load.start()
    return loads


def lay_feed_kernel(digit_ref, a, b, c, d, up_ref, down_ref, proj_ref, in_ref, held_ref, in_sem, out_sem):
    rows = in_ref.shape[1]
    for s, load in enumerate(fetch((a, b, c, d), in_ref, in_sem)):
        at = (digit_ref[0] ^ s) * rows
        load.wait()
        held_ref[pl.ds(pl.multiple_of(at, 16), rows), :] = in_ref[s].astype(F32)
    depth, half = up_ref.shape
    parts = [
        (held_ref.at[pl.ds(at, depth)], up_ref.at[:, pl.ds(at, depth)]) for at in range(0, half, depth)
    ]
    parts.append((held_ref.at[pl.ds(half, half)], down_ref))
    parts.append((held_ref.at[pl.ds(2 * half, proj_ref.shape[0])], proj_ref))
    stores = [pltpu.make_async_copy(x, y, out_sem.at[i]) for i, (x, y) in enumerate(parts)]
    for store in stores:
        store.start()
    for store in stores:
        store.wait()


def lay_feed(outer, blocks, depth, half, narrow):
    rows = 2 * half + narrow
    return pl.pallas_call(
        lay_feed_kernel,
        in_specs=[SCALARS] + [FAR] * 4,
        out_specs=[FAR] * 3,
        out_shape=[
            jax.ShapeDtypeStruct((depth, half), F32),
            jax.ShapeDtypeStruct((half, depth), F32),
            jax.ShapeDtypeStruct((narrow, depth), F32),
        ],
        scratch_shapes=[
            pltpu.VMEM((4, rows // 4, depth), BF),
            pltpu.VMEM((rows, depth), F32),
            pltpu.SemaphoreType.DMA((4,)),
            pltpu.SemaphoreType.DMA((half // depth + 2,)),
        ],
        compiler_params=params(mib=12),
        cost_estimate=cost(1_000_000, 8_000_000),
        name="lay_feed",
    )(outer, *blocks)


def lay_rest_kernel(
    halves, digit_ref, a, b, c, d,
    gw_ref, shift_ref, scale_ref, w1_ref, b1_ref, w2_ref, gb1_ref, bp_ref, g1_ref, h1_ref, bd_ref, g2_ref, h2_ref,
    in_ref, held_ref, in_sem,
):
    depth = gw_ref.shape[1]
    quarter = held_ref.shape[0] // 4
    for s, load in enumerate(fetch((a, b, c, d), in_ref, in_sem)):
        at = (digit_ref[0] ^ s) * quarter
        load.wait()
        held_ref[pl.ds(pl.multiple_of(at, 16), quarter), :] = in_ref[s, :quarter, :]
    small = add_all([in_ref[s, quarter:, :] for s in range(4)])
    for g in range(halves):
        for i in range(3):
            at = (g * 3 + i) * depth
            gw_ref[i, :, g * LANES : (g + 1) * LANES] = held_ref[at : at + depth, :].astype(F32)
    row = 0

    def line(length):
        nonlocal row
        count = length // LANES
        out = cat([small[row + i : row + i + 1, :] for i in range(count)])
        row += count
        return out

    for ref in (bp_ref, g1_ref, h1_ref, bd_ref, g2_ref, h2_ref):
        ref[...] = line(ref.shape[1])
    w1_ref[...] = cat([line(w1_ref.shape[1]) for _ in range(2)], 0)
    b1_ref[...] = line(b1_ref.shape[1])
    gb1_ref[...] = line(gb1_ref.shape[1])
    heads, units = w2_ref.shape
    w2_ref[...] = cat([line(units) for _ in range(heads)], 0)
    groups = [[line(LANES) for _ in range(3)] for _ in range(halves)]
    for i in range(2):
        shift_ref[i : i + 1, :] = cat([group[i] for group in groups])
    scale = cat([group[2] for group in groups])
    pick = iota((1, scale.shape[1]), 1)
    scale_ref[...] = cat(
        [jnp.sum(jnp.where(pick == h * HEAD, scale, 0.0), axis=1, keepdims=True) for h in range(heads)]
    )


def lay_rest(outer, blocks, depth, halves, half, units):
    width = halves * LANES
    heads = halves * PER_GROUP
    shapes = [(3, depth, width), (2, width), (1, heads), (2, units), (1, units), (heads, units), (1, half)]
    shapes += [(1, depth)] * 6
    return pl.pallas_call(
        functools.partial(lay_rest_kernel, halves),
        in_specs=[SCALARS] + [FAR] * 4,
        out_specs=[NEAR] * len(shapes),
        out_shape=[jax.ShapeDtypeStruct(s, F32) for s in shapes],
        scratch_shapes=[
            pltpu.VMEM((4,) + blocks[0].shape, BF),
            pltpu.VMEM((halves * 3 * depth, LANES), BF),
            pltpu.SemaphoreType.DMA((4,)),
        ],
        compiler_params=params(mib=16),
        cost_estimate=cost(1_000_000, 8_000_000),
        name="lay_rest",
    )(outer, *blocks)


def on_device(
    size, tokens, query_key_value_matrix, query_value_bias, head_logit_scale, bias_net_first_weight,
    bias_net_first_bias, bias_net_second_weight, relative_pair_index, attention_out_weight, attention_out_bias,
    attention_norm_weight, attention_norm_bias, ffn_input_weight, hidden_ffn_bias, ffn_output_weight,
    output_ffn_bias, feedforward_norm_weight, feedforward_norm_bias, output_gradient,
):
    depth = tokens.shape[1]
    width = query_key_value_matrix.shape[2]
    halves = width // LANES
    half = ffn_input_weight.shape[1]
    units = bias_net_first_bias.shape[0]

    def pair(array):
        return array, swap(array)

    ws = pair(jnp.transpose(query_key_value_matrix, (1, 0, 2)))
    ps = pair(
        jnp.concatenate(
            [
                query_value_bias.astype(F32),
                jnp.repeat(jnp.exp(head_logit_scale.astype(F32)), HEAD)[None],
                hidden_ffn_bias.astype(F32).reshape(-1, TILE),
                jnp.zeros((5 - half // TILE, width), F32),
            ]
        )
    )
    net_seconds = pair(bias_net_second_weight.T)
    wos = pair(attention_out_weight)
    w1s = pair(ffn_input_weight)
    w2s = pair(ffn_output_weight)

    coords = jnp.asarray(coord_rows())
    net_first = (bias_net_first_weight, bias_net_first_bias.reshape(1, units))
    stat, scale_lanes, *saved, cells, gather, scatter = attention_forward(
        relative_pair_index, tokens, ws, ps, coords, net_first, net_seconds
    )
    saved.append(stat)
    vectors = [
        v.reshape(1, depth)
        for v in (
            attention_out_bias, attention_norm_weight, attention_norm_bias,
            output_ffn_bias, feedforward_norm_weight, feedforward_norm_bias,
        )
    ]
    block_out, d_middle, d_attn, own, other, vector_grads, gb1 = feed_forward(
        scatter, tokens, saved[1], wos, w1s, w2s, ps, vectors, output_gradient
    )

    def backward(which, dctx):
        return attention_backward(which * halves, halves, cells, scale_lanes, dctx, saved)

    def tail_small(results):
        return table_back(
            coords, net_first, net_seconds, scale_lanes, vector_grads, gb1,
            [r[2] for r in results], [r[3] for r in results],
        )

    def lines(array):
        return array.reshape(-1, LANES)

    dctx = context_grad(gather, d_attn, wos)
    if size == 16:
        dp, mp = lax.axis_index("dp"), lax.axis_index("mp")
        plan, rest_plan = ((1, 4), (4, 1)), ((1, 4), (1, 4))
        near, far = dp & 3, dp >> 2
        outer = jnp.where(mp == 0, near, far).reshape(1)

        def spread(blocks, phase, plan=plan):
            return [send(b, plan, phase, t + 1) for t, b in enumerate(blocks)]

        got, dctx = tie(swap(other), dctx)
        blocks = rotate_sum([own, got], outer)
        blocks, dctx = tie(blocks, dctx)
        got = spread(blocks[1:], 0)
        theirs = backward(1, dctx)
        got, theirs, dctx = tie(got, theirs, dctx)
        low = add_all([blocks[0]] + got).astype(BF)
        low, dctx = tie(low, dctx)
        got = spread([low] * 3, 1)
        rest_got = swap(lines(theirs[0]))
        mine = backward(0, dctx)
        got, rest_got, mine = tie(got, rest_got, mine)
        low = add_all([low] + got).astype(BF)
        rest = rotate_sum([lines(mine[0]), rest_got], near.reshape(1))
        rest, low = tie(rest, low)
        rest_got = spread(rest[1:], 0, rest_plan)
        gathered = spread([low] * 2, 0)
        results = [mine, theirs]
        small_own, small_other = tail_small(results)
        small = small_own + swap(small_other)
        rest_got, small, gathered[1] = tie(rest_got, small, gathered[1])
        gathered += spread([gathered[1]], 0)
        message = jnp.concatenate([add_all([rest[0]] + rest_got), small]).astype(BF)
        rest_got = spread([message] * 3, 1, rest_plan)
        tokens_grad = input_grad(scatter, d_middle, [r[1] for r in results], ws)
        rest_got, tokens_grad = tie(rest_got, tokens_grad)
        message = add_all([message] + rest_got).astype(BF)
        rest_got = spread([message] * 3, 0, rest_plan)
        feed = lay_feed(outer, [low] + gathered, depth, half, width)
        rest_got, feed = tie(rest_got, feed)
        final = lay_rest(near.reshape(1), [message] + rest_got, depth, halves, half, units)
    else:
        results = [backward(0, dctx), backward(1, dctx)]
        small_own, small_other = tail_small(results)
        tokens_grad = input_grad(scatter, d_middle, [r[1] for r in results], ws)
        outer = jnp.zeros((1,), jnp.int32)

        def total(array):
            return lax.psum(array, "dp").astype(BF)

        def quarters(array):
            rows = array.shape[0] // 4
            return [array[s * rows : (s + 1) * rows] for s in range(4)]

        feed = lay_feed(outer, quarters(total(own.astype(F32) + swap(other).astype(F32))), depth, half, width)
        rest = total(lines(results[0][0]).astype(F32) + swap(lines(results[1][0])).astype(F32))
        small = total(small_own + swap(small_other))
        none = jnp.zeros_like(small)
        blocks = [jnp.concatenate([block, none if s else small]) for s, block in enumerate(quarters(rest))]
        final = lay_rest(outer, blocks, depth, halves, half, units)

    grad_up, grad_down, grad_proj = feed
    grad_qkv, grad_shift, grad_scale, grad_w1, grad_b1, grad_w2, grad_hidden, *vec = final
    vec = [v.reshape(-1) for v in vec]
    return (
        block_out, tokens_grad, jnp.transpose(grad_qkv, (1, 0, 2)), grad_shift, grad_scale.reshape(-1),
        grad_w1, grad_b1.reshape(-1), grad_w2.T, grad_proj, vec[0], vec[1], vec[2],
        grad_up, grad_hidden.reshape(-1), grad_down, vec[3], vec[4], vec[5],
    )


def solution(mesh):
    in_specs = (
        P(("dp", "mp"), None), P(None, None, "mp"), P(None, "mp"), P("mp"), P(), P(), P(None, "mp"), P(),
        P("mp", None), P(), P(), P(), P(None, "mp"), P("mp"), P("mp", None), P(), P(), P(), P(("dp", "mp"), None),
    )
    out_specs = (
        P(("dp", "mp"), None), P(("dp", "mp"), None), P(None, None, "mp"), P(None, "mp"), P("mp"), P(), P(),
        P(None, "mp"), P("mp", None), P(), P(), P(), P(None, "mp"), P("mp"), P("mp", None), P(), P(), P(),
    )
    return jax.shard_map(
        functools.partial(on_device, mesh.shape["dp"]),
        mesh=mesh, in_specs=in_specs, out_specs=out_specs, check_vma=False,
    )
```
